32 devices in a mesh: parts: 2 (over x), tm: 8 (over z, y), stn: 2 (over core).
Axes of the slice: x: 2, y: 2, z: 4, core: 2. Of those that a mesh axis runs over, the one named last changes fastest.
Arguments:
- voltages: bfloat16 [256, 2, 32, 2, 2048], P(('parts', 'stn'), None, 'tm'), parts along dimension 0, may hold values from -6 to 6
- filter_taps: float32 [16, 2048], replicated, may hold values from -1.5 to 1.5
- use_mask: int32 [512, 8], P('parts'), parts along dimension 0, may hold values 0 or 1
- block_index: int32 [512, 8], P('parts'), parts along dimension 0, may hold values from 0 to 127
- weight_blocks: bfloat16 [128, 512], P('tm'), may hold values from -0.5 to 0.5
Outputs:
- power: float32 [2048, 32, 512], P('stn', 'tm', 'parts'), parts along dimension 2
The draws below stay inside these ranges and needn't reach their ends.
There are 2 independent parts, one for each index of `parts`. The reference program is written for one: setup_inputs(seed, part) draws one part's arguments, and reference() takes and returns one part's arrays. A program takes and returns all parts, laid end to end along the dimension named above; an argument that names none is the same for every part. Nothing has to cross between parts.
All inputs are finite; a program needn't handle non-finite values.
Results may differ from the reference program's by a relative error of at most 0.008.
Values may be sent and summed in bfloat16 or wider, within the bound.
No kernel may reach another device: no remote copies, remote signals or barrier semaphores. Data moves between devices by JAX's collectives and lax.ppermute only.
A program may use at most 192 MiB of HBM per device.

```python
import math
import jax
import jax.numpy as jnp
from jax import lax

C = 2048
P_SIZE = 64
Q = 32
BEAMS = 256
TAPS = 16
SB = 16
G = 16
S_DEV = 64
STATIONS = 128
FRAMES = 32
NB = 8
NWB = 128


def touch_ends(entries, own_key, low, largest):
    longest = entries.shape.index(max(entries.shape))
    spots = []
    for shift in (0, 1):
        where = [jax.random.randint(jax.random.fold_in(own_key, axis), (), 0, length) for axis, length in enumerate(entries.shape)]
        where[longest] = (where[longest] + shift) % entries.shape[longest]
        spots.append(tuple(where))
    return entries.at[spots[0]].set(low).at[spots[1]].set(largest)


def levels(own_key, dims, shards, smallest, top_value):
    level = 1.0
    for dim, shards_of in shards:
        heights = jax.random.uniform(jax.random.fold_in(jax.random.fold_in(own_key, 6), dim), (shards_of,), jnp.float32, smallest / len(shards), top_value / len(shards))
        level = level * jnp.repeat(jnp.exp(heights), dims[dim] // shards_of).reshape((-1,) + (1,) * (len(dims) - 1 - dim))
    return level


def bell_draw(rng, dims, deviation, most, pieces=(), kind=jnp.bfloat16):
    loudness = levels(rng, dims, pieces, -0.22, 0.18) if pieces else 1.0
    result = jax.random.normal(rng, dims, jnp.float32) * deviation * loudness
    return jnp.minimum(jnp.maximum(result, -most), most).astype(kind)


def setup_inputs(seed: int = 0, part: int = 0) -> dict:
    splits = jax.random.split(jax.random.key(seed), 6)
    part_keys = jax.random.split(jax.random.fold_in(splits[5], part), 6)
    voltages = bell_draw(part_keys[0], (STATIONS, 2, FRAMES, 2, C), 1.0, 6.0, ((0, 2), (2, 8)))
    filter_taps = bell_draw(splits[1], (TAPS, C), 0.25, 1.5, (), jnp.float32)
    use_mask = touch_ends((jax.random.randint(part_keys[2], (BEAMS, NB), 0, 2) < 1).astype(jnp.int32), jax.random.fold_in(part_keys[2], 1), 0, 1)
    block_index = touch_ends(jax.random.randint(part_keys[3], (BEAMS, NB), 0, NWB), jax.random.fold_in(part_keys[3], 1), 0, NWB - 1).astype(jnp.int32)
    weight_blocks = bell_draw(splits[4], (NWB, G * 2 * SB), (2 * S_DEV) ** -0.5, 0.5, ((0, 8),))
    return dict(voltages=voltages, filter_taps=filter_taps, use_mask=use_mask, block_index=block_index, weight_blocks=weight_blocks)


def transform_tables(first_size, second_size):
    full_size = first_size * second_size
    first_range = jnp.arange(first_size, dtype=jnp.int32)
    second_range = jnp.arange(second_size, dtype=jnp.int32)
    first_angle = (first_range[:, None] * first_range[None, :] % first_size).astype(jnp.float32) * (2.0 * math.pi / first_size)
    cosine_first = jnp.cos(first_angle)
    sine_first = jnp.sin(first_angle)
    section_one = jnp.stack([jnp.stack([cosine_first, -sine_first], axis=1), jnp.stack([sine_first, cosine_first], axis=1)], axis=0)
    second_angle = (second_range[:, None] * second_range[None, :] % second_size).astype(jnp.float32) * (2.0 * math.pi / second_size)
    cosine_second = jnp.cos(second_angle)
    sine_second = jnp.sin(second_angle)
    section_two = jnp.stack([jnp.stack([cosine_second, sine_second], axis=-1), jnp.stack([-sine_second, cosine_second], axis=-1)], axis=1)
    section_two = section_two.reshape(2 * second_size, 2 * second_size)
    twist_angle = (second_range[:, None] * first_range[None, :] % full_size).astype(jnp.float32) * (2.0 * math.pi / full_size)
    return (section_one.astype(jnp.bfloat16), jnp.cos(twist_angle), jnp.sin(twist_angle), section_two.astype(jnp.bfloat16))

def filter_frames(window, filter_taps, frame_count):
    history = filter_taps.shape[0] - 1
    shape_out = window.shape[:2] + (frame_count,) + window.shape[3:]
    summed = jnp.zeros(shape_out, jnp.float32)
    for tap_index in range(filter_taps.shape[0]):
        sliced = lax.slice_in_dim(window, history - tap_index, history - tap_index + frame_count, axis=2)
        summed = summed + filter_taps[tap_index] * sliced.astype(jnp.float32)
    return summed.astype(jnp.bfloat16)

def channelize(filtered, tables):
    section_one, twist_cos, twist_sin, section_two = tables
    first_size = section_one.shape[1]
    second_size = twist_cos.shape[0]
    station_count, frame_count = (filtered.shape[0], filtered.shape[2])
    reshaped = filtered.reshape(station_count, 2, frame_count, 2, first_size, second_size)
    first_section = jnp.einsum('spfrae,raob->spfeob', reshaped.astype(jnp.float32), section_one.astype(jnp.float32))
    real_part = first_section[:, :, :, :, 0, :]
    imag_part = first_section[:, :, :, :, 1, :]
    norm_factor = 1.0 / math.sqrt(first_size * second_size)
    twist_real = (real_part * twist_cos + imag_part * twist_sin) * norm_factor
    twist_imag = (imag_part * twist_cos - real_part * twist_sin) * norm_factor
    twiddled = jnp.stack([twist_real, twist_imag], axis=-2).astype(jnp.bfloat16)
    twiddled = twiddled.reshape(station_count, 2, frame_count, 2 * second_size, first_size)
    spectra = jnp.einsum('dk,spfkb->spfdb', section_two.astype(jnp.float32), twiddled.astype(jnp.float32))
    return spectra.astype(jnp.bfloat16).reshape(station_count, 2, frame_count, second_size, 2, first_size)

def beam_matrix(use_rows, picked):
    beam_count, block_count = use_rows.shape
    shaped = picked.reshape(beam_count, block_count, G, 2, SB) * use_rows.astype(jnp.bfloat16)[:, :, None, None, None]
    real_part = shaped[:, :, :, 0, :].transpose(2, 1, 3, 0).reshape(G, block_count * SB, beam_count)
    imag_part = shaped[:, :, :, 1, :].transpose(2, 1, 3, 0).reshape(G, block_count * SB, beam_count)
    upper_rows = jnp.stack([real_part, imag_part], axis=2)
    lower_rows = jnp.stack([-imag_part, real_part], axis=2)
    return jnp.stack([upper_rows, lower_rows], axis=1)

def form_beams(row_block, weights):
    row_count = row_block.shape[0]
    group_count = weights.shape[0]
    reshaped = row_block.reshape(group_count, -1, row_block.shape[2]).astype(jnp.float32)
    matrices = weights.reshape(group_count, row_block.shape[2], -1).astype(jnp.float32)
    product = jnp.einsum('gmk,gkn->gmn', reshaped, matrices)
    return product.reshape(row_count, -1)

def detect(summed):
    shaped = summed.reshape(summed.shape[0], 4, -1)
    return lax.optimization_barrier(jnp.sum(shaped * shaped, axis=1))

def reference(voltages, filter_taps, use_mask, block_index, weight_blocks):
    tables = transform_tables(P_SIZE, Q)
    history = TAPS - 1

    def per_station(station):
        window = jnp.pad(station[None], ((0, 0), (0, 0), (history, 0), (0, 0), (0, 0)))
        filtered = filter_frames(window, filter_taps, FRAMES)
        return channelize(filtered, tables)[0]
    spectra = lax.map(per_station, voltages)
    turned = spectra.transpose(2, 3, 5, 1, 4, 0).reshape(FRAMES, C, 2, 2, STATIONS)
    picked = weight_blocks[block_index]
    matrix = beam_matrix(use_mask, picked)
    member_count = STATIONS // S_DEV

    def per_frame(frame_rows):
        summed = jnp.zeros((C, 4 * BEAMS), jnp.float32)
        for member in range(member_count):
            low = member * S_DEV
            row_block = frame_rows[:, :, :, low:low + S_DEV].reshape(C, 2, 2 * S_DEV)
            weights = matrix[:, :, low:low + S_DEV]
            partial_value = form_beams(row_block, weights).astype(jnp.bfloat16)
            partial_value = lax.optimization_barrier(partial_value)
            summed = summed + partial_value.astype(jnp.float32)
        return detect(summed)
    detected = lax.map(per_frame, turned)
    return detected.transpose(1, 0, 2)
```

```python
import functools
import math

import jax
import jax.numpy as jnp
import ml_dtypes
import numpy as np
from jax import lax
from jax.experimental import pallas as pl
from jax.experimental.pallas import tpu as pltpu
from jax.sharding import PartitionSpec as P

SB = 16
G = 16
RADIX = 16
LANES = 128
CORES = 2
VMEM_LIMIT = 56 * 1024 * 1024
F32 = jnp.float32
BF16 = jnp.bfloat16


def dft_tables(channels):
    per_half = channels // RADIX // CORES
    b = np.arange(RADIX)[None, :, None, None]
    e = np.arange(LANES)[None, None, None, :]
    d = np.arange(CORES * per_half).reshape(CORES, 1, per_half, 1)
    angle = (e * (RADIX * d + b) % channels) * (2.0 * math.pi / channels)
    cosine, sine = np.cos(angle), np.sin(angle)
    real_rows = np.concatenate([cosine, sine], axis=3)
    imag_rows = np.concatenate([-sine, cosine], axis=3)
    table = np.concatenate([real_rows, imag_rows], axis=2) / math.sqrt(channels)
    return table.astype(ml_dtypes.bfloat16)


def turned(value, step, size):
    re, im = value
    step %= size
    if step == 0:
        return re, im
    if 4 * step == size:
        return im, -re
    if 2 * step == size:
        return -re, -im
    if 4 * step == 3 * size:
        return -im, re
    cosine, sine = math.cos(2 * math.pi * step / size), math.sin(2 * math.pi * step / size)
    if 8 * step == size:
        return (re + im) * cosine, (im - re) * cosine
    if 8 * step == 3 * size:
        return (im - re) * sine, -(re + im) * sine
    return re * cosine + im * sine, im * cosine - re * sine


def four_points(values):
    (r0, i0), (r1, i1), (r2, i2), (r3, i3) = values
    sr, si, dr, di = r0 + r2, i0 + i2, r0 - r2, i0 - i2
    tr, ti, er, ei = r1 + r3, i1 + i3, r1 - r3, i1 - i3
    return [(sr + tr, si + ti), (dr + ei, di - er), (sr - tr, si - ti), (dr - ei, di + er)]


def sixteen_points(values):
    inner = [four_points([values[4 * a1 + a0] for a1 in range(4)]) for a0 in range(4)]
    result = [None] * 16
    for b0 in range(4):
        outer = four_points([turned(inner[a0][b0], a0 * b0, 16) for a0 in range(4)])
        for b1 in range(4):
            result[4 * b1 + b0] = outer[b1]
    return result


def filter_kernel(place, taps, own, other, own_back, other_back, far, keep, send):
    tap_count = taps.shape[0]
    history = tap_count - 1
    frames = own.shape[0]
    count = 2 * frames
    stations, samples = own.shape[2:]
    tiles = stations // SB

    def run(first, second, first_back, second_back, first_out, second_out):
        window = [(far, i) for i in range(far.shape[0])]
        for ref in (first_back, second_back, first, second):
            window += [(ref, i) for i in range(frames)]

        for low in range(0, samples, LANES):
            lanes = slice(low, low + LANES)
            tap_rows = [jnp.broadcast_to(taps[k : k + 1, lanes], (SB, LANES)) for k in range(tap_count)]

            def step(i, carry):
                part, rows = i // tiles, pl.ds(pl.multiple_of(i % tiles * SB, SB), SB)
                sums = [None] * count
                for j, (ref, index) in enumerate(window):
                    value = ref[index, part, rows, lanes].astype(F32)
                    for f in range(count):
                        k = f + history - j
                        if 0 <= k <= history:
                            term = tap_rows[k] * value
                            sums[f] = term if sums[f] is None else sums[f] + term
                for f in range(count):
                    out = first_out if f < frames else second_out
                    out[f % frames, part, rows, lanes] = sums[f].astype(BF16)
                return carry

            lax.fori_loop(0, 2 * tiles, step, 0)

    @pl.when(place[0] == 0)
    def _():
        run(own, other, own_back, other_back, keep, send)

    @pl.when(place[0] == 1)
    def _():
        run(other, own, other_back, own_back, send, keep)


def filter_frames(place, taps, own, other, own_back, other_back, far, low):
    frames, _, _, samples = own.shape
    stations = far.shape[2]
    block = 512
    where = low // stations

    def spec(depth, station_block):
        return pl.BlockSpec((depth, 2, stations, block), lambda i, place: (0, 0, station_block, i))

    shape = jax.ShapeDtypeStruct((frames, 2, stations, samples), BF16)
    return pl.pallas_call(
        filter_kernel,
        out_shape=(shape, shape),
        grid_spec=pltpu.PrefetchScalarGridSpec(
            num_scalar_prefetch=1,
            grid=(samples // block,),
            in_specs=[pl.BlockSpec((taps.shape[0], block), lambda i, place: (0, i))]
            + [spec(frames, where)] * 4
            + [spec(far.shape[0], 0)],
            out_specs=[spec(frames, 0)] * 2,
        ),
        compiler_params=pltpu.CompilerParams(vmem_limit_bytes=VMEM_LIMIT),
        cost_estimate=pl.CostEstimate(
            flops=2 * 2 * frames * 2 * stations * samples * taps.shape[0],
            bytes_accessed=2 * 2 * stations * samples * (6 * frames + far.shape[0]),
            transcendentals=0,
        ),
        name="filter",
    )(place, taps, own, other, own_back, other_back, far)


def onward_kernel(low, place, own_back, other_back, far, sems):
    frames = own_back.shape[0]
    stations = far.shape[2]
    drop = 2 * frames - far.shape[0]
    rows = pl.ds(low, stations)

    def run(first, second):
        copies = [
            pltpu.make_async_copy(first.at[drop:, :, rows], far.at[: frames - drop], sems.at[0]),
            pltpu.make_async_copy(second.at[:, :, rows], far.at[frames - drop :], sems.at[1]),
        ]
        for copy in copies:
            copy.start()
        for copy in copies:
            copy.wait()

    @pl.when(place[0] == 0)
    def _():
        run(own_back, other_back)

    @pl.when(place[0] == 1)
    def _():
        run(other_back, own_back)


def onward(place, own_back, other_back, low, stations, history):
    _, parts, _, samples = own_back.shape
    return pl.pallas_call(
        functools.partial(onward_kernel, low),
        out_shape=jax.ShapeDtypeStruct((history, parts, stations, samples), BF16),
        in_specs=[pl.BlockSpec(memory_space=pltpu.SMEM)] + [pl.BlockSpec(memory_space=pl.ANY)] * 2,
        out_specs=pl.BlockSpec(memory_space=pl.ANY),
        scratch_shapes=[pltpu.SemaphoreType.DMA((2,))],
        cost_estimate=pl.CostEstimate(
            flops=0, bytes_accessed=4 * history * parts * stations * samples, transcendentals=0
        ),
        name="onward",
    )(place, own_back, other_back)


def weight_kernel(table, index, mask, out):
    groups, depth, width = out.shape
    beams = width // 2
    half = depth // 2
    rows = lax.broadcasted_iota(jnp.int32, (table.shape[0], beams), 0)
    for q in range(index.shape[0]):
        hit = jnp.where((rows == index[q : q + 1, :]) & (mask[q : q + 1, :] != 0), 1.0, 0.0).astype(BF16)
        picked = lax.dot_general(table[...], hit, (((0,), (0,)), ((), ())), preferred_element_type=F32)
        picked = picked.reshape(groups, 2, SB, beams)
        low = q * SB
        re, im = picked[:, 0], picked[:, 1]
        out[:, low : low + SB, :beams] = re.astype(BF16)
        out[:, low : low + SB, beams:] = im.astype(BF16)
        out[:, half + low : half + low + SB, :beams] = (-im).astype(BF16)
        out[:, half + low : half + low + SB, beams:] = re.astype(BF16)


def beam_weights(table, index, mask):
    blocks, beams = index.shape
    groups = table.shape[1] // (2 * SB)
    shape = (groups, 2 * blocks * SB, 2 * beams)
    return pl.pallas_call(
        weight_kernel,
        out_shape=jax.ShapeDtypeStruct(shape, BF16),
        compiler_params=pltpu.CompilerParams(vmem_limit_bytes=VMEM_LIMIT),
        cost_estimate=pl.CostEstimate(
            flops=2 * table.shape[0] * table.shape[1] * blocks * beams,
            bytes_accessed=2 * math.prod(shape),
            transcendentals=0,
        ),
        name="weights",
    )(table, index, mask)


def beam_kernel(source_count, has_earlier, *refs):
    refs = list(refs)
    refs.pop(0)
    sources = [refs.pop(0) for _ in range(source_count)]
    table, weights = refs.pop(0), refs.pop(0)
    earlier = refs.pop(0) if has_earlier else None
    out, mixed, spectra = refs[:3]
    summed = refs[3] if has_earlier else out
    step = pl.program_id(0)
    pair = sources[0].shape[0]
    station_count = sum(ref.shape[2] for ref in sources)
    groups = weights.shape[0]
    beams = weights.shape[2] // 2
    rows_of = table.shape[2] // 2 // groups
    frames = pl.num_programs(0) * pair
    frame_count = out.shape[1] if has_earlier else 4
    lane_tiles = beams // LANES
    per_channel = lane_tiles * frame_count

    low = 0
    for ref in sources:
        tiles = ref.shape[2] // SB

        def radix(i, carry, ref=ref, low=low, tiles=tiles):
            f, rows = i // tiles, pl.ds(pl.multiple_of(i % tiles * SB, SB), SB)
            values = [
                tuple(ref[f, part, rows, a * LANES : (a + 1) * LANES].astype(F32) for part in range(2))
                for a in range(RADIX)
            ]
            target = pl.ds(pl.multiple_of(f * station_count + low + i % tiles * SB, SB), SB)
            for b, (re, im) in enumerate(sixteen_points(values)):
                mixed[b, target, :LANES] = re.astype(BF16)
                mixed[b, target, LANES:] = im.astype(BF16)
            return carry

        lax.fori_loop(0, pair * tiles, radix, 0)
        low += ref.shape[2]

    def transform(b, carry):
        product = lax.dot_general(
            table[0, b], mixed[b], (((1,), (1,)), ((), ())), preferred_element_type=F32
        )
        product = product.reshape(2, groups, rows_of, pair * station_count)
        for part in range(2):
            value = jnp.concatenate(
                [product[part, :, :, f * station_count : (f + 1) * station_count] for f in range(pair)], axis=1
            )
            spectra[:, b, :, part * station_count : (part + 1) * station_count] = value.astype(BF16)
        return carry

    lax.fori_loop(0, RADIX, transform, 0)

    def form(g, carry):
        rows = spectra[g].reshape(RADIX * pair * rows_of, 2 * station_count)
        beam = jnp.dot(rows, weights[g], preferred_element_type=F32)
        re, im = beam[:, :beams], beam[:, beams:]
        power = re * re + im * im
        for b in range(RADIX):
            for f in range(pair):
                at = (b * pair + f) * rows_of
                for t in range(lane_tiles):
                    start = (g * rows_of * RADIX + b) * per_channel + t * frame_count + step * pair + f
                    summed[pl.ds(start, rows_of, stride=RADIX * per_channel), :] = power[
                        at : at + rows_of, t * LANES : (t + 1) * LANES
                    ]
        return carry

    lax.fori_loop(0, groups, form, 0)

    if has_earlier:

        @pl.when(step == pl.num_programs(0) - 1)
        def _():
            def finish(i, carry):
                for k in range(8):
                    c = i * 8 + k
                    rows = pl.ds(pl.multiple_of(c * per_channel, per_channel), per_channel)
                    value = summed[rows, :] + earlier[rows, :]
                    for t in range(lane_tiles):
                        out[c, :, t * LANES : (t + 1) * LANES] = value[t * frame_count : (t + 1) * frame_count]
                return carry

            lax.fori_loop(0, out.shape[0] // 8, finish, 0)


def beam_power(place, sources, table, weights, earlier, channels):
    frames, _, _, samples = sources[0].shape
    groups, depth, width = weights.shape
    beams = width // 2
    pair = 2
    station_count = sum(s.shape[2] for s in sources)
    flat = (channels * frames * beams // LANES, LANES)
    flat_spec = pl.BlockSpec(flat, lambda i, place: (0, 0))
    in_specs = [pl.BlockSpec((pair, 2, s.shape[2], samples), lambda i, place: (i, 0, 0, 0)) for s in sources]
    in_specs += [
        pl.BlockSpec((1,) + table.shape[1:], lambda i, place: (place[1], 0, 0, 0)),
        pl.BlockSpec(weights.shape, lambda i, place: (0, 0, 0)),
    ]
    operands = list(sources) + [table, weights]
    scratch = [
        pltpu.VMEM((RADIX, pair * station_count, 2 * LANES), BF16),
        pltpu.VMEM((groups, RADIX, pair * channels // groups // RADIX, 2 * station_count), BF16),
    ]
    if earlier is None:
        out_shape = jax.ShapeDtypeStruct(flat, F32)
        out_spec = flat_spec
    else:
        out_shape = jax.ShapeDtypeStruct((channels, frames, beams), F32)
        out_spec = pl.BlockSpec(out_shape.shape, lambda i, place: (0, 0, 0))
        operands.append(earlier)
        in_specs.append(flat_spec)
        scratch.append(pltpu.VMEM(flat, F32))
    return pl.pallas_call(
        functools.partial(beam_kernel, len(sources), earlier is not None),
        out_shape=out_shape,
        grid_spec=pltpu.PrefetchScalarGridSpec(
            num_scalar_prefetch=1,
            grid=(frames // pair,),
            in_specs=in_specs,
            out_specs=out_spec,
            scratch_shapes=scratch,
        ),
        compiler_params=pltpu.CompilerParams(vmem_limit_bytes=VMEM_LIMIT),
        cost_estimate=pl.CostEstimate(
            flops=2 * channels * frames * depth * width + 8 * frames * station_count * LANES * channels,
            bytes_accessed=4 * math.prod(flat) + 4 * frames * station_count * samples + 2 * math.prod(weights.shape),
            transcendentals=0,
        ),
        name="beams",
    )(place, *operands)


def flipped(rows, bit):
    return jnp.where(bit == 1, rows[::-1], rows)


def body(voltages, filter_taps, use_mask, block_index, weight_blocks):
    stations, pols, frames, parts, samples = voltages.shape
    history = filter_taps.shape[0] - 1
    half = stations // 2
    time_devices = lax.axis_size("tm")
    side = lax.axis_index("tm") % 2
    core = lax.axis_index("stn")
    place = jnp.stack([side, core]).astype(jnp.int32)

    def pair(block):
        return lax.ppermute(block, "tm", [(i, i ^ 1) for i in range(time_devices)])

    def hop(block, skip=0):
        return lax.ppermute(block, "tm", [(i, i + 2) for i in range(skip, time_devices - 2)])

    def swap(block):
        return lax.ppermute(block, "stn", [(0, 1), (1, 0)])

    columns = weight_blocks.shape[1] // CORES
    shard = lax.dynamic_slice_in_dim(weight_blocks, core * columns, columns, 1)
    shard = lax.all_gather(shard, "tm", axis=0, tiled=True)
    voltages, shard = lax.optimization_barrier((voltages, shard))

    def some(pol, start):
        block = lax.dynamic_slice_in_dim(voltages, start, half, 0)[:, pol]
        return block.transpose(1, 2, 0, 3)

    own, other = [], []
    for pol in range(pols):
        other.append(pair(some(pol, half * (1 - side))))
        own.append(some(pol, half * side))
    own_back = [hop(block) for block in own]
    other_back = [hop(block) for block in other]

    def ordered(rows):
        rows = rows.T.reshape(2, 2, 2, -1)
        rows = flipped(rows, core)
        rows = flipped(rows.swapaxes(0, 1), side).swapaxes(0, 1)
        return rows.reshape(8, -1)

    weights = beam_weights(shard, ordered(block_index), ordered(use_mask))
    table = jnp.asarray(dft_tables(samples))

    power = None
    for pol in range(pols):
        chunks = [(0, half)] if pol == 0 else [(0, half // 2), (half // 2, half // 2)]
        keeps, sents = [], []
        for low, size in chunks:
            far = hop(onward(place, own_back[pol], other_back[pol], low, size, history - 2 * frames), 2)
            keep, send = filter_frames(
                place, filter_taps, own[pol], other[pol], own_back[pol], other_back[pol], far, low
            )
            keeps.append(keep)
            sents.append(pair(send))
        sources = keeps + sents + [swap(b) for b in keeps] + [swap(b) for b in sents]
        power = beam_power(place, sources, table, weights, power, samples // CORES)
    return power


def solution(mesh):
    in_specs = (
        P(("parts", "stn"), None, "tm", None, None),
        P(),
        P("parts", None),
        P("parts", None),
        P("tm", None),
    )
    out_specs = P("stn", "tm", "parts")
    return jax.shard_map(body, mesh=mesh, in_specs=in_specs, out_specs=out_specs, check_vma=False)
```

```python
import functools
import math

import jax
import jax.numpy as jnp
import ml_dtypes
import numpy as np
from jax import lax
from jax.experimental import pallas as pl
from jax.experimental.pallas import tpu as pltpu
from jax.sharding import PartitionSpec as P

SB = 16
G = 16
RADIX = 16
LANES = 128
CORES = 2
VMEM_LIMIT = 56 * 1024 * 1024
F32 = jnp.float32
BF16 = jnp.bfloat16


def cost(microseconds):
    return pl.CostEstimate(flops=0, bytes_accessed=int(microseconds * 3.3e6), transcendentals=0)


def dft_tables(channels):
    per_half = channels // RADIX // CORES
    b = np.arange(RADIX)[None, :, None, None]
    e = np.arange(LANES)[None, None, None, :]
    d = np.arange(CORES * per_half).reshape(CORES, 1, per_half, 1)
    angle = (e * (RADIX * d + b) % channels) * (2.0 * math.pi / channels)
    cosine, sine = np.cos(angle), np.sin(angle)
    real_rows = np.concatenate([cosine, sine], axis=3)
    imag_rows = np.concatenate([-sine, cosine], axis=3)
    table = np.concatenate([real_rows, imag_rows], axis=2) / math.sqrt(channels)
    return table.astype(ml_dtypes.bfloat16)


def turned(value, step, size):
    re, im = value
    step %= size
    if step == 0:
        return re, im
    if 4 * step == size:
        return im, -re
    if 2 * step == size:
        return -re, -im
    if 4 * step == 3 * size:
        return -im, re
    cosine, sine = math.cos(2 * math.pi * step / size), math.sin(2 * math.pi * step / size)
    if 8 * step == size:
        return (re + im) * cosine, (im - re) * cosine
    if 8 * step == 3 * size:
        return (im - re) * sine, -(re + im) * sine
    return re * cosine + im * sine, im * cosine - re * sine


def four_points(values):
    (r0, i0), (r1, i1), (r2, i2), (r3, i3) = values
    sr, si, dr, di = r0 + r2, i0 + i2, r0 - r2, i0 - i2
    tr, ti, er, ei = r1 + r3, i1 + i3, r1 - r3, i1 - i3
    return [(sr + tr, si + ti), (dr + ei, di - er), (sr - tr, si - ti), (dr - ei, di + er)]


def sixteen_points(values):
    inner = [four_points([values[4 * a1 + a0] for a1 in range(4)]) for a0 in range(4)]
    result = [None] * 16
    for b0 in range(4):
        outer = four_points([turned(inner[a0][b0], a0 * b0, 16) for a0 in range(4)])
        for b1 in range(4):
            result[4 * b1 + b0] = outer[b1]
    return result


def after(block, *earlier):
    return pl.pallas_call(
        lambda *refs: None,
        out_shape=jax.ShapeDtypeStruct(block.shape, block.dtype),
        in_specs=[pl.BlockSpec(memory_space=pl.ANY)] * (1 + len(earlier)),
        out_specs=pl.BlockSpec(memory_space=pl.ANY),
        input_output_aliases={0: 0},
        compiler_params=pltpu.CompilerParams(vmem_limit_bytes=VMEM_LIMIT),
        cost_estimate=cost(0),
        name="after",
    )(block, *earlier)


def filter_kernel(place, taps, own, other, own_back, other_back, far, *rest):
    keep, send = rest[-2:]
    tap_count = taps.shape[0]
    history = tap_count - 1
    frames = own.shape[0]
    count = 2 * frames
    stations, samples = own.shape[2:]
    tiles = stations // SB
    lane_tiles = samples // LANES

    def run(first, second, first_back, second_back, first_out, second_out):
        window = [(far, i) for i in range(far.shape[0])]
        for ref in (first_back, second_back, first, second):
            window += [(ref, i) for i in range(frames)]

        def step(i, carry):
            lanes = pl.ds(pl.multiple_of(i % lane_tiles * LANES, LANES), LANES)
            part = i // lane_tiles % 2
            rows = pl.ds(pl.multiple_of(i // (2 * lane_tiles) * SB, SB), SB)
            tap_rows = [jnp.broadcast_to(taps[k : k + 1, lanes], (SB, LANES)) for k in range(tap_count)]
            sums = [None] * count
            for j, (ref, index) in enumerate(window):
                value = ref[index, part, rows, lanes].astype(F32)
                for f in range(count):
                    k = f + history - j
                    if 0 <= k <= history:
                        term = tap_rows[k] * value
                        sums[f] = term if sums[f] is None else sums[f] + term
            for f in range(count):
                out = first_out if f < frames else second_out
                out[f % frames, part, rows, lanes] = sums[f].astype(BF16)
            return carry

        lax.fori_loop(0, 2 * tiles * lane_tiles, step, 0, unroll=2)

    @pl.when(place[0] == 0)
    def _():
        run(own, other, own_back, other_back, keep, send)

    @pl.when(place[0] == 1)
    def _():
        run(other, own, other_back, own_back, send, keep)


def filter_frames(place, taps, own, other, own_back, other_back, far, pol, low, earlier=()):
    frames, _, _, samples = other.shape
    stations = far.shape[2]
    block = 512
    where = low // stations

    def spec(depth, station_block):
        return pl.BlockSpec((depth, 2, stations, block), lambda i, place: (0, 0, station_block, i))

    both = pl.BlockSpec((None, frames, 2, stations, block), lambda i, place: (pol, 0, 0, where, i))
    one = spec(frames, where)
    shape = jax.ShapeDtypeStruct((frames, 2, stations, samples), BF16)
    return pl.pallas_call(
        filter_kernel,
        out_shape=(shape, shape),
        grid_spec=pltpu.PrefetchScalarGridSpec(
            num_scalar_prefetch=1,
            grid=(samples // block,),
            in_specs=[pl.BlockSpec((taps.shape[0], block), lambda i, place: (0, i))]
            + [both, one, both, one, spec(far.shape[0], 0)]
            + [pl.BlockSpec(memory_space=pl.ANY)] * len(earlier),
            out_specs=[spec(frames, 0)] * 2,
        ),
        compiler_params=pltpu.CompilerParams(vmem_limit_bytes=VMEM_LIMIT),
        cost_estimate=cost(8 * stations / 32),
        name="filter",
    )(place, taps, own, other, own_back, other_back, far, *earlier)


def onward_kernel(place, own_back, other_back, *rest):
    far = rest[-1]
    frames = own_back.shape[0]
    kept = far.shape[0] - frames

    def run(first, second):
        far[:kept] = first[frames - kept :]
        far[kept:] = second[...]

    @pl.when(place[0] == 0)
    def _():
        run(own_back, other_back)

    @pl.when(place[0] == 1)
    def _():
        run(other_back, own_back)


def onward(place, own_back, other_back, pol, low, stations, history, earlier=()):
    frames, parts, _, samples = other_back.shape
    where = low // stations
    return pl.pallas_call(
        onward_kernel,
        out_shape=jax.ShapeDtypeStruct((history, parts, stations, samples), BF16),
        grid_spec=pltpu.PrefetchScalarGridSpec(
            num_scalar_prefetch=1,
            grid=(parts,),
            in_specs=[
                pl.BlockSpec((None, frames, 1, stations, samples), lambda i, place: (pol, 0, i, where, 0)),
                pl.BlockSpec((frames, 1, stations, samples), lambda i, place: (0, i, where, 0)),
            ]
            + [pl.BlockSpec(memory_space=pl.ANY)] * len(earlier),
            out_specs=pl.BlockSpec((history, 1, stations, samples), lambda i, place: (0, i, 0, 0)),
        ),
        compiler_params=pltpu.CompilerParams(vmem_limit_bytes=VMEM_LIMIT),
        cost_estimate=cost(3 * stations / 32),
        name="onward",
    )(place, own_back, other_back, *earlier)


def weight_kernel(table, index, mask, out):
    groups, depth, width = out.shape
    beams = width // 2
    half = depth // 2
    rows = lax.broadcasted_iota(jnp.int32, (table.shape[0], beams), 0)
    for q in range(index.shape[0]):
        hit = jnp.where((rows == index[q : q + 1, :]) & (mask[q : q + 1, :] != 0), 1.0, 0.0).astype(BF16)
        picked = lax.dot_general(table[...], hit, (((0,), (0,)), ((), ())), preferred_element_type=F32)
        picked = picked.reshape(groups, 2, SB, beams)
        low = q * SB
        re, im = picked[:, 0], picked[:, 1]
        out[:, low : low + SB, :beams] = re.astype(BF16)
        out[:, low : low + SB, beams:] = im.astype(BF16)
        out[:, half + low : half + low + SB, :beams] = (-im).astype(BF16)
        out[:, half + low : half + low + SB, beams:] = re.astype(BF16)


def beam_weights(table, index, mask):
    blocks, beams = index.shape
    groups = table.shape[1] // (2 * SB)
    shape = (groups, 2 * blocks * SB, 2 * beams)
    return pl.pallas_call(
        weight_kernel,
        out_shape=jax.ShapeDtypeStruct(shape, BF16),
        compiler_params=pltpu.CompilerParams(vmem_limit_bytes=VMEM_LIMIT),
        cost_estimate=cost(4),
        name="weights",
    )(table, index, mask)


def beam_kernel(source_count, has_earlier, *refs):
    refs = list(refs)
    refs.pop(0)
    sources = [refs.pop(0) for _ in range(source_count)]
    table, weights = refs.pop(0), refs.pop(0)
    earlier = refs.pop(0) if has_earlier else None
    out, mixed, spectra = refs[:3]
    step = pl.program_id(0)
    frames = sources[0].shape[0]
    station_count = sum(ref.shape[2] for ref in sources)
    groups = spectra.shape[0]
    beams = weights.shape[2] // 2
    rows_of = table.shape[2] // 2 // groups
    pair = 2
    lane_tiles = beams // LANES
    per_channel = lane_tiles * frames

    @pl.when(step == 0)
    def _():
        low = 0
        for ref in sources:
            tiles = ref.shape[2] // SB

            def radix(i, carry, ref=ref, low=low, tiles=tiles):
                f, rows = i // tiles, pl.ds(pl.multiple_of(i % tiles * SB, SB), SB)
                values = [
                    tuple(ref[f, part, rows, a * LANES : (a + 1) * LANES].astype(F32) for part in range(2))
                    for a in range(RADIX)
                ]
                target = pl.ds(pl.multiple_of(f * station_count + low + i % tiles * SB, SB), SB)
                for b, (re, im) in enumerate(sixteen_points(values)):
                    mixed[b, target, :LANES] = re.astype(BF16)
                    mixed[b, target, LANES:] = im.astype(BF16)
                return carry

            lax.fori_loop(0, frames * tiles, radix, 0)
            low += ref.shape[2]

        def transform(b, carry):
            for start in range(0, frames, pair):
                product = lax.dot_general(
                    table[0, b],
                    mixed[b, start * station_count : (start + pair) * station_count],
                    (((1,), (1,)), ((), ())),
                    preferred_element_type=F32,
                )
                product = product.reshape(2, groups, rows_of, pair * station_count)
                rows = slice(start * rows_of, (start + pair) * rows_of)
                for part in range(2):
                    value = jnp.concatenate(
                        [product[part, :, :, f * station_count : (f + 1) * station_count] for f in range(pair)], axis=1
                    )
                    columns = slice(part * station_count, (part + 1) * station_count)
                    spectra[:, b, rows, columns] = value.astype(BF16)
            return carry

        lax.fori_loop(0, RADIX, transform, 0, unroll=4)

    for k in range(weights.shape[0]):
        rows = spectra[step * weights.shape[0] + k].reshape(RADIX * frames * rows_of, 2 * station_count)
        beam = jnp.dot(rows, weights[k], preferred_element_type=F32)
        re, im = beam[:, :beams], beam[:, beams:]
        power = re * re + im * im
        if not has_earlier:
            out[k] = power
            continue
        power = power + earlier[k]
        for b in range(RADIX):
            for f in range(frames):
                at = (b * frames + f) * rows_of
                for t in range(lane_tiles):
                    start = (k * rows_of * RADIX + b) * per_channel + t * frames + f
                    refs[3][pl.ds(start, rows_of, stride=RADIX * per_channel), :] = power[
                        at : at + rows_of, t * LANES : (t + 1) * LANES
                    ]

    if has_earlier:

        def finish(c, carry):
            value = refs[3][pl.ds(pl.multiple_of(c * per_channel, per_channel), per_channel), :]
            for t in range(lane_tiles):
                out[c, :, t * LANES : (t + 1) * LANES] = value[t * frames : (t + 1) * frames]
            return carry

        lax.fori_loop(0, out.shape[0], finish, 0, unroll=8)


def beam_power(place, sources, table, weights, earlier, channels):
    frames, _, _, samples = sources[0].shape
    groups, depth, width = weights.shape
    beams = width // 2
    station_count = sum(s.shape[2] for s in sources)
    at_once = 2
    flat = (groups, channels // groups * frames, beams)
    flat_spec = pl.BlockSpec((at_once,) + flat[1:], lambda i, place: (i, 0, 0))
    in_specs = [pl.BlockSpec(s.shape, lambda i, place: (0, 0, 0, 0)) for s in sources]
    in_specs += [
        pl.BlockSpec((1,) + table.shape[1:], lambda i, place: (place[1], 0, 0, 0)),
        pl.BlockSpec((at_once, depth, width), lambda i, place: (i, 0, 0)),
    ]
    operands = list(sources) + [table, weights]
    scratch = [
        pltpu.VMEM((RADIX, frames * station_count, 2 * LANES), BF16),
        pltpu.VMEM((groups, RADIX, frames * channels // groups // RADIX, 2 * station_count), BF16),
    ]
    if earlier is None:
        out_shape = jax.ShapeDtypeStruct(flat, F32)
        out_spec = flat_spec
    else:
        out_shape = jax.ShapeDtypeStruct((channels, frames, beams), F32)
        out_spec = pl.BlockSpec((channels // groups * at_once, frames, beams), lambda i, place: (i, 0, 0))
        operands.append(earlier)
        in_specs.append(flat_spec)
        scratch.append(pltpu.VMEM((math.prod(out_spec.block_shape) // LANES, LANES), F32))
    return pl.pallas_call(
        functools.partial(beam_kernel, len(sources), earlier is not None),
        out_shape=out_shape,
        grid_spec=pltpu.PrefetchScalarGridSpec(
            num_scalar_prefetch=1,
            grid=(groups // at_once,),
            in_specs=in_specs,
            out_specs=out_spec,
            scratch_shapes=scratch,
        ),
        compiler_params=pltpu.CompilerParams(vmem_limit_bytes=VMEM_LIMIT),
        cost_estimate=cost(0),
        name="beams",
    )(place, *operands)


def flipped(rows, bit):
    return jnp.where(bit == 1, rows[::-1], rows)


def body(voltages, filter_taps, use_mask, block_index, weight_blocks):
    stations, pols, frames, parts, samples = voltages.shape
    history = filter_taps.shape[0] - 1
    half = stations // 2
    time_devices = lax.axis_size("tm")
    side = lax.axis_index("tm") % 2
    core = lax.axis_index("stn")
    place = jnp.stack([side, core]).astype(jnp.int32)

    def pair(block):
        return lax.ppermute(block, "tm", [(i, i ^ 1) for i in range(time_devices)])

    def hop(block, skip=0):
        return lax.ppermute(block, "tm", [(i, i + 2) for i in range(skip, time_devices - 2)])

    def swap(block):
        return lax.ppermute(block, "stn", [(0, 1), (1, 0)])

    columns = weight_blocks.shape[1] // CORES
    shard = lax.dynamic_slice_in_dim(weight_blocks, core * columns, columns, 1)
    shard = jnp.concatenate([shard, pair(shard)])
    shards = [shard] + [
        lax.ppermute(shard, "tm", [(i, i ^ far) for i in range(time_devices)]) for far in range(2, time_devices, 2)
    ]

    other = [lax.dynamic_slice_in_dim(voltages, half * (1 - side), half, 0)[:, p].transpose(1, 2, 0, 3) for p in range(pols)]
    own = lax.dynamic_slice_in_dim(voltages, half * side, half, 0).transpose(1, 2, 3, 0, 4)
    other, own, shards = lax.optimization_barrier((other, own, shards))
    other = [pair(block) for block in other]
    own_back = hop(own)
    other_back = [hop(block) for block in other]

    def ordered(rows):
        rows = rows.T.reshape(2, 2, 2, -1)
        rows = flipped(rows, core)
        rows = flipped(rows.swapaxes(0, 1), side).swapaxes(0, 1)
        return rows.reshape(8, -1)

    index = block_index ^ (lax.axis_index("tm") * weight_blocks.shape[0])
    weights = beam_weights(jnp.concatenate(shards), ordered(index), ordered(use_mask))
    table = jnp.asarray(dft_tables(samples))

    chunks = [(pol, low, half // 2) for pol in range(pols) for low in (0, half // 2)]
    further = [
        onward(place, own_back, other_back[pol], pol, low, size, history - 2 * frames, other_back)
        for pol, low, size in chunks
    ]
    far = [hop(block, 2) for block in further]
    keeps, sends = [], []
    for (pol, low, _), block in zip(chunks, far):
        earlier = keeps[-1:] if keeps else further[1:] + [weights]
        keep, send = filter_frames(
            place, filter_taps, own, other[pol], own_back, other_back[pol], block, pol, low, earlier
        )
        keeps.append(keep)
        sends.append(send)
    sents = [pair(block) for block in sends]
    sents[:2] = [after(block, keeps[-1]) for block in sents[:2]]

    def power_of(pol, earlier):
        here = [i for i, chunk in enumerate(chunks) if chunk[0] == pol]
        sources = [keeps[i] for i in here] + [sents[i] for i in here]
        sources += [swap(block) for block in sources]
        return beam_power(place, sources, table, weights, earlier, samples // CORES)

    power = power_of(0, None)
    sents[-1] = after(sents[-1], power)
    return power_of(1, power)


def solution(mesh):
    in_specs = (
        P(("parts", "stn"), None, "tm", None, None),
        P(),
        P("parts", None),
        P("parts", None),
        P("tm", None),
    )
    out_specs = P("stn", "tm", "parts")
    return jax.shard_map(body, mesh=mesh, in_specs=in_specs, out_specs=out_specs, check_vma=False)
```

```python
import functools
import math

import jax
import jax.numpy as jnp
import ml_dtypes
import numpy as np
from jax import lax
from jax.experimental import pallas as pl
from jax.experimental.pallas import tpu as pltpu
from jax.sharding import PartitionSpec as P

SB = 16
G = 16
RADIX = 16
LANES = 128
CORES = 2
VMEM_LIMIT = 56 * 1024 * 1024
F32 = jnp.float32
BF16 = jnp.bfloat16


def cost(microseconds):
    return pl.CostEstimate(flops=0, bytes_accessed=int(microseconds * 3.3e6), transcendentals=0)


def dft_tables(channels):
    per_half = channels // RADIX // CORES
    b = np.arange(RADIX)[None, :, None, None]
    e = np.arange(LANES)[None, None, None, :]
    d = np.arange(CORES * per_half).reshape(CORES, 1, per_half, 1)
    angle = (e * (RADIX * d + b) % channels) * (2.0 * math.pi / channels)
    cosine, sine = np.cos(angle), np.sin(angle)
    real_rows = np.concatenate([cosine, sine], axis=3)
    imag_rows = np.concatenate([-sine, cosine], axis=3)
    table = np.concatenate([real_rows, imag_rows], axis=2) / math.sqrt(channels)
    return table.astype(ml_dtypes.bfloat16)


def turned(value, step, size):
    re, im = value
    step %= size
    if step == 0:
        return re, im
    if 4 * step == size:
        return im, -re
    if 2 * step == size:
        return -re, -im
    if 4 * step == 3 * size:
        return -im, re
    cosine, sine = math.cos(2 * math.pi * step / size), math.sin(2 * math.pi * step / size)
    if 8 * step == size:
        return (re + im) * cosine, (im - re) * cosine
    if 8 * step == 3 * size:
        return (im - re) * sine, -(re + im) * sine
    return re * cosine + im * sine, im * cosine - re * sine


def four_points(values):
    (r0, i0), (r1, i1), (r2, i2), (r3, i3) = values
    sr, si, dr, di = r0 + r2, i0 + i2, r0 - r2, i0 - i2
    tr, ti, er, ei = r1 + r3, i1 + i3, r1 - r3, i1 - i3
    return [(sr + tr, si + ti), (dr + ei, di - er), (sr - tr, si - ti), (dr - ei, di + er)]


def sixteen_points(values):
    inner = [four_points([values[4 * a1 + a0] for a1 in range(4)]) for a0 in range(4)]
    result = [None] * 16
    for b0 in range(4):
        outer = four_points([turned(inner[a0][b0], a0 * b0, 16) for a0 in range(4)])
        for b1 in range(4):
            result[4 * b1 + b0] = outer[b1]
    return result


def after(block, *earlier):
    return pl.pallas_call(
        lambda *refs: None,
        out_shape=jax.ShapeDtypeStruct(block.shape, block.dtype),
        in_specs=[pl.BlockSpec(memory_space=pl.ANY)] * (1 + len(earlier)),
        out_specs=pl.BlockSpec(memory_space=pl.ANY),
        input_output_aliases={0: 0},
        cost_estimate=cost(0),
        name="after",
    )(block, *earlier)


def split_kernel(cuts, place, voltages, own, *rest):
    outs, (own_buffer, other_buffer, sems) = rest[: len(cuts)], rest[len(cuts) :]
    half = own.shape[0]
    side = place[0]

    def load(start, buffer, k):
        return pltpu.make_async_copy(voltages.at[pl.ds(start * half, half)], buffer, sems.at[k])

    stores = [pltpu.make_async_copy(own_buffer, own, sems.at[2])]
    for k, (out, (pol, low, size)) in enumerate(zip(outs, cuts)):
        stores.append(pltpu.make_async_copy(other_buffer.at[low : low + size, pol], out, sems.at[3 + k]))
    load(side, own_buffer, 0).start()
    load(1 - side, other_buffer, 1).start()
    load(side, own_buffer, 0).wait()
    stores[0].start()
    load(1 - side, other_buffer, 1).wait()
    for copy in stores[1:]:
        copy.start()
    for copy in stores:
        copy.wait()


def split(place, voltages, cuts):
    stations, pols, frames, parts, samples = voltages.shape
    half = (stations // 2, pols, frames, parts, samples)
    shapes = [half] + [(size, frames, parts, samples) for _, _, size in cuts]
    return pl.pallas_call(
        functools.partial(split_kernel, cuts),
        out_shape=[jax.ShapeDtypeStruct(shape, BF16) for shape in shapes],
        in_specs=[pl.BlockSpec(memory_space=pltpu.SMEM), pl.BlockSpec(memory_space=pl.ANY)],
        out_specs=[pl.BlockSpec(memory_space=pl.ANY)] * len(shapes),
        scratch_shapes=[
            pltpu.VMEM(half, BF16),
            pltpu.VMEM(half, BF16),
            pltpu.SemaphoreType.DMA((3 + len(cuts),)),
        ],
        compiler_params=pltpu.CompilerParams(vmem_limit_bytes=VMEM_LIMIT),
        cost_estimate=cost(3),
        name="split",
    )(place, voltages)


def filter_kernel(place, taps, own, other, own_back, other_back, far, *rest):
    keep, send = rest[-2:]
    tap_count = taps.shape[0]
    history = tap_count - 1
    frames = own.shape[0]
    count = 2 * frames
    stations, samples = own.shape[2:]
    tiles = stations // SB
    lane_tiles = samples // LANES

    def run(first, second, first_back, second_back, first_out, second_out):
        window = [(far, i) for i in range(far.shape[0])]
        for ref in (first_back, second_back, first, second):
            window += [(ref, i) for i in range(frames)]

        def step(i, carry):
            lanes = pl.ds(pl.multiple_of(i % lane_tiles * LANES, LANES), LANES)
            part = i // lane_tiles % 2
            rows = pl.ds(pl.multiple_of(i // (2 * lane_tiles) * SB, SB), SB)
            tap_rows = [taps[k, :, lanes][None] for k in range(tap_count)]
            sums = [None] * count
            for j, (ref, index) in enumerate(window):
                value = ref[index, part, rows, lanes].astype(F32).reshape(SB // 8, 8, LANES)
                for f in range(count):
                    k = f + history - j
                    if 0 <= k <= history:
                        term = tap_rows[k] * value
                        sums[f] = term if sums[f] is None else sums[f] + term
            for f in range(count):
                out = first_out if f < frames else second_out
                out[f % frames, part, rows, lanes] = sums[f].reshape(SB, LANES).astype(BF16)
            return carry

        lax.fori_loop(0, 2 * tiles * lane_tiles, step, 0, unroll=2)

    @pl.when(place[0] == 0)
    def _():
        run(own, other, own_back, other_back, keep, send)

    @pl.when(place[0] == 1)
    def _():
        run(other, own, other_back, own_back, send, keep)


def filter_frames(place, taps, own, other, own_back, other_back, far, pol, low, earlier=()):
    frames, _, _, samples = other.shape
    stations = far.shape[2]
    block = 512
    where = low // stations

    def spec(depth, station_block):
        return pl.BlockSpec((depth, 2, stations, block), lambda i, place: (0, 0, station_block, i))

    both = pl.BlockSpec((None, frames, 2, stations, block), lambda i, place: (pol, 0, 0, where, i))
    one = spec(frames, where)
    shape = jax.ShapeDtypeStruct((frames, 2, stations, samples), BF16)
    return pl.pallas_call(
        filter_kernel,
        out_shape=(shape, shape),
        grid_spec=pltpu.PrefetchScalarGridSpec(
            num_scalar_prefetch=1,
            grid=(samples // block,),
            in_specs=[pl.BlockSpec((taps.shape[0], 8, block), lambda i, place: (0, 0, i))]
            + [both, one, both, one, spec(far.shape[0], 0)]
            + [pl.BlockSpec(memory_space=pl.ANY)] * len(earlier),
            out_specs=[spec(frames, 0)] * 2,
        ),
        compiler_params=pltpu.CompilerParams(vmem_limit_bytes=VMEM_LIMIT),
        cost_estimate=cost(8 * stations / 32),
        name="filter",
    )(place, taps, own, other, own_back, other_back, far, *earlier)


def onward_kernel(place, own_back, other_back, *rest):
    far = rest[-1]
    frames = own_back.shape[0]
    kept = far.shape[0] - frames

    def run(first, second):
        far[:kept] = first[frames - kept :]
        far[kept:] = second[...]

    @pl.when(place[0] == 0)
    def _():
        run(own_back, other_back)

    @pl.when(place[0] == 1)
    def _():
        run(other_back, own_back)


def onward(place, own_back, other_back, pol, low, stations, history, earlier=()):
    frames, parts, _, samples = other_back.shape
    where = low // stations
    return pl.pallas_call(
        onward_kernel,
        out_shape=jax.ShapeDtypeStruct((history, parts, stations, samples), BF16),
        grid_spec=pltpu.PrefetchScalarGridSpec(
            num_scalar_prefetch=1,
            grid=(parts,),
            in_specs=[
                pl.BlockSpec((None, frames, 1, stations, samples), lambda i, place: (pol, 0, i, where, 0)),
                pl.BlockSpec((frames, 1, stations, samples), lambda i, place: (0, i, where, 0)),
            ]
            + [pl.BlockSpec(memory_space=pl.ANY)] * len(earlier),
            out_specs=pl.BlockSpec((history, 1, stations, samples), lambda i, place: (0, i, 0, 0)),
        ),
        compiler_params=pltpu.CompilerParams(vmem_limit_bytes=VMEM_LIMIT),
        cost_estimate=cost(3 * stations / 32),
        name="onward",
    )(place, own_back, other_back, *earlier)


def weight_kernel(table, index, mask, *rest):
    out = rest[-1]
    groups, depth, width = out.shape
    beams = width // 2
    half = depth // 2
    rows = lax.broadcasted_iota(jnp.int32, (table.shape[0], beams), 0)
    for q in range(index.shape[0]):
        hit = jnp.where((rows == index[q : q + 1, :]) & (mask[q : q + 1, :] != 0), 1.0, 0.0).astype(BF16)
        picked = lax.dot_general(table[...], hit, (((0,), (0,)), ((), ())), preferred_element_type=F32)
        picked = picked.reshape(groups, 2, SB, beams)
        low = q % 2 * half + q // 2 * SB
        re, im = picked[:, 0], picked[:, 1]
        out[:, low : low + SB, :beams] = re.astype(BF16)
        out[:, low : low + SB, beams:] = im.astype(BF16)
        low += half // 2
        out[:, low : low + SB, :beams] = (-im).astype(BF16)
        out[:, low : low + SB, beams:] = re.astype(BF16)


def beam_weights(table, index, mask, earlier):
    blocks, beams = index.shape
    groups = table.shape[1] // (2 * SB)
    shape = (groups, 2 * blocks * SB, 2 * beams)
    return pl.pallas_call(
        weight_kernel,
        out_shape=jax.ShapeDtypeStruct(shape, BF16),
        in_specs=[pl.BlockSpec(memory_space=pltpu.VMEM)] * 3 + [pl.BlockSpec(memory_space=pl.ANY)] * len(earlier),
        compiler_params=pltpu.CompilerParams(vmem_limit_bytes=VMEM_LIMIT),
        cost_estimate=cost(4),
        name="weights",
    )(table, index, mask, *earlier)


def transform(sources, table, mixed, spectra):
    frames = sources[0].shape[0]
    station_count = sum(ref.shape[2] for ref in sources)
    groups = spectra.shape[0]
    rows_of = table.shape[2] // 2 // groups

    low = 0
    for ref in sources:
        tiles = ref.shape[2] // SB

        def radix(i, carry, ref=ref, low=low, tiles=tiles):
            f, rows = i // tiles, pl.ds(pl.multiple_of(i % tiles * SB, SB), SB)
            values = [
                tuple(ref[f, part, rows, a * LANES : (a + 1) * LANES].astype(F32) for part in range(2))
                for a in range(RADIX)
            ]
            target = pl.ds(pl.multiple_of(f * station_count + low + i % tiles * SB, SB), SB)
            for b, (re, im) in enumerate(sixteen_points(values)):
                mixed[b, target, :LANES] = re.astype(BF16)
                mixed[b, target, LANES:] = im.astype(BF16)
            return carry

        lax.fori_loop(0, frames * tiles, radix, 0)
        low += ref.shape[2]

    def step(b, carry):
        product = lax.dot_general(table[0, b], mixed[b], (((1,), (1,)), ((), ())), preferred_element_type=F32)
        product = product.reshape(2, groups, rows_of, frames * station_count)
        value = [
            jnp.concatenate([product[part, :, :, f * station_count : (f + 1) * station_count] for f in range(frames)], axis=1)
            for part in range(2)
        ]
        spectra[:, b] = jnp.concatenate(value, axis=2).astype(BF16)
        return carry

    lax.fori_loop(0, RADIX, step, 0, unroll=4)


def spectra_kernel(place, *refs):
    *sources, table, out, mixed = refs
    transform(sources, table, mixed, out)


def spectra_shape(sources, channels, groups):
    frames = sources[0].shape[0]
    return (groups, RADIX, frames * channels // groups // RADIX, 2 * sum(s.shape[2] for s in sources))


def mixed_shape(sources):
    return (RADIX, sources[0].shape[0] * sum(s.shape[2] for s in sources), 2 * LANES)


def station_spectra(place, sources, table, channels, groups):
    shape = spectra_shape(sources, channels, groups)
    return pl.pallas_call(
        spectra_kernel,
        out_shape=jax.ShapeDtypeStruct(shape, BF16),
        grid_spec=pltpu.PrefetchScalarGridSpec(
            num_scalar_prefetch=1,
            grid=(1,),
            in_specs=[pl.BlockSpec(s.shape, lambda i, place: (0, 0, 0, 0)) for s in sources]
            + [pl.BlockSpec((1,) + table.shape[1:], lambda i, place: (place[1], 0, 0, 0))],
            out_specs=pl.BlockSpec(shape, lambda i, place: (0, 0, 0, 0)),
            scratch_shapes=[pltpu.VMEM(mixed_shape(sources), BF16)],
        ),
        compiler_params=pltpu.CompilerParams(vmem_limit_bytes=VMEM_LIMIT),
        cost_estimate=cost(5),
        name="spectra",
    )(place, *sources, table)


def beam_kernel(source_count, has_earlier, place, first, *refs):
    refs = list(refs)
    sources = [refs.pop(0) for _ in range(source_count)]
    table, weights = refs.pop(0), refs.pop(0)
    earlier = refs.pop(0) if has_earlier else None
    out, mixed, second = refs[:3]
    step = pl.program_id(0)
    frames = sources[0].shape[0]
    beams = weights.shape[2] // 2
    rows_of = first.shape[2] // frames
    lane_tiles = beams // LANES
    per_channel = lane_tiles * frames

    @pl.when(step == 0)
    def _():
        transform(sources, table, mixed, second)

    for k in range(weights.shape[0]):
        rows = jnp.concatenate([first[k], second[step * weights.shape[0] + k]], axis=2)
        rows = rows.reshape(RADIX * frames * rows_of, rows.shape[2])
        beam = jnp.dot(rows, weights[k], preferred_element_type=F32)
        re, im = beam[:, :beams], beam[:, beams:]
        power = re * re + im * im
        if not has_earlier:
            out[k] = power
            continue
        power = power + earlier[k]
        for b in range(RADIX):
            for f in range(frames):
                at = (b * frames + f) * rows_of
                for t in range(lane_tiles):
                    start = (k * rows_of * RADIX + b) * per_channel + t * frames + f
                    refs[3][pl.ds(start, rows_of, stride=RADIX * per_channel), :] = power[
                        at : at + rows_of, t * LANES : (t + 1) * LANES
                    ]

    if has_earlier:

        def finish(c, carry):
            value = refs[3][pl.ds(pl.multiple_of(c * per_channel, per_channel), per_channel), :]
            for t in range(lane_tiles):
                out[c, :, t * LANES : (t + 1) * LANES] = value[t * frames : (t + 1) * frames]
            return carry

        lax.fori_loop(0, out.shape[0], finish, 0, unroll=8)


def beam_power(place, first, sources, table, weights, earlier, channels):
    frames, _, _, samples = sources[0].shape
    groups, depth, width = weights.shape
    beams = width // 2
    at_once = 2
    flat = (groups, channels // groups * frames, beams)
    flat_spec = pl.BlockSpec((at_once,) + flat[1:], lambda i, place: (i, 0, 0))
    in_specs = [pl.BlockSpec((at_once,) + first.shape[1:], lambda i, place: (i, 0, 0, 0))]
    in_specs += [pl.BlockSpec(s.shape, lambda i, place: (0, 0, 0, 0)) for s in sources]
    in_specs += [
        pl.BlockSpec((1,) + table.shape[1:], lambda i, place: (place[1], 0, 0, 0)),
        pl.BlockSpec((at_once, depth, width), lambda i, place: (i, 0, 0)),
    ]
    operands = [first] + list(sources) + [table, weights]
    scratch = [pltpu.VMEM(mixed_shape(sources), BF16), pltpu.VMEM(spectra_shape(sources, channels, groups), BF16)]
    if earlier is None:
        out_shape = jax.ShapeDtypeStruct(flat, F32)
        out_spec = flat_spec
    else:
        out_shape = jax.ShapeDtypeStruct((channels, frames, beams), F32)
        out_spec = pl.BlockSpec((channels // groups * at_once, frames, beams), lambda i, place: (i, 0, 0))
        operands.append(earlier)
        in_specs.append(flat_spec)
        scratch.append(pltpu.VMEM((math.prod(out_spec.block_shape) // LANES, LANES), F32))
    return pl.pallas_call(
        functools.partial(beam_kernel, len(sources), earlier is not None),
        out_shape=out_shape,
        grid_spec=pltpu.PrefetchScalarGridSpec(
            num_scalar_prefetch=1,
            grid=(groups // at_once,),
            in_specs=in_specs,
            out_specs=out_spec,
            scratch_shapes=scratch,
        ),
        compiler_params=pltpu.CompilerParams(vmem_limit_bytes=VMEM_LIMIT),
        cost_estimate=cost(0),
        name="beams",
    )(place, *operands)


def flipped(rows, bit):
    return jnp.where(bit == 1, rows[::-1], rows)


def body(voltages, filter_taps, use_mask, block_index, weight_blocks):
    stations, pols, frames, parts, samples = voltages.shape
    history = filter_taps.shape[0] - 1
    half = stations // 2
    time_devices = lax.axis_size("tm")
    side = lax.axis_index("tm") % 2
    core = lax.axis_index("stn")
    place = jnp.stack([side, core]).astype(jnp.int32)

    def pair(block):
        return lax.ppermute(block, "tm", [(i, i ^ 1) for i in range(time_devices)])

    def hop(block, skip=0):
        return lax.ppermute(block, "tm", [(i, i + 2) for i in range(skip, time_devices - 2)])

    def swap(block):
        return lax.ppermute(block, "stn", [(0, 1), (1, 0)])

    def laid(block):
        return jnp.moveaxis(block, 0, -2)

    quarter = half // 2
    cuts = [(pol, 0, half) for pol in range(pols)]
    own, *other = split(place, voltages, cuts)
    own, other = laid(own), [pair(laid(block)) for block in other]

    columns = weight_blocks.shape[1] // CORES
    shard = lax.dynamic_slice_in_dim(weight_blocks, core * columns, columns, 1)
    shard = jnp.concatenate([shard, pair(shard)])
    shards = [shard] + [
        lax.ppermute(shard, "tm", [(i, i ^ far) for i in range(time_devices)]) for far in range(2, time_devices, 2)
    ]

    def ordered(rows):
        rows = rows.T.reshape(2, 2, 2, -1)
        rows = flipped(rows, core)
        rows = flipped(rows.swapaxes(0, 1), side).swapaxes(0, 1)
        return rows.reshape(8, -1)

    index = block_index ^ (lax.axis_index("tm") * weight_blocks.shape[0])
    weights = beam_weights(jnp.concatenate(shards), ordered(index), ordered(use_mask), other)
    table = jnp.asarray(dft_tables(samples))
    taps = jnp.broadcast_to(filter_taps[:, None, :], (history + 1, 8, samples))

    own_back = hop(own)
    other_back = [hop(other[0])]
    chunks = [(pol, low) for pol in range(pols) for low in (0, quarter)]
    further = []
    for pol, low in chunks:
        if pol >= len(other_back):
            other_back.append(hop(after(other[pol], further[0])))
        further.append(onward(place, own_back, other_back[pol], pol, low, quarter, history - 2 * frames, [weights]))
    far = [hop(block, 2) for block in further]
    keeps, sents, power = [], [], None
    for k, (pol, low) in enumerate(chunks):
        earlier = sents[-1:] + ([power] if k == len(chunks) - 1 else [])
        keep, send = filter_frames(
            place, taps, own, other[pol], own_back, other_back[pol], far[k], pol, low, earlier
        )
        keeps.append(keep)
        sents.append(pair(send))
        if k % 2 == 1:
            sources = [[keeps[i], sents[i], swap(keeps[i]), swap(sents[i])] for i in (k - 1, k)]
            first = station_spectra(place, sources[0], table, samples // CORES, weights.shape[0])
            power = beam_power(place, first, sources[1], table, weights, power, samples // CORES)
    return power


def solution(mesh):
    in_specs = (
        P(("parts", "stn"), None, "tm", None, None),
        P(),
        P("parts", None),
        P("parts", None),
        P("tm", None),
    )
    out_specs = P("stn", "tm", "parts")
    return jax.shard_map(body, mesh=mesh, in_specs=in_specs, out_specs=out_specs, check_vma=False)
```

```python
import functools
import math

import jax
import jax.numpy as jnp
import ml_dtypes
import numpy as np
from jax import lax
from jax.experimental import pallas as pl
from jax.experimental.pallas import tpu as pltpu
from jax.sharding import PartitionSpec as P

SB = 16
G = 16
RADIX = 16
LANES = 128
CORES = 2
VMEM_LIMIT = 56 * 1024 * 1024
F32 = jnp.float32
BF16 = jnp.bfloat16


def cost(microseconds):
    return pl.CostEstimate(flops=0, bytes_accessed=int(microseconds * 3.3e6), transcendentals=0)


def dft_tables(channels):
    per_half = channels // RADIX // CORES
    b = np.arange(RADIX)[None, :, None, None]
    e = np.arange(LANES)[None, None, None, :]
    d = np.arange(CORES * per_half).reshape(CORES, 1, per_half, 1)
    angle = (e * (RADIX * d + b) % channels) * (2.0 * math.pi / channels)
    cosine, sine = np.cos(angle), np.sin(angle)
    real_rows = np.concatenate([cosine, sine], axis=3)
    imag_rows = np.concatenate([-sine, cosine], axis=3)
    table = np.concatenate([real_rows, imag_rows], axis=2) / math.sqrt(channels)
    return table.astype(ml_dtypes.bfloat16)


def turned(value, step, size):
    re, im = value
    step %= size
    if step == 0:
        return re, im
    if 4 * step == size:
        return im, -re
    if 2 * step == size:
        return -re, -im
    if 4 * step == 3 * size:
        return -im, re
    cosine, sine = math.cos(2 * math.pi * step / size), math.sin(2 * math.pi * step / size)
    if 8 * step == size:
        return (re + im) * cosine, (im - re) * cosine
    if 8 * step == 3 * size:
        return (im - re) * sine, -(re + im) * sine
    return re * cosine + im * sine, im * cosine - re * sine


def four_points(values):
    (r0, i0), (r1, i1), (r2, i2), (r3, i3) = values
    sr, si, dr, di = r0 + r2, i0 + i2, r0 - r2, i0 - i2
    tr, ti, er, ei = r1 + r3, i1 + i3, r1 - r3, i1 - i3
    return [(sr + tr, si + ti), (dr + ei, di - er), (sr - tr, si - ti), (dr - ei, di + er)]


def sixteen_points(values):
    inner = [four_points([values[4 * a1 + a0] for a1 in range(4)]) for a0 in range(4)]
    result = [None] * 16
    for b0 in range(4):
        outer = four_points([turned(inner[a0][b0], a0 * b0, 16) for a0 in range(4)])
        for b1 in range(4):
            result[4 * b1 + b0] = outer[b1]
    return result


def after(block, *earlier):
    return pl.pallas_call(
        lambda *refs: None,
        out_shape=jax.ShapeDtypeStruct(block.shape, block.dtype),
        in_specs=[pl.BlockSpec(memory_space=pl.ANY)] * (1 + len(earlier)),
        out_specs=pl.BlockSpec(memory_space=pl.ANY),
        input_output_aliases={0: 0},
        cost_estimate=cost(0),
        name="after",
    )(block, *earlier)


def cut_kernel(mine, place, voltages, *rest):
    outs, (buffer, loads, stores) = rest[-3 - len(mine) : -3], rest[-3:]
    stations = buffer.shape[0]
    pieces = loads.shape[0]
    size = stations // pieces
    start = jnp.where(place[0] == mine[0][0], 0, stations)

    def load(k):
        return pltpu.make_async_copy(
            voltages.at[pl.ds(start + k * size, size)], buffer.at[pl.ds(k * size, size)], loads.at[k]
        )

    def store(k, i):
        source = buffer.at[pl.ds(k * size, size)]
        if mine[i][1] is not None:
            source = source.at[:, mine[i][1]]
        return pltpu.make_async_copy(source, outs[i].at[pl.ds(k * size, size)], stores.at[k, i])

    every = [(k, i) for k in range(pieces) for i in range(len(mine))]
    for k in range(pieces):
        load(k).start()
    for k in range(pieces):
        load(k).wait()
        for i in range(len(mine)):
            store(k, i).start()
    for k, i in every:
        store(k, i).wait()


def cut(place, voltages, mine, earlier=()):
    stations, pols, frames, parts, samples = voltages.shape
    half = stations // 2
    pieces = 4
    shapes = [(half,) + ((pols,) if pol is None else ()) + (frames, parts, samples) for _, pol in mine]
    anywhere = pl.BlockSpec(memory_space=pl.ANY)
    return pl.pallas_call(
        functools.partial(cut_kernel, mine),
        out_shape=[jax.ShapeDtypeStruct(shape, BF16) for shape in shapes],
        in_specs=[pl.BlockSpec(memory_space=pltpu.SMEM), anywhere] + [anywhere] * len(earlier),
        out_specs=[anywhere] * len(shapes),
        scratch_shapes=[
            pltpu.VMEM((half, pols, frames, parts, samples), BF16),
            pltpu.SemaphoreType.DMA((pieces,)),
            pltpu.SemaphoreType.DMA((pieces, len(mine))),
        ],
        compiler_params=pltpu.CompilerParams(vmem_limit_bytes=VMEM_LIMIT),
        cost_estimate=cost(2),
        name="cut",
    )(place, voltages, *earlier)


def weighted(taps, window, count, lanes, part, rows, sums):
    tap_count = taps.shape[0]
    tap_rows = [taps[k, :, lanes][None] for k in range(tap_count)]
    for j, ref, index in window:
        value = ref[index, part, rows, lanes].astype(F32).reshape(SB // 8, 8, LANES)
        for f in range(count):
            k = f - j
            if 0 <= k < tap_count:
                term = tap_rows[k] * value
                sums[f] = term if sums[f] is None else sums[f] + term
    return sums


def over_tiles(stations, samples, step):
    tiles, lane_tiles = stations // SB, samples // LANES

    def body(i, carry):
        lanes = pl.ds(pl.multiple_of(i % lane_tiles * LANES, LANES), LANES)
        rows = pl.ds(pl.multiple_of(i // (2 * lane_tiles) * SB, SB), SB)
        step(lanes, i // lane_tiles % 2, rows)
        return carry

    lax.fori_loop(0, 2 * tiles * lane_tiles, body, 0, unroll=2)


def near_kernel(place, taps, own, other, own_back, other_back, *rest):
    partial = rest[-1]
    frames = own.shape[0]
    count = 2 * frames

    def run(first, second, first_back, second_back):
        window = []
        for start, ref in ((-count, first_back), (frames - count, second_back), (0, first), (frames, second)):
            window += [(start + i, ref, i) for i in range(frames)]

        def step(lanes, part, rows):
            sums = weighted(taps, window, count, lanes, part, rows, [None] * count)
            for f in range(count):
                partial[f, part, rows, lanes] = sums[f].reshape(SB, LANES)

        over_tiles(*own.shape[2:], step)

    @pl.when(place[0] == 0)
    def _():
        run(own, other, own_back, other_back)

    @pl.when(place[0] == 1)
    def _():
        run(other, own, other_back, own_back)


def far_kernel(place, taps, partial, far, *rest):
    keep, send = rest[-2:]
    frames = keep.shape[0]
    count = 2 * frames
    history = taps.shape[0] - 1

    def run(first_out, second_out):
        window = [(i - history, far, i) for i in range(far.shape[0])]

        def step(lanes, part, rows):
            sums = [partial[f, part, rows, lanes].reshape(SB // 8, 8, LANES) for f in range(count)]
            sums = weighted(taps, window, count, lanes, part, rows, sums)
            for f in range(count):
                out = first_out if f < frames else second_out
                out[f % frames, part, rows, lanes] = sums[f].reshape(SB, LANES).astype(BF16)

        over_tiles(*keep.shape[2:], step)

    @pl.when(place[0] == 0)
    def _():
        run(keep, send)

    @pl.when(place[0] == 1)
    def _():
        run(send, keep)


def near_filter(place, taps, own, other, own_back, other_back, pol, earlier):
    frames, parts, stations, samples = other.shape
    block = 512
    both = pl.BlockSpec((None, frames, parts, stations, block), lambda i, place: (pol, 0, 0, 0, i))
    one = pl.BlockSpec((frames, parts, stations, block), lambda i, place: (0, 0, 0, i))
    return pl.pallas_call(
        near_kernel,
        out_shape=jax.ShapeDtypeStruct((2 * frames, parts, stations, samples), F32),
        grid_spec=pltpu.PrefetchScalarGridSpec(
            num_scalar_prefetch=1,
            grid=(samples // block,),
            in_specs=[pl.BlockSpec((taps.shape[0], 8, block), lambda i, place: (0, 0, i)), both, one, both, one]
            + [pl.BlockSpec(memory_space=pl.ANY)] * len(earlier),
            out_specs=pl.BlockSpec((2 * frames, parts, stations, block), lambda i, place: (0, 0, 0, i)),
        ),
        compiler_params=pltpu.CompilerParams(vmem_limit_bytes=VMEM_LIMIT),
        cost_estimate=cost(10),
        name="near",
    )(place, taps, own, other, own_back, other_back, *earlier)


def far_filter(place, taps, partial, far, low, earlier):
    count, parts, _, samples = partial.shape
    stations = far.shape[2]
    block = 512

    def spec(depth, where):
        return pl.BlockSpec((depth, parts, stations, block), lambda i, place: (0, 0, where, i))

    shape = jax.ShapeDtypeStruct((count // 2, parts, stations, samples), BF16)
    return pl.pallas_call(
        far_kernel,
        out_shape=(shape, shape),
        grid_spec=pltpu.PrefetchScalarGridSpec(
            num_scalar_prefetch=1,
            grid=(samples // block,),
            in_specs=[
                pl.BlockSpec((taps.shape[0], 8, block), lambda i, place: (0, 0, i)),
                spec(count, low // stations),
                spec(far.shape[0], 0),
            ]
            + [pl.BlockSpec(memory_space=pl.ANY)] * len(earlier),
            out_specs=[spec(count // 2, 0)] * 2,
        ),
        compiler_params=pltpu.CompilerParams(vmem_limit_bytes=VMEM_LIMIT),
        cost_estimate=cost(3),
        name="far",
    )(place, taps, partial, far, *earlier)


def onward_kernel(place, own_back, other_back, *rest):
    far = rest[-1]
    frames = own_back.shape[0]
    kept = far.shape[0] - frames

    def run(first, second):
        far[:kept] = first[frames - kept :]
        far[kept:] = second[...]

    @pl.when(place[0] == 0)
    def _():
        run(own_back, other_back)

    @pl.when(place[0] == 1)
    def _():
        run(other_back, own_back)


def onward(place, own_back, other_back, pol, low, stations, history, earlier=()):
    frames, parts, _, samples = other_back.shape
    where = low // stations
    return pl.pallas_call(
        onward_kernel,
        out_shape=jax.ShapeDtypeStruct((history, parts, stations, samples), BF16),
        grid_spec=pltpu.PrefetchScalarGridSpec(
            num_scalar_prefetch=1,
            grid=(parts,),
            in_specs=[
                pl.BlockSpec((None, frames, 1, stations, samples), lambda i, place: (pol, 0, i, where, 0)),
                pl.BlockSpec((frames, 1, stations, samples), lambda i, place: (0, i, where, 0)),
            ]
            + [pl.BlockSpec(memory_space=pl.ANY)] * len(earlier),
            out_specs=pl.BlockSpec((history, 1, stations, samples), lambda i, place: (0, i, 0, 0)),
        ),
        compiler_params=pltpu.CompilerParams(vmem_limit_bytes=VMEM_LIMIT),
        cost_estimate=cost(3 * stations / 32),
        name="onward",
    )(place, own_back, other_back, *earlier)


def weight_kernel(table, index, mask, *rest):
    out = rest[-1]
    groups, depth, width = out.shape
    beams = width // 2
    half = depth // 2
    rows = lax.broadcasted_iota(jnp.int32, (table.shape[0], beams), 0)
    for q in range(index.shape[0]):
        hit = jnp.where((rows == index[q : q + 1, :]) & (mask[q : q + 1, :] != 0), 1.0, 0.0).astype(BF16)
        picked = lax.dot_general(table[...], hit, (((0,), (0,)), ((), ())), preferred_element_type=F32)
        picked = picked.reshape(groups, 2, SB, beams)
        low = q * SB
        re, im = picked[:, 0], picked[:, 1]
        out[:, low : low + SB, :beams] = re.astype(BF16)
        out[:, low : low + SB, beams:] = im.astype(BF16)
        low += half
        out[:, low : low + SB, :beams] = (-im).astype(BF16)
        out[:, low : low + SB, beams:] = re.astype(BF16)


def beam_weights(table, index, mask, earlier):
    blocks, beams = index.shape
    groups = table.shape[1] // (2 * SB)
    shape = (groups, 2 * blocks * SB, 2 * beams)
    return pl.pallas_call(
        weight_kernel,
        out_shape=jax.ShapeDtypeStruct(shape, BF16),
        in_specs=[pl.BlockSpec(memory_space=pltpu.VMEM)] * 3 + [pl.BlockSpec(memory_space=pl.ANY)] * len(earlier),
        compiler_params=pltpu.CompilerParams(vmem_limit_bytes=VMEM_LIMIT),
        cost_estimate=cost(4),
        name="weights",
    )(table, index, mask, *earlier)


def beam_kernel(source_count, has_earlier, *refs):
    refs = list(refs)
    refs.pop(0)
    sources = [refs.pop(0) for _ in range(source_count)]
    table, weights = refs.pop(0), refs.pop(0)
    earlier = refs.pop(0) if has_earlier else None
    out, mixed, spectra = refs[:3]
    step = pl.program_id(0)
    frames = sources[0].shape[0]
    station_count = sum(ref.shape[2] for ref in sources)
    groups = spectra.shape[0]
    beams = weights.shape[2] // 2
    rows_of = table.shape[2] // 2 // groups
    pair = 2
    lane_tiles = beams // LANES
    per_channel = lane_tiles * frames

    @pl.when(step == 0)
    def _():
        low = 0
        for ref in sources:
            tiles = ref.shape[2] // SB

            def radix(i, carry, ref=ref, low=low, tiles=tiles):
                f, rows = i // tiles, pl.ds(pl.multiple_of(i % tiles * SB, SB), SB)
                values = [
                    tuple(ref[f, part, rows, a * LANES : (a + 1) * LANES].astype(F32) for part in range(2))
                    for a in range(RADIX)
                ]
                target = pl.ds(pl.multiple_of(f * station_count + low + i % tiles * SB, SB), SB)
                for b, (re, im) in enumerate(sixteen_points(values)):
                    mixed[b, target, :LANES] = re.astype(BF16)
                    mixed[b, target, LANES:] = im.astype(BF16)
                return carry

            lax.fori_loop(0, frames * tiles, radix, 0)
            low += ref.shape[2]

        def transform(b, carry):
            for start in range(0, frames, pair):
                product = lax.dot_general(
                    table[0, b],
                    mixed[b, start * station_count : (start + pair) * station_count],
                    (((1,), (1,)), ((), ())),
                    preferred_element_type=F32,
                )
                product = product.reshape(2, groups, rows_of, pair * station_count)
                rows = slice(start * rows_of, (start + pair) * rows_of)
                for part in range(2):
                    value = jnp.concatenate(
                        [product[part, :, :, f * station_count : (f + 1) * station_count] for f in range(pair)], axis=1
                    )
                    columns = slice(part * station_count, (part + 1) * station_count)
                    spectra[:, b, rows, columns] = value.astype(BF16)
            return carry

        lax.fori_loop(0, RADIX, transform, 0, unroll=4)

    for k in range(weights.shape[0]):
        rows = spectra[step * weights.shape[0] + k].reshape(RADIX * frames * rows_of, 2 * station_count)
        beam = jnp.dot(rows, weights[k], preferred_element_type=F32)
        re, im = beam[:, :beams], beam[:, beams:]
        power = re * re + im * im
        if not has_earlier:
            out[k] = power
            continue
        power = power + earlier[k]
        for b in range(RADIX):
            for f in range(frames):
                at = (b * frames + f) * rows_of
                for t in range(lane_tiles):
                    start = (k * rows_of * RADIX + b) * per_channel + t * frames + f
                    refs[3][pl.ds(start, rows_of, stride=RADIX * per_channel), :] = power[
                        at : at + rows_of, t * LANES : (t + 1) * LANES
                    ]

    if has_earlier:

        def finish(c, carry):
            value = refs[3][pl.ds(pl.multiple_of(c * per_channel, per_channel), per_channel), :]
            for t in range(lane_tiles):
                out[c, :, t * LANES : (t + 1) * LANES] = value[t * frames : (t + 1) * frames]
            return carry

        lax.fori_loop(0, out.shape[0], finish, 0, unroll=8)


def beam_power(place, sources, table, weights, earlier, channels):
    frames, _, _, samples = sources[0].shape
    groups, depth, width = weights.shape
    beams = width // 2
    station_count = sum(s.shape[2] for s in sources)
    at_once = 2
    flat = (groups, channels // groups * frames, beams)
    flat_spec = pl.BlockSpec((at_once,) + flat[1:], lambda i, place: (i, 0, 0))
    in_specs = [pl.BlockSpec(s.shape, lambda i, place: (0, 0, 0, 0)) for s in sources]
    in_specs += [
        pl.BlockSpec((1,) + table.shape[1:], lambda i, place: (place[1], 0, 0, 0)),
        pl.BlockSpec((at_once, depth, width), lambda i, place: (i, 0, 0)),
    ]
    operands = list(sources) + [table, weights]
    scratch = [
        pltpu.VMEM((RADIX, frames * station_count, 2 * LANES), BF16),
        pltpu.VMEM((groups, RADIX, frames * channels // groups // RADIX, 2 * station_count), BF16),
    ]
    if earlier is None:
        out_shape = jax.ShapeDtypeStruct(flat, F32)
        out_spec = flat_spec
    else:
        out_shape = jax.ShapeDtypeStruct((channels, frames, beams), F32)
        out_spec = pl.BlockSpec((channels // groups * at_once, frames, beams), lambda i, place: (i, 0, 0))
        operands.append(earlier)
        in_specs.append(flat_spec)
        scratch.append(pltpu.VMEM((math.prod(out_spec.block_shape) // LANES, LANES), F32))
    return pl.pallas_call(
        functools.partial(beam_kernel, len(sources), earlier is not None),
        out_shape=out_shape,
        grid_spec=pltpu.PrefetchScalarGridSpec(
            num_scalar_prefetch=1,
            grid=(groups // at_once,),
            in_specs=in_specs,
            out_specs=out_spec,
            scratch_shapes=scratch,
        ),
        compiler_params=pltpu.CompilerParams(vmem_limit_bytes=VMEM_LIMIT),
        cost_estimate=cost(0),
        name="beams",
    )(place, *operands)


def flipped(rows, bit):
    return jnp.where(bit == 1, rows[::-1], rows)


def body(voltages, filter_taps, use_mask, block_index, weight_blocks):
    stations, pols, frames, parts, samples = voltages.shape
    history = filter_taps.shape[0] - 1
    half = stations // 2
    time_devices = lax.axis_size("tm")
    side = lax.axis_index("tm") % 2
    core = lax.axis_index("stn")
    place = jnp.stack([side, core]).astype(jnp.int32)

    def pair(block):
        return lax.ppermute(block, "tm", [(i, i ^ 1) for i in range(time_devices)])

    def hop(block, skip=0):
        return lax.ppermute(block, "tm", [(i, i + 2) for i in range(skip, time_devices - 2)])

    def swap(block):
        return lax.ppermute(block, "stn", [(0, 1), (1, 0)])

    def laid(block):
        return jnp.moveaxis(block, 0, -2)

    columns = weight_blocks.shape[1] // CORES
    shard = lax.dynamic_slice_in_dim(weight_blocks, core * columns, columns, 1)

    def doubled(block, distance):
        arrived = lax.ppermute(block, "tm", [(i, i ^ distance) for i in range(time_devices)])
        return jnp.concatenate([block, arrived])

    for distance in (1, 2):
        shard = doubled(shard, distance)
    (own,) = cut(place, voltages, [(0, None)], [shard])
    distance = 4
    while distance < time_devices:
        shard = doubled(shard, distance)
        distance *= 2
    other = cut(place, voltages, [(1, pol) for pol in range(pols)])
    own_back = laid(after(hop(own)))
    own = laid(own)
    other = [pair(block) for block in other]
    other = [laid(after(other[0]))] + [laid(after(block, shard)) for block in other[1:]]

    def ordered(rows):
        rows = rows.T.reshape(2, 2, 2, -1)
        rows = flipped(rows, core)
        rows = flipped(rows.swapaxes(0, 1), side).swapaxes(0, 1)
        return rows.reshape(8, -1)

    index = block_index ^ (lax.axis_index("tm") * weight_blocks.shape[0])
    weights = beam_weights(shard, ordered(index), ordered(use_mask), other)
    table = jnp.asarray(dft_tables(samples))
    taps = jnp.broadcast_to(filter_taps[:, None, :], (history + 1, 8, samples))

    quarter = half // 2
    chunks = [(pol, low) for pol in range(pols) for low in (0, quarter)]
    other_back = [hop(other[0])]
    further, partial = [], []
    for pol, low in chunks:
        if pol >= len(other_back):
            other_back.append(hop(after(other[pol], further[0])))
        further.append(onward(place, own_back, other_back[pol], pol, low, quarter, history - 2 * frames))
        if low:
            partial.append(near_filter(place, taps, own, other[pol], own_back, other_back[pol], pol, further[-2:] + [weights]))
    far = [hop(block, 2) for block in further]
    keeps, sents, power = [], [], None
    for k, (pol, low) in enumerate(chunks):
        earlier = sents[-1:] + ([power] if k == len(chunks) - 1 else [])
        keep, send = far_filter(place, taps, partial[pol], far[k], low, earlier)
        keeps.append(keep)
        sents.append(pair(send))
        if low:
            sources = keeps[-2:] + sents[-2:]
            sources += [swap(block) for block in sources]
            power = beam_power(place, sources, table, weights, power, samples // CORES)
    return power


def solution(mesh):
    in_specs = (
        P(("parts", "stn"), None, "tm", None, None),
        P(),
        P("parts", None),
        P("parts", None),
        P("tm", None),
    )
    out_specs = P("stn", "tm", "parts")
    return jax.shard_map(body, mesh=mesh, in_specs=in_specs, out_specs=out_specs, check_vma=False)
```

```python
import functools
import math

import jax
import jax.numpy as jnp
import ml_dtypes
import numpy as np
from jax import lax
from jax.experimental import pallas as pl
from jax.experimental.pallas import tpu as pltpu
from jax.sharding import PartitionSpec as P

SB = 16
G = 16
RADIX = 16
LANES = 128
CORES = 2
VMEM_LIMIT = 56 * 1024 * 1024
F32 = jnp.float32
BF16 = jnp.bfloat16


def cost(microseconds):
    return pl.CostEstimate(flops=0, bytes_accessed=int(microseconds * 3.3e6), transcendentals=0)


def dft_tables(channels):
    per_half = channels // RADIX // CORES
    b = np.arange(RADIX)[None, :, None, None]
    e = np.arange(LANES)[None, None, None, :]
    d = np.arange(CORES * per_half).reshape(CORES, 1, per_half, 1)
    angle = (e * (RADIX * d + b) % channels) * (2.0 * math.pi / channels)
    cosine, sine = np.cos(angle), np.sin(angle)
    real_rows = np.concatenate([cosine, sine], axis=3)
    imag_rows = np.concatenate([-sine, cosine], axis=3)
    table = np.concatenate([real_rows, imag_rows], axis=2) / math.sqrt(channels)
    return table.astype(ml_dtypes.bfloat16)


def turned(value, step, size):
    re, im = value
    step %= size
    if step == 0:
        return re, im
    if 4 * step == size:
        return im, -re
    if 2 * step == size:
        return -re, -im
    if 4 * step == 3 * size:
        return -im, re
    cosine, sine = math.cos(2 * math.pi * step / size), math.sin(2 * math.pi * step / size)
    if 8 * step == size:
        return (re + im) * cosine, (im - re) * cosine
    if 8 * step == 3 * size:
        return (im - re) * sine, -(re + im) * sine
    return re * cosine + im * sine, im * cosine - re * sine


def four_points(values):
    (r0, i0), (r1, i1), (r2, i2), (r3, i3) = values
    sr, si, dr, di = r0 + r2, i0 + i2, r0 - r2, i0 - i2
    tr, ti, er, ei = r1 + r3, i1 + i3, r1 - r3, i1 - i3
    return [(sr + tr, si + ti), (dr + ei, di - er), (sr - tr, si - ti), (dr - ei, di + er)]


def sixteen_points(values):
    inner = [four_points([values[4 * a1 + a0] for a1 in range(4)]) for a0 in range(4)]
    result = [None] * 16
    for b0 in range(4):
        outer = four_points([turned(inner[a0][b0], a0 * b0, 16) for a0 in range(4)])
        for b1 in range(4):
            result[4 * b1 + b0] = outer[b1]
    return result


def after(block, *earlier):
    return pl.pallas_call(
        lambda *refs: None,
        out_shape=jax.ShapeDtypeStruct(block.shape, block.dtype),
        in_specs=[pl.BlockSpec(memory_space=pl.ANY)] * (1 + len(earlier)),
        out_specs=pl.BlockSpec(memory_space=pl.ANY),
        input_output_aliases={0: 0},
        cost_estimate=cost(0),
        name="after",
    )(block, *earlier)


def cut_kernel(mine, place, voltages, *rest):
    outs, (buffer, loads, stores) = rest[-3 - len(mine) : -3], rest[-3:]
    stations = buffer.shape[0]
    pieces = loads.shape[0]
    size = stations // pieces
    start = jnp.where(place[0] == mine[0][0], 0, stations)

    def load(k):
        return pltpu.make_async_copy(
            voltages.at[pl.ds(start + k * size, size)], buffer.at[pl.ds(k * size, size)], loads.at[k]
        )

    def store(k, i):
        source = buffer.at[pl.ds(k * size, size)]
        if mine[i][1] is not None:
            source = source.at[:, mine[i][1]]
        return pltpu.make_async_copy(source, outs[i].at[pl.ds(k * size, size)], stores.at[k, i])

    every = [(k, i) for k in range(pieces) for i in range(len(mine))]
    for k in range(pieces):
        load(k).start()
    for k in range(pieces):
        load(k).wait()
        for i in range(len(mine)):
            store(k, i).start()
    for k, i in every:
        store(k, i).wait()


def cut(place, voltages, mine, earlier=()):
    stations, pols, frames, parts, samples = voltages.shape
    half = stations // 2
    pieces = 4
    shapes = [(half,) + ((pols,) if pol is None else ()) + (frames, parts, samples) for _, pol in mine]
    anywhere = pl.BlockSpec(memory_space=pl.ANY)
    return pl.pallas_call(
        functools.partial(cut_kernel, mine),
        out_shape=[jax.ShapeDtypeStruct(shape, BF16) for shape in shapes],
        in_specs=[pl.BlockSpec(memory_space=pltpu.SMEM), anywhere] + [anywhere] * len(earlier),
        out_specs=[anywhere] * len(shapes),
        scratch_shapes=[
            pltpu.VMEM((half, pols, frames, parts, samples), BF16),
            pltpu.SemaphoreType.DMA((pieces,)),
            pltpu.SemaphoreType.DMA((pieces, len(mine))),
        ],
        compiler_params=pltpu.CompilerParams(vmem_limit_bytes=VMEM_LIMIT),
        cost_estimate=cost(2),
        name="cut",
    )(place, voltages, *earlier)


def weighted(taps, window, count, lanes, part, rows, sums):
    tap_count = taps.shape[0]
    tap_rows = [taps[k, :, lanes][None] for k in range(tap_count)]
    for j, ref, index in window:
        value = ref[index, part, rows, lanes].astype(F32).reshape(SB // 8, 8, LANES)
        for f in range(count):
            k = f - j
            if 0 <= k < tap_count:
                term = tap_rows[k] * value
                sums[f] = term if sums[f] is None else sums[f] + term
    return sums


def over_tiles(stations, samples, step):
    tiles, lane_tiles = stations // SB, samples // LANES

    def body(i, carry):
        lanes = pl.ds(pl.multiple_of(i % lane_tiles * LANES, LANES), LANES)
        rows = pl.ds(pl.multiple_of(i // (2 * lane_tiles) * SB, SB), SB)
        step(lanes, i // lane_tiles % 2, rows)
        return carry

    lax.fori_loop(0, 2 * tiles * lane_tiles, body, 0, unroll=2)


def near_kernel(place, taps, own, other, own_back, other_back, *rest):
    partial = rest[-1]
    frames = own.shape[0]
    count = 2 * frames

    def run(first, second, first_back, second_back):
        window = []
        for start, ref in ((-count, first_back), (frames - count, second_back), (0, first), (frames, second)):
            window += [(start + i, ref, i) for i in range(frames)]

        def step(lanes, part, rows):
            sums = weighted(taps, window, count, lanes, part, rows, [None] * count)
            for f in range(count):
                partial[f, part, rows, lanes] = sums[f].reshape(SB, LANES)

        over_tiles(*own.shape[2:], step)

    @pl.when(place[0] == 0)
    def _():
        run(own, other, own_back, other_back)

    @pl.when(place[0] == 1)
    def _():
        run(other, own, other_back, own_back)


def far_kernel(place, taps, partial, far, *rest):
    keep, send = rest[-2:]
    frames = keep.shape[0]
    count = 2 * frames
    history = taps.shape[0] - 1

    def run(first_out, second_out):
        window = [(i - history, far, i) for i in range(far.shape[0])]

        def step(lanes, part, rows):
            sums = [partial[f, part, rows, lanes].reshape(SB // 8, 8, LANES) for f in range(count)]
            sums = weighted(taps, window, count, lanes, part, rows, sums)
            for f in range(count):
                out = first_out if f < frames else second_out
                out[f % frames, part, rows, lanes] = sums[f].reshape(SB, LANES).astype(BF16)

        over_tiles(*keep.shape[2:], step)

    @pl.when(place[0] == 0)
    def _():
        run(keep, send)

    @pl.when(place[0] == 1)
    def _():
        run(send, keep)


def near_filter(place, taps, own, other, own_back, other_back, pol, earlier):
    frames, parts, stations, samples = other.shape
    block = 512
    both = pl.BlockSpec((None, frames, parts, stations, block), lambda i, place: (pol, 0, 0, 0, i))
    one = pl.BlockSpec((frames, parts, stations, block), lambda i, place: (0, 0, 0, i))
    return pl.pallas_call(
        near_kernel,
        out_shape=jax.ShapeDtypeStruct((2 * frames, parts, stations, samples), F32),
        grid_spec=pltpu.PrefetchScalarGridSpec(
            num_scalar_prefetch=1,
            grid=(samples // block,),
            in_specs=[pl.BlockSpec((taps.shape[0], 8, block), lambda i, place: (0, 0, i)), both, one, both, one]
            + [pl.BlockSpec(memory_space=pl.ANY)] * len(earlier),
            out_specs=pl.BlockSpec((2 * frames, parts, stations, block), lambda i, place: (0, 0, 0, i)),
        ),
        compiler_params=pltpu.CompilerParams(vmem_limit_bytes=VMEM_LIMIT),
        cost_estimate=cost(10),
        name="near",
    )(place, taps, own, other, own_back, other_back, *earlier)


def far_filter(place, taps, partial, far, low, earlier):
    count, parts, _, samples = partial.shape
    stations = far.shape[2]
    block = samples // 2

    def spec(depth, where):
        return pl.BlockSpec((depth, parts, stations, block), lambda i, place: (0, 0, where, i))

    shape = jax.ShapeDtypeStruct((count // 2, parts, stations, samples), BF16)
    return pl.pallas_call(
        far_kernel,
        out_shape=(shape, shape),
        grid_spec=pltpu.PrefetchScalarGridSpec(
            num_scalar_prefetch=1,
            grid=(samples // block,),
            in_specs=[
                pl.BlockSpec((taps.shape[0], 8, block), lambda i, place: (0, 0, i)),
                spec(count, low // stations),
                spec(far.shape[0], 0),
            ]
            + [pl.BlockSpec(memory_space=pl.ANY)] * len(earlier),
            out_specs=[spec(count // 2, 0)] * 2,
        ),
        compiler_params=pltpu.CompilerParams(vmem_limit_bytes=VMEM_LIMIT),
        cost_estimate=cost(3),
        name="far",
    )(place, taps, partial, far, *earlier)


def onward_kernel(place, own_back, other_back, *rest):
    far = rest[-1]
    frames = own_back.shape[0]
    kept = far.shape[0] - frames

    def run(first, second):
        far[:kept] = first[frames - kept :]
        far[kept:] = second[...]

    @pl.when(place[0] == 0)
    def _():
        run(own_back, other_back)

    @pl.when(place[0] == 1)
    def _():
        run(other_back, own_back)


def onward(place, own_back, other_back, pol, low, stations, history, earlier=()):
    frames, parts, _, samples = other_back.shape
    where = low // stations
    return pl.pallas_call(
        onward_kernel,
        out_shape=jax.ShapeDtypeStruct((history, parts, stations, samples), BF16),
        grid_spec=pltpu.PrefetchScalarGridSpec(
            num_scalar_prefetch=1,
            grid=(parts,),
            in_specs=[
                pl.BlockSpec((None, frames, 1, stations, samples), lambda i, place: (pol, 0, i, where, 0)),
                pl.BlockSpec((frames, 1, stations, samples), lambda i, place: (0, i, where, 0)),
            ]
            + [pl.BlockSpec(memory_space=pl.ANY)] * len(earlier),
            out_specs=pl.BlockSpec((history, 1, stations, samples), lambda i, place: (0, i, 0, 0)),
        ),
        compiler_params=pltpu.CompilerParams(vmem_limit_bytes=VMEM_LIMIT),
        cost_estimate=cost(3 * stations / 32),
        name="onward",
    )(place, own_back, other_back, *earlier)


def weight_kernel(table, index, mask, *rest):
    out = rest[-1]
    groups, depth, width = out.shape
    beams = width // 2
    half = depth // 2
    rows = lax.broadcasted_iota(jnp.int32, (table.shape[0], beams), 0)
    for q in range(index.shape[0]):
        hit = jnp.where((rows == index[q : q + 1, :]) & (mask[q : q + 1, :] != 0), 1.0, 0.0).astype(BF16)
        picked = lax.dot_general(table[...], hit, (((0,), (0,)), ((), ())), preferred_element_type=F32)
        picked = picked.reshape(groups, 2, SB, beams)
        low = q * SB
        re, im = picked[:, 0], picked[:, 1]
        out[:, low : low + SB, :beams] = re.astype(BF16)
        out[:, low : low + SB, beams:] = im.astype(BF16)
        low += half
        out[:, low : low + SB, :beams] = (-im).astype(BF16)
        out[:, low : low + SB, beams:] = re.astype(BF16)


def beam_weights(table, index, mask, earlier):
    blocks, beams = index.shape
    groups = table.shape[1] // (2 * SB)
    shape = (groups, 2 * blocks * SB, 2 * beams)
    return pl.pallas_call(
        weight_kernel,
        out_shape=jax.ShapeDtypeStruct(shape, BF16),
        in_specs=[pl.BlockSpec(memory_space=pltpu.VMEM)] * 3 + [pl.BlockSpec(memory_space=pl.ANY)] * len(earlier),
        compiler_params=pltpu.CompilerParams(vmem_limit_bytes=VMEM_LIMIT),
        cost_estimate=cost(4),
        name="weights",
    )(table, index, mask, *earlier)


def beam_kernel(source_count, has_earlier, *refs):
    refs = list(refs)
    refs.pop(0)
    sources = [refs.pop(0) for _ in range(source_count)]
    table, weights = refs.pop(0), refs.pop(0)
    earlier = refs.pop(0) if has_earlier else None
    out, mixed, spectra, sems, *refs = refs
    held, refs = refs[:source_count], refs[source_count:]
    step = pl.program_id(0)
    frames = sources[0].shape[0]
    station_count = sum(ref.shape[2] for ref in sources)
    groups = spectra.shape[0]
    beams = weights.shape[2] // 2
    rows_of = table.shape[2] // 2 // groups
    pair = 2
    lane_tiles = beams // LANES
    per_channel = lane_tiles * frames

    @pl.when(step == 0)
    def _():
        low = 0
        copies = [pltpu.make_async_copy(ref, to, sems.at[k]) for k, (ref, to) in enumerate(zip(sources, held))]
        for copy in copies:
            copy.start()
        for copy, ref in zip(copies, held):
            copy.wait()
            tiles = ref.shape[2] // SB

            def radix(i, carry, ref=ref, low=low, tiles=tiles):
                f, rows = i // tiles, pl.ds(pl.multiple_of(i % tiles * SB, SB), SB)
                values = [
                    tuple(ref[f, part, rows, a * LANES : (a + 1) * LANES].astype(F32) for part in range(2))
                    for a in range(RADIX)
                ]
                target = pl.ds(pl.multiple_of(f * station_count + low + i % tiles * SB, SB), SB)
                for b, (re, im) in enumerate(sixteen_points(values)):
                    mixed[b, target, :LANES] = re.astype(BF16)
                    mixed[b, target, LANES:] = im.astype(BF16)
                return carry

            lax.fori_loop(0, frames * tiles, radix, 0)
            low += ref.shape[2]

        def transform(b, carry):
            for start in range(0, frames, pair):
                product = lax.dot_general(
                    table[0, b],
                    mixed[b, start * station_count : (start + pair) * station_count],
                    (((1,), (1,)), ((), ())),
                    preferred_element_type=F32,
                )
                product = product.reshape(2, groups, rows_of, pair * station_count)
                rows = slice(start * rows_of, (start + pair) * rows_of)
                for part in range(2):
                    value = jnp.concatenate(
                        [product[part, :, :, f * station_count : (f + 1) * station_count] for f in range(pair)], axis=1
                    )
                    columns = slice(part * station_count, (part + 1) * station_count)
                    spectra[:, b, rows, columns] = value.astype(BF16)
            return carry

        lax.fori_loop(0, RADIX, transform, 0, unroll=4)

    for k in range(weights.shape[0]):
        rows = spectra[step * weights.shape[0] + k].reshape(RADIX * frames * rows_of, 2 * station_count)
        beam = jnp.dot(rows, weights[k], preferred_element_type=F32)
        re, im = beam[:, :beams], beam[:, beams:]
        power = re * re + im * im
        if not has_earlier:
            out[k] = power
            continue
        power = power + earlier[k]
        for b in range(RADIX):
            for f in range(frames):
                at = (b * frames + f) * rows_of
                for t in range(lane_tiles):
                    start = (k * rows_of * RADIX + b) * per_channel + t * frames + f
                    refs[0][pl.ds(start, rows_of, stride=RADIX * per_channel), :] = power[
                        at : at + rows_of, t * LANES : (t + 1) * LANES
                    ]

    if has_earlier:

        def finish(c, carry):
            value = refs[0][pl.ds(pl.multiple_of(c * per_channel, per_channel), per_channel), :]
            for t in range(lane_tiles):
                out[c, :, t * LANES : (t + 1) * LANES] = value[t * frames : (t + 1) * frames]
            return carry

        lax.fori_loop(0, out.shape[0], finish, 0, unroll=8)


def beam_power(place, sources, table, weights, earlier, channels):
    frames, _, _, samples = sources[0].shape
    groups, depth, width = weights.shape
    beams = width // 2
    station_count = sum(s.shape[2] for s in sources)
    at_once = 2
    flat = (groups, channels // groups * frames, beams)
    flat_spec = pl.BlockSpec((at_once,) + flat[1:], lambda i, place: (i, 0, 0))
    in_specs = [pl.BlockSpec(memory_space=pltpu.HBM) for s in sources]
    in_specs += [
        pl.BlockSpec((1,) + table.shape[1:], lambda i, place: (place[1], 0, 0, 0)),
        pl.BlockSpec((at_once, depth, width), lambda i, place: (i, 0, 0)),
    ]
    operands = list(sources) + [table, weights]
    scratch = [
        pltpu.VMEM((RADIX, frames * station_count, 2 * LANES), BF16),
        pltpu.VMEM((groups, RADIX, frames * channels // groups // RADIX, 2 * station_count), BF16),
        pltpu.SemaphoreType.DMA((len(sources),)),
    ]
    scratch += [pltpu.VMEM(s.shape, BF16) for s in sources]
    if earlier is None:
        out_shape = jax.ShapeDtypeStruct(flat, F32)
        out_spec = flat_spec
    else:
        out_shape = jax.ShapeDtypeStruct((channels, frames, beams), F32)
        out_spec = pl.BlockSpec((channels // groups * at_once, frames, beams), lambda i, place: (i, 0, 0))
        operands.append(earlier)
        in_specs.append(flat_spec)
        scratch.append(pltpu.VMEM((math.prod(out_spec.block_shape) // LANES, LANES), F32))
    return pl.pallas_call(
        functools.partial(beam_kernel, len(sources), earlier is not None),
        out_shape=out_shape,
        grid_spec=pltpu.PrefetchScalarGridSpec(
            num_scalar_prefetch=1,
            grid=(groups // at_once,),
            in_specs=in_specs,
            out_specs=out_spec,
            scratch_shapes=scratch,
        ),
        compiler_params=pltpu.CompilerParams(vmem_limit_bytes=VMEM_LIMIT),
        cost_estimate=cost(0),
        name="beams",
    )(place, *operands)


def flipped(rows, bit):
    return jnp.where(bit == 1, rows[::-1], rows)


def body(voltages, filter_taps, use_mask, block_index, weight_blocks):
    stations, pols, frames, parts, samples = voltages.shape
    history = filter_taps.shape[0] - 1
    half = stations // 2
    time_devices = lax.axis_size("tm")
    side = lax.axis_index("tm") % 2
    core = lax.axis_index("stn")
    place = jnp.stack([side, core]).astype(jnp.int32)

    def pair(block):
        return lax.ppermute(block, "tm", [(i, i ^ 1) for i in range(time_devices)])

    def hop(block, skip=0):
        return lax.ppermute(block, "tm", [(i, i + 2) for i in range(skip, time_devices - 2)])

    def swap(block):
        return lax.ppermute(block, "stn", [(0, 1), (1, 0)])

    def laid(block):
        return jnp.moveaxis(block, 0, -2)

    columns = weight_blocks.shape[1] // CORES
    shard = lax.dynamic_slice_in_dim(weight_blocks, core * columns, columns, 1)
    shards = [shard] + [
        lax.ppermute(shard, "tm", [(i, i ^ far) for i in range(time_devices)]) for far in range(2, time_devices, 2)
    ]
    (own,) = cut(place, voltages, [(0, None)])
    own = after(own, *shards[1:])
    other = cut(place, voltages, [(1, pol) for pol in range(pols)], [own])
    own_back = laid(after(hop(own)))
    own = laid(own)
    other = [laid(after(pair(block))) for block in other]
    shards = jnp.concatenate(shards)
    shards = jnp.concatenate([shards, pair(shards)])

    def ordered(rows):
        rows = rows.T.reshape(2, 2, 2, -1)
        rows = flipped(rows, core)
        rows = flipped(rows.swapaxes(0, 1), side).swapaxes(0, 1)
        return rows.reshape(8, -1)

    each = weight_blocks.shape[0]
    apart = block_index // each ^ lax.axis_index("tm")
    index = (apart % 2 * (time_devices // 2) + apart // 2) * each + block_index % each
    weights = beam_weights(shards, ordered(index), ordered(use_mask), other)
    table = jnp.asarray(dft_tables(samples))
    taps = jnp.broadcast_to(filter_taps[:, None, :], (history + 1, 8, samples))

    quarter = half // 2
    chunks = [(pol, low) for pol in range(pols) for low in (0, quarter)]
    other_back = [hop(other[0])]
    further, partial = [], []
    for pol, low in chunks:
        if pol >= len(other_back):
            other_back.append(hop(after(other[pol], further[0])))
        further.append(onward(place, own_back, other_back[pol], pol, low, quarter, history - 2 * frames))
        if low:
            partial.append(near_filter(place, taps, own, other[pol], own_back, other_back[pol], pol, further[-2:] + [weights]))
    far = [hop(block, 2) for block in further]
    keeps, sents, power = [], [], None
    for k, (pol, low) in enumerate(chunks):
        earlier = sents[-1:] + ([power] if k == len(chunks) - 1 else []) + (partial[1:] if k == 1 else [])
        keep, send = far_filter(place, taps, partial[pol], far[k], low, earlier)
        keeps.append(keep)
        sents.append(pair(send))
        if low:
            sources = keeps[-2:] + sents[-2:]
            sources += [swap(block) for block in sources]
            power = beam_power(place, sources, table, weights, power, samples // CORES)
    return power


def solution(mesh):
    in_specs = (
        P(("parts", "stn"), None, "tm", None, None),
        P(),
        P("parts", None),
        P("parts", None),
        P("tm", None),
    )
    out_specs = P("stn", "tm", "parts")
    return jax.shard_map(body, mesh=mesh, in_specs=in_specs, out_specs=out_specs, check_vma=False)
```

```python
import functools
import math

import jax
import jax.numpy as jnp
import ml_dtypes
import numpy as np
from jax import lax
from jax.experimental import pallas as pl
from jax.experimental.pallas import tpu as pltpu
from jax.sharding import PartitionSpec as P

SB = 16
G = 16
RADIX = 16
LANES = 128
CORES = 2
VMEM_LIMIT = 56 * 1024 * 1024
F32 = jnp.float32
BF16 = jnp.bfloat16


def cost(microseconds):
    return pl.CostEstimate(flops=0, bytes_accessed=int(microseconds * 3.3e6), transcendentals=0)


def dft_tables(channels):
    per_half = channels // RADIX // CORES
    b = np.arange(RADIX)[None, :, None, None]
    e = np.arange(LANES)[None, None, None, :]
    d = np.arange(CORES * per_half).reshape(CORES, 1, per_half, 1)
    angle = (e * (RADIX * d + b) % channels) * (2.0 * math.pi / channels)
    cosine, sine = np.cos(angle), np.sin(angle)
    real_rows = np.concatenate([cosine, sine], axis=3)
    imag_rows = np.concatenate([-sine, cosine], axis=3)
    table = np.concatenate([real_rows, imag_rows], axis=2) / math.sqrt(channels)
    return table.astype(ml_dtypes.bfloat16)


def turned(value, step, size):
    re, im = value
    step %= size
    if step == 0:
        return re, im
    if 4 * step == size:
        return im, -re
    if 2 * step == size:
        return -re, -im
    if 4 * step == 3 * size:
        return -im, re
    cosine, sine = math.cos(2 * math.pi * step / size), math.sin(2 * math.pi * step / size)
    if 8 * step == size:
        return (re + im) * cosine, (im - re) * cosine
    if 8 * step == 3 * size:
        return (im - re) * sine, -(re + im) * sine
    return re * cosine + im * sine, im * cosine - re * sine


def four_points(values):
    (r0, i0), (r1, i1), (r2, i2), (r3, i3) = values
    sr, si, dr, di = r0 + r2, i0 + i2, r0 - r2, i0 - i2
    tr, ti, er, ei = r1 + r3, i1 + i3, r1 - r3, i1 - i3
    return [(sr + tr, si + ti), (dr + ei, di - er), (sr - tr, si - ti), (dr - ei, di + er)]


def sixteen_points(values):
    inner = [four_points([values[4 * a1 + a0] for a1 in range(4)]) for a0 in range(4)]
    result = [None] * 16
    for b0 in range(4):
        outer = four_points([turned(inner[a0][b0], a0 * b0, 16) for a0 in range(4)])
        for b1 in range(4):
            result[4 * b1 + b0] = outer[b1]
    return result


def after(block, *earlier):
    return pl.pallas_call(
        lambda *refs: None,
        out_shape=jax.ShapeDtypeStruct(block.shape, block.dtype),
        in_specs=[pl.BlockSpec(memory_space=pl.ANY)] * (1 + len(earlier)),
        out_specs=pl.BlockSpec(memory_space=pl.ANY),
        input_output_aliases={0: 0},
        cost_estimate=cost(0),
        name="after",
    )(block, *earlier)


def cut_kernel(cuts, place, voltages, *rest):
    (own, *outs), (buffer, loads, stores) = rest[-4 - len(cuts) : -3], rest[-3:]
    half = own.shape[0]
    pieces = loads.shape[1]
    size = half // pieces
    side = place[0]

    def load(h, k):
        start = jnp.where(side == h, 0, half) + k * size
        return pltpu.make_async_copy(
            voltages.at[pl.ds(start, size)], buffer.at[h, pl.ds(k * size, size)], loads.at[h, k]
        )

    def store(h, k):
        copies = []
        if h == 0:
            copies.append(pltpu.make_async_copy(buffer.at[0, pl.ds(k * size, size)], own.at[pl.ds(k * size, size)], stores.at[0, k]))
        else:
            for pol in range(voltages.shape[1]):
                for out, (which, low, count) in zip(outs, cuts):
                    if which == pol and low <= k * size < low + count:
                        copies.append(
                            pltpu.make_async_copy(
                                buffer.at[1, pl.ds(k * size, size), pol],
                                out.at[pl.ds(k * size - low, size)],
                                stores.at[1 + pol, k],
                            )
                        )
        return copies

    order = [(h, k) for h in range(2) for k in range(pieces)]
    for h, k in order:
        load(h, k).start()
    for h, k in order:
        load(h, k).wait()
        for copy in store(h, k):
            copy.start()
    for h, k in order:
        for copy in store(h, k):
            copy.wait()


def cut(place, voltages, cuts, earlier):
    stations, pols, frames, parts, samples = voltages.shape
    half = stations // 2
    pieces = 4
    shapes = [(half, pols, frames, parts, samples)] + [(size, frames, parts, samples) for _, _, size in cuts]
    anywhere = pl.BlockSpec(memory_space=pltpu.HBM)
    return pl.pallas_call(
        functools.partial(cut_kernel, cuts),
        out_shape=[jax.ShapeDtypeStruct(shape, BF16) for shape in shapes],
        in_specs=[pl.BlockSpec(memory_space=pltpu.SMEM), anywhere] + [pl.BlockSpec(memory_space=pl.ANY)] * len(earlier),
        out_specs=[anywhere] * len(shapes),
        scratch_shapes=[
            pltpu.VMEM((2,) + shapes[0], BF16),
            pltpu.SemaphoreType.DMA((2, pieces)),
            pltpu.SemaphoreType.DMA((1 + pols, pieces)),
        ],
        compiler_params=pltpu.CompilerParams(vmem_limit_bytes=VMEM_LIMIT),
        cost_estimate=cost(4),
        name="cut",
    )(place, voltages, *earlier)


def weighted(taps, window, count, lanes, part, rows, sums):
    tap_count = taps.shape[0]
    tap_rows = [taps[k, :, lanes][None] for k in range(tap_count)]
    for j, ref, index in window:
        value = ref[index, part, rows, lanes].astype(F32).reshape(SB // 8, 8, LANES)
        for f in range(count):
            k = f - j
            if 0 <= k < tap_count:
                term = tap_rows[k] * value
                sums[f] = term if sums[f] is None else sums[f] + term
    return sums


def over_tiles(stations, samples, step):
    tiles, lane_tiles = stations // SB, samples // LANES

    def body(i, carry):
        lanes = pl.ds(pl.multiple_of(i % lane_tiles * LANES, LANES), LANES)
        rows = pl.ds(pl.multiple_of(i // (2 * lane_tiles) * SB, SB), SB)
        step(lanes, i // lane_tiles % 2, rows)
        return carry

    lax.fori_loop(0, 2 * tiles * lane_tiles, body, 0, unroll=2)


def near_kernel(place, taps, own, other, own_back, other_back, *rest):
    partial = rest[-1]
    frames = own.shape[0]
    count = 2 * frames

    def run(first, second, first_back, second_back):
        window = []
        for start, ref in ((-count, first_back), (frames - count, second_back), (0, first), (frames, second)):
            window += [(start + i, ref, i) for i in range(frames)]

        def step(lanes, part, rows):
            sums = weighted(taps, window, count, lanes, part, rows, [None] * count)
            for f in range(count):
                partial[f, part, rows, lanes] = sums[f].reshape(SB, LANES)

        over_tiles(*own.shape[2:], step)

    @pl.when(place[0] == 0)
    def _():
        run(own, other, own_back, other_back)

    @pl.when(place[0] == 1)
    def _():
        run(other, own, other_back, own_back)


def far_kernel(place, taps, partial, straight, mixed, *rest):
    keep, send = rest[-2:]
    frames = keep.shape[0]
    count = 2 * frames
    first = 1 - 2 * count

    def run(early, late, early_low, late_low, first_out, second_out):
        window = [(first + i, early, early_low + i) for i in range(frames - 1)]
        window += [(first + frames - 1, mixed, 0)]
        window += [(first + frames + i, late, late_low + i) for i in range(frames - 1)]

        def step(lanes, part, rows):
            sums = [partial[f, part, rows, lanes].reshape(SB // 8, 8, LANES) for f in range(count)]
            sums = weighted(taps, window, count, lanes, part, rows, sums)
            for f in range(count):
                out = first_out if f < frames else second_out
                out[f % frames, part, rows, lanes] = sums[f].reshape(SB, LANES).astype(BF16)

        over_tiles(*keep.shape[2:], step)

    @pl.when(place[0] == 0)
    def _():
        run(straight, mixed, 0, 1, keep, send)

    @pl.when(place[0] == 1)
    def _():
        run(mixed, straight, 1, 0, send, keep)


def near_filter(place, taps, own, other, own_back, other_back, pol, earlier):
    frames, parts, stations, samples = other.shape
    block = 512
    both = pl.BlockSpec((None, frames, parts, stations, block), lambda i, place: (pol, 0, 0, 0, i))
    one = pl.BlockSpec((frames, parts, stations, block), lambda i, place: (0, 0, 0, i))
    return pl.pallas_call(
        near_kernel,
        out_shape=jax.ShapeDtypeStruct((2 * frames, parts, stations, samples), F32),
        grid_spec=pltpu.PrefetchScalarGridSpec(
            num_scalar_prefetch=1,
            grid=(samples // block,),
            in_specs=[pl.BlockSpec((taps.shape[0], 8, block), lambda i, place: (0, 0, i)), both, one, both, one]
            + [pl.BlockSpec(memory_space=pl.ANY)] * len(earlier),
            out_specs=pl.BlockSpec((2 * frames, parts, stations, block), lambda i, place: (0, 0, 0, i)),
        ),
        compiler_params=pltpu.CompilerParams(vmem_limit_bytes=VMEM_LIMIT),
        cost_estimate=cost(8 * stations / 32),
        name="near",
    )(place, taps, own, other, own_back, other_back, *earlier)


def far_filter(place, taps, partial, straight, mixed, low, earlier):
    count, parts, _, samples = partial.shape
    frames, _, stations, _ = mixed.shape
    block = samples // 2

    def spec(depth, where):
        return pl.BlockSpec((depth, parts, stations, block), lambda i, place: (0, 0, where, i))

    shape = jax.ShapeDtypeStruct((frames, parts, stations, samples), BF16)
    return pl.pallas_call(
        far_kernel,
        out_shape=(shape, shape),
        grid_spec=pltpu.PrefetchScalarGridSpec(
            num_scalar_prefetch=1,
            grid=(samples // block,),
            in_specs=[
                pl.BlockSpec((taps.shape[0], 8, block), lambda i, place: (0, 0, i)),
                spec(count, low // stations),
                spec(frames - 1, low // stations),
                spec(frames, 0),
            ]
            + [pl.BlockSpec(memory_space=pl.ANY)] * len(earlier),
            out_specs=[spec(frames, 0)] * 2,
        ),
        compiler_params=pltpu.CompilerParams(vmem_limit_bytes=VMEM_LIMIT),
        cost_estimate=cost(3),
        name="far",
    )(place, taps, partial, straight, mixed, *earlier)


def onward_kernel(place, own_back, other_back, *rest):
    out = rest[-1]

    @pl.when(place[0] == 0)
    def _():
        out[:1] = other_back[:1]

    @pl.when(place[0] == 1)
    def _():
        out[:1] = own_back[...]

    out[1:] = other_back[1:]


def onward(place, own_back, other_back, pol, low, stations, earlier=()):
    frames, parts, _, samples = other_back.shape
    where = low // stations
    shape = (frames, parts, stations, samples)
    return pl.pallas_call(
        onward_kernel,
        out_shape=jax.ShapeDtypeStruct(shape, BF16),
        grid_spec=pltpu.PrefetchScalarGridSpec(
            num_scalar_prefetch=1,
            grid=(parts,),
            in_specs=[
                pl.BlockSpec((None, 1, 1, stations, samples), lambda i, place: (pol, 0, i, where, 0)),
                pl.BlockSpec((frames, 1, stations, samples), lambda i, place: (0, i, where, 0)),
            ]
            + [pl.BlockSpec(memory_space=pl.ANY)] * len(earlier),
            out_specs=pl.BlockSpec((frames, 1, stations, samples), lambda i, place: (0, i, 0, 0)),
        ),
        compiler_params=pltpu.CompilerParams(vmem_limit_bytes=VMEM_LIMIT),
        cost_estimate=cost(3 * stations / 32),
        name="onward",
    )(place, own_back, other_back, *earlier)


def weight_kernel(table, index, mask, *rest):
    out = rest[-1]
    groups, depth, width = out.shape
    beams = width // 2
    half = depth // 2
    rows = lax.broadcasted_iota(jnp.int32, (table.shape[0], beams), 0)
    for q in range(index.shape[0]):
        hit = jnp.where((rows == index[q : q + 1, :]) & (mask[q : q + 1, :] != 0), 1.0, 0.0).astype(BF16)
        picked = lax.dot_general(table[...], hit, (((0,), (0,)), ((), ())), preferred_element_type=F32)
        picked = picked.reshape(groups, 2, SB, beams)
        low = q % 2 * (half // 2) + q // 2 * SB
        re, im = picked[:, 0], picked[:, 1]
        out[:, low : low + SB, :beams] = re.astype(BF16)
        out[:, low : low + SB, beams:] = im.astype(BF16)
        low += half
        out[:, low : low + SB, :beams] = (-im).astype(BF16)
        out[:, low : low + SB, beams:] = re.astype(BF16)


def beam_weights(table, index, mask, earlier):
    blocks, beams = index.shape
    groups = table.shape[1] // (2 * SB)
    shape = (groups, 2 * blocks * SB, 2 * beams)
    return pl.pallas_call(
        weight_kernel,
        out_shape=jax.ShapeDtypeStruct(shape, BF16),
        in_specs=[pl.BlockSpec(memory_space=pltpu.VMEM)] * 3 + [pl.BlockSpec(memory_space=pl.ANY)] * len(earlier),
        compiler_params=pltpu.CompilerParams(vmem_limit_bytes=VMEM_LIMIT),
        cost_estimate=cost(4),
        name="weights",
    )(table, index, mask, *earlier)


def radix(source, mixed, low):
    tiles = source.shape[2] // SB

    def step(i, carry):
        f, tile = i // tiles, i % tiles
        rows = pl.ds(pl.multiple_of(tile * SB, SB), SB)
        values = [
            tuple(source[f, part, rows, a * LANES : (a + 1) * LANES].astype(F32) for part in range(2))
            for a in range(RADIX)
        ]
        target = pl.ds(pl.multiple_of(low + tile * SB, SB), SB)
        for b, (re, im) in enumerate(sixteen_points(values)):
            mixed[b, f, target, :LANES] = re.astype(BF16)
            mixed[b, f, target, LANES:] = im.astype(BF16)
        return carry

    lax.fori_loop(0, source.shape[0] * tiles, step, 0)


def radix_kernel(place, *refs):
    *sources, mixed = refs
    low = 0
    for ref in sources:
        radix(ref, mixed, low)
        low += ref.shape[2]


def radix_stage(place, sources):
    frames, parts, _, samples = sources[0].shape
    stations = sum(s.shape[2] for s in sources)
    return pl.pallas_call(
        radix_kernel,
        out_shape=jax.ShapeDtypeStruct((RADIX, frames, stations, 2 * LANES), BF16),
        grid_spec=pltpu.PrefetchScalarGridSpec(
            num_scalar_prefetch=1,
            grid=(frames,),
            in_specs=[pl.BlockSpec((1, parts, s.shape[2], samples), lambda i, place: (i, 0, 0, 0)) for s in sources],
            out_specs=pl.BlockSpec((RADIX, 1, stations, 2 * LANES), lambda i, place: (0, i, 0, 0)),
        ),
        compiler_params=pltpu.CompilerParams(vmem_limit_bytes=VMEM_LIMIT),
        cost_estimate=cost(3),
        name="radix",
    )(place, *sources)


def beam_kernel(source_count, has_earlier, place, first, *refs):
    refs = list(refs)
    sources = [refs.pop(0) for _ in range(source_count)]
    table, weights = refs.pop(0), refs.pop(0)
    earlier = refs.pop(0) if has_earlier else None
    out, mixed, spectra, sems, *refs = refs
    held, refs = refs[:source_count], refs[source_count:]
    step = pl.program_id(0)
    frames = sources[0].shape[0]
    station_count = mixed.shape[2]
    groups = spectra.shape[0]
    beams = weights.shape[2] // 2
    rows_of = table.shape[2] // 2 // groups
    pair = 2
    lane_tiles = beams // LANES
    per_channel = lane_tiles * frames

    @pl.when(step == 0)
    def _():
        copies = [pltpu.make_async_copy(ref, to, sems.at[k]) for k, (ref, to) in enumerate(zip(sources, held))]
        copies.append(pltpu.make_async_copy(first, mixed.at[:, :, : first.shape[2]], sems.at[source_count]))
        for copy in copies:
            copy.start()
        low = first.shape[2]
        for copy, ref in zip(copies, held):
            copy.wait()
            radix(ref, mixed, low)
            low += ref.shape[2]
        copies[-1].wait()

        def transform(b, carry):
            for start in range(0, frames, pair):
                product = lax.dot_general(
                    table[0, b],
                    mixed[b, start : start + pair].reshape(pair * station_count, 2 * LANES),
                    (((1,), (1,)), ((), ())),
                    preferred_element_type=F32,
                )
                product = product.reshape(2, groups, rows_of, pair * station_count)
                rows = slice(start * rows_of, (start + pair) * rows_of)
                for part in range(2):
                    value = jnp.concatenate(
                        [product[part, :, :, f * station_count : (f + 1) * station_count] for f in range(pair)], axis=1
                    )
                    columns = slice(part * station_count, (part + 1) * station_count)
                    spectra[:, b, rows, columns] = value.astype(BF16)
            return carry

        lax.fori_loop(0, RADIX, transform, 0, unroll=4)

    for k in range(weights.shape[0]):
        rows = spectra[step * weights.shape[0] + k].reshape(RADIX * frames * rows_of, 2 * station_count)
        beam = jnp.dot(rows, weights[k], preferred_element_type=F32)
        re, im = beam[:, :beams], beam[:, beams:]
        power = re * re + im * im
        if not has_earlier:
            out[k] = power
            continue
        power = power + earlier[k]
        for b in range(RADIX):
            for f in range(frames):
                at = (b * frames + f) * rows_of
                for t in range(lane_tiles):
                    start = (k * rows_of * RADIX + b) * per_channel + t * frames + f
                    refs[0][pl.ds(start, rows_of, stride=RADIX * per_channel), :] = power[
                        at : at + rows_of, t * LANES : (t + 1) * LANES
                    ]

    if has_earlier:

        def finish(c, carry):
            value = refs[0][pl.ds(pl.multiple_of(c * per_channel, per_channel), per_channel), :]
            for t in range(lane_tiles):
                out[c, :, t * LANES : (t + 1) * LANES] = value[t * frames : (t + 1) * frames]
            return carry

        lax.fori_loop(0, out.shape[0], finish, 0, unroll=8)


def beam_power(place, first, sources, table, weights, earlier, channels):
    frames, _, _, samples = sources[0].shape
    groups, depth, width = weights.shape
    beams = width // 2
    station_count = first.shape[2] + sum(s.shape[2] for s in sources)
    at_once = 2
    flat = (groups, channels // groups * frames, beams)
    flat_spec = pl.BlockSpec((at_once,) + flat[1:], lambda i, place: (i, 0, 0))
    in_specs = [pl.BlockSpec(memory_space=pltpu.HBM) for s in (first, *sources)]
    in_specs += [
        pl.BlockSpec((1,) + table.shape[1:], lambda i, place: (place[1], 0, 0, 0)),
        pl.BlockSpec((at_once, depth, width), lambda i, place: (i, 0, 0)),
    ]
    operands = [first] + list(sources) + [table, weights]
    scratch = [
        pltpu.VMEM((RADIX, frames, station_count, 2 * LANES), BF16),
        pltpu.VMEM((groups, RADIX, frames * channels // groups // RADIX, 2 * station_count), BF16),
        pltpu.SemaphoreType.DMA((len(sources) + 1,)),
    ]
    scratch += [pltpu.VMEM(s.shape, BF16) for s in sources]
    if earlier is None:
        out_shape = jax.ShapeDtypeStruct(flat, F32)
        out_spec = flat_spec
    else:
        out_shape = jax.ShapeDtypeStruct((channels, frames, beams), F32)
        out_spec = pl.BlockSpec((channels // groups * at_once, frames, beams), lambda i, place: (i, 0, 0))
        operands.append(earlier)
        in_specs.append(flat_spec)
        scratch.append(pltpu.VMEM((math.prod(out_spec.block_shape) // LANES, LANES), F32))
    return pl.pallas_call(
        functools.partial(beam_kernel, len(sources), earlier is not None),
        out_shape=out_shape,
        grid_spec=pltpu.PrefetchScalarGridSpec(
            num_scalar_prefetch=1,
            grid=(groups // at_once,),
            in_specs=in_specs,
            out_specs=out_spec,
            scratch_shapes=scratch,
        ),
        compiler_params=pltpu.CompilerParams(vmem_limit_bytes=VMEM_LIMIT),
        cost_estimate=cost(0),
        name="beams",
    )(place, *operands)


def flipped(rows, bit):
    return jnp.where(bit == 1, rows[::-1], rows)


def body(voltages, filter_taps, use_mask, block_index, weight_blocks):
    stations, pols, frames, parts, samples = voltages.shape
    history = filter_taps.shape[0] - 1
    half = stations // 2
    time_devices = lax.axis_size("tm")
    side = lax.axis_index("tm") % 2
    core = lax.axis_index("stn")
    place = jnp.stack([side, core]).astype(jnp.int32)

    def pair(block):
        return lax.ppermute(block, "tm", [(i, i ^ 1) for i in range(time_devices)])

    def hop(block, skip=0):
        return lax.ppermute(block, "tm", [(i, i + 2) for i in range(skip, time_devices - 2)])

    def swap(block):
        return lax.ppermute(block, "stn", [(0, 1), (1, 0)])

    def laid(block):
        return jnp.moveaxis(block, 0, -2)

    columns = weight_blocks.shape[1] // CORES
    shard = lax.dynamic_slice_in_dim(weight_blocks, core * columns, columns, 1)
    shards = [shard] + [
        lax.ppermute(shard, "tm", [(i, i ^ far) for i in range(time_devices)]) for far in range(2, time_devices, 2)
    ]
    own, *other = cut(place, voltages, [(pol, 0, half) for pol in range(pols)], shards[1:])
    own_back = laid(after(hop(own)))
    own = laid(own)
    other = [laid(after(pair(block))) for block in other]
    shards = jnp.concatenate(shards)
    shards = jnp.concatenate([shards, pair(shards)])

    def ordered(rows):
        rows = rows.T.reshape(2, 2, 2, -1)
        rows = flipped(rows, core)
        rows = flipped(rows.swapaxes(0, 1), side).swapaxes(0, 1)
        return rows.reshape(8, -1)

    each = weight_blocks.shape[0]
    apart = block_index // each ^ lax.axis_index("tm")
    index = (apart % 2 * (time_devices // 2) + apart // 2) * each + block_index % each
    weights = beam_weights(shards, ordered(index), ordered(use_mask), other)
    table = jnp.asarray(dft_tables(samples))
    taps = jnp.broadcast_to(filter_taps[:, None, :], (history + 1, 8, samples))

    quarter = half // 2
    chunks = [(pol, low) for pol in range(pols) for low in (0, quarter)]
    other_back = [hop(other[0])]
    straight = [hop(own_back[0, 1:], 2)]
    further = [onward(place, own_back, other_back[0], 0, low, quarter) for low in (0, quarter)]
    other_back.append(hop(after(other[1], further[0])))
    straight.append(hop(after(own_back[1, 1:], further[0]), 2))
    further += [onward(place, own_back, other_back[1], 1, low, quarter) for low in (0, quarter)]
    partial = []
    for pol in range(pols):
        earlier = further[: 2 * pol + 2] + [weights]
        partial.append(near_filter(place, taps, own, other[pol], own_back, other_back[pol], pol, earlier))
    far = [hop(block, 2) for block in further]
    keeps, sents, sources, power = [], [], [], None
    for k, (pol, low) in enumerate(chunks):
        earlier = sents[-1:] + partial[k : k + 1] + ([power] if k == len(chunks) - 1 else [])
        keep, send = far_filter(place, taps, partial[pol], straight[pol], far[k], low, earlier)
        keeps.append(keep)
        sents.append(pair(send))
        sources.append([keep, sents[-1], swap(keep), swap(sents[-1])])
        if k == 2:
            radixed = radix_stage(place, sources[0])
            power = beam_power(place, radixed, sources[1], table, weights, None, samples // CORES)
    radixed = radix_stage(place, sources[2])
    return beam_power(place, radixed, sources[3], table, weights, power, samples // CORES)


def solution(mesh):
    in_specs = (
        P(("parts", "stn"), None, "tm", None, None),
        P(),
        P("parts", None),
        P("parts", None),
        P("tm", None),
    )
    out_specs = P("stn", "tm", "parts")
    return jax.shard_map(body, mesh=mesh, in_specs=in_specs, out_specs=out_specs, check_vma=False)
```

```python
import functools
import math

import jax
import jax.numpy as jnp
import ml_dtypes
import numpy as np
from jax import lax
from jax.experimental import pallas as pl
from jax.experimental.pallas import tpu as pltpu
from jax.sharding import PartitionSpec as P

SB = 16
G = 16
RADIX = 16
LANES = 128
CORES = 2
VMEM_LIMIT = 56 * 1024 * 1024
F32 = jnp.float32
BF16 = jnp.bfloat16


def cost(microseconds):
    return pl.CostEstimate(flops=0, bytes_accessed=int(microseconds * 3.3e6), transcendentals=0)


def dft_tables(channels):
    per_half = channels // RADIX // CORES
    b = np.arange(RADIX)[None, :, None, None]
    e = np.arange(LANES)[None, None, None, :]
    d = np.arange(CORES * per_half).reshape(CORES, 1, per_half, 1)
    angle = (e * (RADIX * d + b) % channels) * (2.0 * math.pi / channels)
    cosine, sine = np.cos(angle), np.sin(angle)
    real_rows = np.concatenate([cosine, sine], axis=3)
    imag_rows = np.concatenate([-sine, cosine], axis=3)
    table = np.concatenate([real_rows, imag_rows], axis=2) / math.sqrt(channels)
    return table.astype(ml_dtypes.bfloat16)


def turned(value, step, size):
    re, im = value
    step %= size
    if step == 0:
        return re, im
    if 4 * step == size:
        return im, -re
    if 2 * step == size:
        return -re, -im
    if 4 * step == 3 * size:
        return -im, re
    cosine, sine = math.cos(2 * math.pi * step / size), math.sin(2 * math.pi * step / size)
    if 8 * step == size:
        return (re + im) * cosine, (im - re) * cosine
    if 8 * step == 3 * size:
        return (im - re) * sine, -(re + im) * sine
    return re * cosine + im * sine, im * cosine - re * sine


def four_points(values):
    (r0, i0), (r1, i1), (r2, i2), (r3, i3) = values
    sr, si, dr, di = r0 + r2, i0 + i2, r0 - r2, i0 - i2
    tr, ti, er, ei = r1 + r3, i1 + i3, r1 - r3, i1 - i3
    return [(sr + tr, si + ti), (dr + ei, di - er), (sr - tr, si - ti), (dr - ei, di + er)]


def sixteen_points(values):
    inner = [four_points([values[4 * a1 + a0] for a1 in range(4)]) for a0 in range(4)]
    result = [None] * 16
    for b0 in range(4):
        outer = four_points([turned(inner[a0][b0], a0 * b0, 16) for a0 in range(4)])
        for b1 in range(4):
            result[4 * b1 + b0] = outer[b1]
    return result


def after(block, *earlier):
    return pl.pallas_call(
        lambda *refs: None,
        out_shape=jax.ShapeDtypeStruct(block.shape, block.dtype),
        in_specs=[pl.BlockSpec(memory_space=pl.ANY)] * (1 + len(earlier)),
        out_specs=pl.BlockSpec(memory_space=pl.ANY),
        input_output_aliases={0: 0},
        cost_estimate=cost(0),
        name="after",
    )(block, *earlier)


def cut_kernel(cuts, place, voltages, *rest):
    (own, *outs), (buffer, loads, stores) = rest[-4 - len(cuts) : -3], rest[-3:]
    half = own.shape[0]
    pieces = loads.shape[1]
    size = half // pieces
    side = place[0]

    def load(h, k):
        start = jnp.where(side == h, 0, half) + k * size
        return pltpu.make_async_copy(
            voltages.at[pl.ds(start, size)], buffer.at[h, pl.ds(k * size, size)], loads.at[h, k]
        )

    def store(h, k):
        copies = []
        if h == 0:
            copies.append(pltpu.make_async_copy(buffer.at[0, pl.ds(k * size, size)], own.at[pl.ds(k * size, size)], stores.at[0, k]))
        else:
            for pol in range(voltages.shape[1]):
                for out, (which, low, count) in zip(outs, cuts):
                    if which == pol and low <= k * size < low + count:
                        copies.append(
                            pltpu.make_async_copy(
                                buffer.at[1, pl.ds(k * size, size), pol],
                                out.at[pl.ds(k * size - low, size)],
                                stores.at[1 + pol, k],
                            )
                        )
        return copies

    order = [(h, k) for h in range(2) for k in range(pieces)]
    for h, k in order:
        load(h, k).start()
    for h, k in order:
        load(h, k).wait()
        for copy in store(h, k):
            copy.start()
    for h, k in order:
        for copy in store(h, k):
            copy.wait()


def cut(place, voltages, cuts, earlier):
    stations, pols, frames, parts, samples = voltages.shape
    half = stations // 2
    pieces = 4
    shapes = [(half, pols, frames, parts, samples)] + [(size, frames, parts, samples) for _, _, size in cuts]
    anywhere = pl.BlockSpec(memory_space=pltpu.HBM)
    return pl.pallas_call(
        functools.partial(cut_kernel, cuts),
        out_shape=[jax.ShapeDtypeStruct(shape, BF16) for shape in shapes],
        in_specs=[pl.BlockSpec(memory_space=pltpu.SMEM), anywhere] + [pl.BlockSpec(memory_space=pl.ANY)] * len(earlier),
        out_specs=[anywhere] * len(shapes),
        scratch_shapes=[
            pltpu.VMEM((2,) + shapes[0], BF16),
            pltpu.SemaphoreType.DMA((2, pieces)),
            pltpu.SemaphoreType.DMA((1 + pols, pieces)),
        ],
        compiler_params=pltpu.CompilerParams(vmem_limit_bytes=VMEM_LIMIT),
        cost_estimate=cost(4),
        name="cut",
    )(place, voltages, *earlier)


def weighted(taps, window, count, lanes, part, rows, sums):
    tap_count = taps.shape[0]
    tap_rows = [taps[k, :, lanes][None] for k in range(tap_count)]
    for j, ref, index in window:
        value = ref[index, part, rows, lanes].astype(F32).reshape(SB // 8, 8, LANES)
        for f in range(count):
            k = f - j
            if 0 <= k < tap_count:
                term = tap_rows[k] * value
                sums[f] = term if sums[f] is None else sums[f] + term
    return sums


def over_tiles(stations, samples, step):
    tiles, lane_tiles = stations // SB, samples // LANES

    def body(i, carry):
        lanes = pl.ds(pl.multiple_of(i % lane_tiles * LANES, LANES), LANES)
        rows = pl.ds(pl.multiple_of(i // (2 * lane_tiles) * SB, SB), SB)
        step(lanes, i // lane_tiles % 2, rows)
        return carry

    lax.fori_loop(0, 2 * tiles * lane_tiles, body, 0, unroll=2)


def near_kernel(place, taps, own, other, own_back, other_back, *rest):
    partial = rest[-1]
    frames = own.shape[0]
    count = 2 * frames

    def run(first, second, first_back, second_back):
        window = []
        for start, ref in ((-count, first_back), (frames - count, second_back), (0, first), (frames, second)):
            window += [(start + i, ref, i) for i in range(frames)]

        def step(lanes, part, rows):
            sums = weighted(taps, window, count, lanes, part, rows, [None] * count)
            for f in range(count):
                partial[f, part, rows, lanes] = sums[f].reshape(SB, LANES)

        over_tiles(*own.shape[2:], step)

    @pl.when(place[0] == 0)
    def _():
        run(own, other, own_back, other_back)

    @pl.when(place[0] == 1)
    def _():
        run(other, own, other_back, own_back)


def far_kernel(place, taps, partial, far, *rest):
    keep, send = rest[-2:]
    frames = keep.shape[0]
    count = 2 * frames
    window = [(i + 1 - 2 * count, far, i) for i in range(far.shape[0])]

    def run(first_out, second_out):
        def step(lanes, part, rows):
            sums = [partial[f, part, rows, lanes].reshape(SB // 8, 8, LANES) for f in range(count)]
            sums = weighted(taps, window, count, lanes, part, rows, sums)
            for f in range(count):
                out = first_out if f < frames else second_out
                out[f % frames, part, rows, lanes] = sums[f].reshape(SB, LANES).astype(BF16)

        over_tiles(*keep.shape[2:], step)

    @pl.when(place[0] == 0)
    def _():
        run(keep, send)

    @pl.when(place[0] == 1)
    def _():
        run(send, keep)


def near_filter(place, taps, own, other, own_back, other_back, pol, earlier):
    frames, parts, stations, samples = other.shape
    block = 512
    both = pl.BlockSpec((None, frames, parts, stations, block), lambda i, place: (pol, 0, 0, 0, i))
    one = pl.BlockSpec((frames, parts, stations, block), lambda i, place: (0, 0, 0, i))
    return pl.pallas_call(
        near_kernel,
        out_shape=jax.ShapeDtypeStruct((2 * frames, parts, stations, samples), F32),
        grid_spec=pltpu.PrefetchScalarGridSpec(
            num_scalar_prefetch=1,
            grid=(samples // block,),
            in_specs=[pl.BlockSpec((taps.shape[0], 8, block), lambda i, place: (0, 0, i)), both, one, both, one]
            + [pl.BlockSpec(memory_space=pl.ANY)] * len(earlier),
            out_specs=pl.BlockSpec((2 * frames, parts, stations, block), lambda i, place: (0, 0, 0, i)),
        ),
        compiler_params=pltpu.CompilerParams(vmem_limit_bytes=VMEM_LIMIT),
        cost_estimate=cost(8 * stations / 32),
        name="near",
    )(place, taps, own, other, own_back, other_back, *earlier)


def far_filter(place, taps, partial, far, low, size, earlier):
    count, parts, stations, _ = partial.shape
    frames = count // 2
    block = math.gcd(512, low, size)

    def spec(depth, start):
        return pl.BlockSpec((depth, parts, stations, block), lambda i, place: (0, 0, 0, start // block + i))

    shape = jax.ShapeDtypeStruct((frames, parts, stations, size), BF16)
    return pl.pallas_call(
        far_kernel,
        out_shape=(shape, shape),
        grid_spec=pltpu.PrefetchScalarGridSpec(
            num_scalar_prefetch=1,
            grid=(size // block,),
            in_specs=[pl.BlockSpec((taps.shape[0], 8, block), lambda i, place: (0, 0, low // block + i))]
            + [spec(count, low), spec(far.shape[0], 0)]
            + [pl.BlockSpec(memory_space=pl.ANY)] * len(earlier),
            out_specs=[spec(frames, 0)] * 2,
        ),
        compiler_params=pltpu.CompilerParams(vmem_limit_bytes=VMEM_LIMIT),
        cost_estimate=cost(1),
        name="far",
    )(place, taps, partial, far, *earlier)


def onward_kernel(place, own_back, other_back, far):
    frames = own_back.shape[0]

    def run(first, second):
        far[: frames - 1] = first[1:]
        far[frames - 1 :] = second[...]

    @pl.when(place[0] == 0)
    def _():
        run(own_back, other_back)

    @pl.when(place[0] == 1)
    def _():
        run(other_back, own_back)


def onward(place, own_back, other_back, pol, low, size):
    frames, parts, stations, _ = other_back.shape
    depth = 2 * frames - 1
    block = math.gcd(low, size)
    where = low // block
    return pl.pallas_call(
        onward_kernel,
        out_shape=jax.ShapeDtypeStruct((depth, parts, stations, size), BF16),
        grid_spec=pltpu.PrefetchScalarGridSpec(
            num_scalar_prefetch=1,
            grid=(parts, size // block),
            in_specs=[
                pl.BlockSpec((None, frames, 1, stations, block), lambda i, j, place: (pol, 0, i, 0, where + j)),
                pl.BlockSpec((frames, 1, stations, block), lambda i, j, place: (0, i, 0, where + j)),
            ],
            out_specs=pl.BlockSpec((depth, 1, stations, block), lambda i, j, place: (0, i, 0, j)),
        ),
        compiler_params=pltpu.CompilerParams(vmem_limit_bytes=VMEM_LIMIT),
        cost_estimate=cost(3),
        name="onward",
    )(place, own_back, other_back)


def weight_kernel(table, index, mask, *rest):
    out = rest[-1]
    groups, depth, width = out.shape
    beams = width // 2
    half = depth // 2
    rows = lax.broadcasted_iota(jnp.int32, (table.shape[0], beams), 0)
    for q in range(index.shape[0]):
        hit = jnp.where((rows == index[q : q + 1, :]) & (mask[q : q + 1, :] != 0), 1.0, 0.0).astype(BF16)
        picked = lax.dot_general(table[...], hit, (((0,), (0,)), ((), ())), preferred_element_type=F32)
        picked = picked.reshape(groups, 2, SB, beams)
        low = q * SB
        re, im = picked[:, 0], picked[:, 1]
        out[:, low : low + SB, :beams] = re.astype(BF16)
        out[:, low : low + SB, beams:] = im.astype(BF16)
        low += half
        out[:, low : low + SB, :beams] = (-im).astype(BF16)
        out[:, low : low + SB, beams:] = re.astype(BF16)


def beam_weights(table, index, mask, earlier):
    blocks, beams = index.shape
    groups = table.shape[1] // (2 * SB)
    shape = (groups, 2 * blocks * SB, 2 * beams)
    return pl.pallas_call(
        weight_kernel,
        out_shape=jax.ShapeDtypeStruct(shape, BF16),
        in_specs=[pl.BlockSpec(memory_space=pltpu.VMEM)] * 3 + [pl.BlockSpec(memory_space=pl.ANY)] * len(earlier),
        compiler_params=pltpu.CompilerParams(vmem_limit_bytes=VMEM_LIMIT),
        cost_estimate=cost(4),
        name="weights",
    )(table, index, mask, *earlier)


def beam_kernel(source_count, ranges, later_count, has_earlier, *refs):
    refs = list(refs)
    refs.pop(0)
    sources = [refs.pop(0) for _ in range(source_count)]
    table, weights = refs.pop(0), refs.pop(0)
    earlier = refs.pop(0) if has_earlier else None
    refs = refs[later_count:]
    out, mixed, spectra, sems, *refs = refs
    held, refs = refs[:source_count], refs[source_count:]
    step = pl.program_id(0)
    frames = sources[0].shape[0]
    stations = sources[0].shape[2]
    tiles = stations // SB
    station_count = stations * (source_count // ranges)
    groups = spectra.shape[0]
    beams = weights.shape[2] // 2
    rows_of = table.shape[2] // 2 // groups
    pair = 2
    lane_tiles = beams // LANES
    per_channel = lane_tiles * frames

    @pl.when(step == 0)
    def _():
        copies = [pltpu.make_async_copy(ref, to, sems.at[k]) for k, (ref, to) in enumerate(zip(sources, held))]
        for copy in copies:
            copy.start()
        for k in range(0, source_count, ranges):
            for copy in copies[k : k + ranges]:
                copy.wait()
            pieces = []
            for ref in held[k : k + ranges]:
                pieces += [(ref, slice(n, n + LANES)) for n in range(0, ref.shape[3], LANES)]

            def radix(i, carry, pieces=pieces, low=k // ranges * stations):
                f, rows = i // tiles, pl.ds(pl.multiple_of(i % tiles * SB, SB), SB)
                values = [tuple(ref[f, part, rows, lanes].astype(F32) for part in range(2)) for ref, lanes in pieces]
                target = pl.ds(pl.multiple_of(f * station_count + low + i % tiles * SB, SB), SB)
                for b, (re, im) in enumerate(sixteen_points(values)):
                    mixed[b, target, :LANES] = re.astype(BF16)
                    mixed[b, target, LANES:] = im.astype(BF16)
                return carry

            lax.fori_loop(0, frames * tiles, radix, 0)

        def transform(b, carry):
            for start in range(0, frames, pair):
                product = lax.dot_general(
                    table[0, b],
                    mixed[b, start * station_count : (start + pair) * station_count],
                    (((1,), (1,)), ((), ())),
                    preferred_element_type=F32,
                )
                product = product.reshape(2, groups, rows_of, pair * station_count)
                rows = slice(start * rows_of, (start + pair) * rows_of)
                for part in range(2):
                    value = jnp.concatenate(
                        [product[part, :, :, f * station_count : (f + 1) * station_count] for f in range(pair)], axis=1
                    )
                    columns = slice(part * station_count, (part + 1) * station_count)
                    spectra[:, b, rows, columns] = value.astype(BF16)
            return carry

        lax.fori_loop(0, RADIX, transform, 0, unroll=4)

    for k in range(weights.shape[0]):
        rows = spectra[step * weights.shape[0] + k].reshape(RADIX * frames * rows_of, 2 * station_count)
        beam = jnp.dot(rows, weights[k], preferred_element_type=F32)
        re, im = beam[:, :beams], beam[:, beams:]
        power = re * re + im * im
        if not has_earlier:
            out[k] = power
            continue
        power = power + earlier[k]
        for b in range(RADIX):
            for f in range(frames):
                at = (b * frames + f) * rows_of
                for t in range(lane_tiles):
                    start = (k * rows_of * RADIX + b) * per_channel + t * frames + f
                    refs[0][pl.ds(start, rows_of, stride=RADIX * per_channel), :] = power[
                        at : at + rows_of, t * LANES : (t + 1) * LANES
                    ]

    if has_earlier:

        def finish(c, carry):
            value = refs[0][pl.ds(pl.multiple_of(c * per_channel, per_channel), per_channel), :]
            for t in range(lane_tiles):
                out[c, :, t * LANES : (t + 1) * LANES] = value[t * frames : (t + 1) * frames]
            return carry

        lax.fori_loop(0, out.shape[0], finish, 0, unroll=8)


def beam_power(place, sources, ranges, table, weights, earlier, channels, later=()):
    frames = sources[0].shape[0]
    groups, depth, width = weights.shape
    beams = width // 2
    station_count = sum(s.shape[2] for s in sources) // ranges
    at_once = 2
    flat = (groups, channels // groups * frames, beams)
    flat_spec = pl.BlockSpec((at_once,) + flat[1:], lambda i, place: (i, 0, 0))
    in_specs = [pl.BlockSpec(memory_space=pltpu.HBM) for s in sources]
    in_specs += [
        pl.BlockSpec((1,) + table.shape[1:], lambda i, place: (place[1], 0, 0, 0)),
        pl.BlockSpec((at_once, depth, width), lambda i, place: (i, 0, 0)),
    ]
    operands = list(sources) + [table, weights]
    free = [pl.BlockSpec(memory_space=pl.ANY)] * len(later)
    scratch = [
        pltpu.VMEM((RADIX, frames * station_count, 2 * LANES), BF16),
        pltpu.VMEM((groups, RADIX, frames * channels // groups // RADIX, 2 * station_count), BF16),
        pltpu.SemaphoreType.DMA((len(sources),)),
    ]
    scratch += [pltpu.VMEM(s.shape, BF16) for s in sources]
    if earlier is None:
        out_shape = jax.ShapeDtypeStruct(flat, F32)
        out_spec = flat_spec
    else:
        out_shape = jax.ShapeDtypeStruct((channels, frames, beams), F32)
        out_spec = pl.BlockSpec((channels // groups * at_once, frames, beams), lambda i, place: (i, 0, 0))
        operands.append(earlier)
        in_specs.append(flat_spec)
        scratch.append(pltpu.VMEM((math.prod(out_spec.block_shape) // LANES, LANES), F32))
    return pl.pallas_call(
        functools.partial(beam_kernel, len(sources), ranges, len(later), earlier is not None),
        out_shape=out_shape,
        grid_spec=pltpu.PrefetchScalarGridSpec(
            num_scalar_prefetch=1,
            grid=(groups // at_once,),
            in_specs=in_specs + free,
            out_specs=out_spec,
            scratch_shapes=scratch,
        ),
        compiler_params=pltpu.CompilerParams(vmem_limit_bytes=VMEM_LIMIT),
        cost_estimate=cost(0),
        name="beams",
    )(place, *operands, *later)


def flipped(rows, bit):
    return jnp.where(bit == 1, rows[::-1], rows)


def body(voltages, filter_taps, use_mask, block_index, weight_blocks):
    stations, pols, frames, parts, samples = voltages.shape
    history = filter_taps.shape[0] - 1
    half = stations // 2
    time_devices = lax.axis_size("tm")
    side = lax.axis_index("tm") % 2
    core = lax.axis_index("stn")
    place = jnp.stack([side, core]).astype(jnp.int32)

    def pair(block):
        return lax.ppermute(block, "tm", [(i, i ^ 1) for i in range(time_devices)])

    def hop(block, skip=0):
        return lax.ppermute(block, "tm", [(i, i + 2) for i in range(skip, time_devices - 2)])

    def swap(block):
        return lax.ppermute(block, "stn", [(0, 1), (1, 0)])

    def laid(block):
        return jnp.moveaxis(block, 0, -2)

    columns = weight_blocks.shape[1] // CORES
    shard = lax.dynamic_slice_in_dim(weight_blocks, core * columns, columns, 1)
    shards = [shard] + [
        lax.ppermute(shard, "tm", [(i, i ^ far) for i in range(time_devices)]) for far in range(2, time_devices, 2)
    ]
    own, *other = cut(place, voltages, [(pol, 0, half) for pol in range(pols)], [])
    own = after(own, *shards[1:])
    own_back = laid(after(hop(own)))
    own = laid(own)
    other = [laid(after(pair(block))) for block in other]
    shards = jnp.concatenate(shards)
    shards = jnp.concatenate([shards, pair(shards)])

    def ordered(rows):
        rows = rows.T.reshape(2, 2, 2, -1)
        rows = flipped(rows, core)
        rows = flipped(rows.swapaxes(0, 1), side).swapaxes(0, 1)
        return rows.reshape(8, -1)

    each = weight_blocks.shape[0]
    apart = block_index // each ^ lax.axis_index("tm")
    index = (apart % 2 * (time_devices // 2) + apart // 2) * each + block_index % each
    weights = beam_weights(shards, ordered(index), ordered(use_mask), other)
    table = jnp.asarray(dft_tables(samples))
    taps = jnp.broadcast_to(filter_taps[:, None, :], (history + 1, 8, samples))

    chunks = [(pol, low, samples // 2) for pol in range(pols) for low in (0, samples // 2)]
    other_back = [hop(block) for block in other]
    further = [onward(place, own_back, other_back[pol], pol, low, size) for pol, low, size in chunks]
    far = [hop(block, 2) for block in further]
    keeps, sents, partial = [], [], []

    def power_of(pol, earlier, later=()):
        here = [k for k, chunk in enumerate(chunks) if chunk[0] == pol]
        mine, pairs = [keeps[k] for k in here], [sents[k] for k in here]
        sources = mine + pairs + [swap(block) for block in mine + pairs]
        return beam_power(place, sources, len(here), table, weights, earlier, samples // CORES, later)

    for k, (pol, low, size) in enumerate(chunks):
        if pol >= len(partial):
            gates = further + keeps[1:2] if pol else further[:2] + [weights]
            partial.append(near_filter(place, taps, own, other[pol], own_back, other_back[pol], pol, gates))
        keep, send = far_filter(place, taps, partial[pol], far[k], low, size, sents[-1:])
        keeps.append(keep)
        sents.append(pair(send))
    power = power_of(0, None, keeps[-1:])
    sents[-1] = after(sents[-1], power)
    return power_of(1, power)


def solution(mesh):
    in_specs = (
        P(("parts", "stn"), None, "tm", None, None),
        P(),
        P("parts", None),
        P("parts", None),
        P("tm", None),
    )
    out_specs = P("stn", "tm", "parts")
    return jax.shard_map(body, mesh=mesh, in_specs=in_specs, out_specs=out_specs, check_vma=False)
```

```python
import functools
import math

import jax
import jax.numpy as jnp
import ml_dtypes
import numpy as np
from jax import lax
from jax.experimental import pallas as pl
from jax.experimental.pallas import tpu as pltpu
from jax.sharding import PartitionSpec as P

SB = 16
G = 16
RADIX = 16
LANES = 128
CORES = 2
VMEM_LIMIT = 63 * 1024 * 1024
F32 = jnp.float32
BF16 = jnp.bfloat16


def cost(microseconds):
    return pl.CostEstimate(flops=0, bytes_accessed=int(microseconds * 3.3e6), transcendentals=0)


def dft_tables(channels):
    per_half = channels // RADIX // CORES
    b = np.arange(RADIX)[None, :, None, None]
    e = np.arange(LANES)[None, None, None, :]
    d = np.arange(CORES * per_half).reshape(CORES, 1, per_half, 1)
    angle = (e * (RADIX * d + b) % channels) * (2.0 * math.pi / channels)
    cosine, sine = np.cos(angle), np.sin(angle)
    real_rows = np.concatenate([cosine, sine], axis=3)
    imag_rows = np.concatenate([-sine, cosine], axis=3)
    table = np.concatenate([real_rows, imag_rows], axis=2) / math.sqrt(channels)
    return table.astype(ml_dtypes.bfloat16)


def turned(value, step, size):
    re, im = value
    step %= size
    if step == 0:
        return re, im
    if 4 * step == size:
        return im, -re
    if 2 * step == size:
        return -re, -im
    if 4 * step == 3 * size:
        return -im, re
    cosine, sine = math.cos(2 * math.pi * step / size), math.sin(2 * math.pi * step / size)
    if 8 * step == size:
        return (re + im) * cosine, (im - re) * cosine
    if 8 * step == 3 * size:
        return (im - re) * sine, -(re + im) * sine
    return re * cosine + im * sine, im * cosine - re * sine


def four_points(values):
    (r0, i0), (r1, i1), (r2, i2), (r3, i3) = values
    sr, si, dr, di = r0 + r2, i0 + i2, r0 - r2, i0 - i2
    tr, ti, er, ei = r1 + r3, i1 + i3, r1 - r3, i1 - i3
    return [(sr + tr, si + ti), (dr + ei, di - er), (sr - tr, si - ti), (dr - ei, di + er)]


def sixteen_points(values):
    inner = [four_points([values[4 * a1 + a0] for a1 in range(4)]) for a0 in range(4)]
    result = [None] * 16
    for b0 in range(4):
        outer = four_points([turned(inner[a0][b0], a0 * b0, 16) for a0 in range(4)])
        for b1 in range(4):
            result[4 * b1 + b0] = outer[b1]
    return result


def after(block, *earlier):
    return pl.pallas_call(
        lambda *refs: None,
        out_shape=jax.ShapeDtypeStruct(block.shape, block.dtype),
        in_specs=[pl.BlockSpec(memory_space=pl.ANY)] * (1 + len(earlier)),
        out_specs=pl.BlockSpec(memory_space=pl.ANY),
        input_output_aliases={0: 0},
        cost_estimate=cost(0),
        name="after",
    )(block, *earlier)


def cut_kernel(cuts, place, voltages, *rest):
    (own, *outs), (buffer, loads, stores) = rest[-4 - len(cuts) : -3], rest[-3:]
    half = own.shape[0]
    pieces = loads.shape[1]
    size = half // pieces
    side = place[0]

    def load(h, k):
        start = jnp.where(side == h, 0, half) + k * size
        return pltpu.make_async_copy(
            voltages.at[pl.ds(start, size)], buffer.at[h, pl.ds(k * size, size)], loads.at[h, k]
        )

    def store(h, k):
        copies = []
        if h == 0:
            copies.append(pltpu.make_async_copy(buffer.at[0, pl.ds(k * size, size)], own.at[pl.ds(k * size, size)], stores.at[0, k]))
        else:
            for pol in range(voltages.shape[1]):
                for out, (which, low, count) in zip(outs, cuts):
                    if which == pol and low <= k * size < low + count:
                        copies.append(
                            pltpu.make_async_copy(
                                buffer.at[1, pl.ds(k * size, size), pol],
                                out.at[pl.ds(k * size - low, size)],
                                stores.at[1 + pol, k],
                            )
                        )
        return copies

    order = [(h, k) for h in range(2) for k in range(pieces)]
    for h, k in order:
        load(h, k).start()
    for h, k in order:
        load(h, k).wait()
        for copy in store(h, k):
            copy.start()
    for h, k in order:
        for copy in store(h, k):
            copy.wait()


def cut(place, voltages, cuts, earlier):
    stations, pols, frames, parts, samples = voltages.shape
    half = stations // 2
    pieces = 4
    shapes = [(half, pols, frames, parts, samples)] + [(size, frames, parts, samples) for _, _, size in cuts]
    anywhere = pl.BlockSpec(memory_space=pltpu.HBM)
    return pl.pallas_call(
        functools.partial(cut_kernel, cuts),
        out_shape=[jax.ShapeDtypeStruct(shape, BF16) for shape in shapes],
        in_specs=[pl.BlockSpec(memory_space=pltpu.SMEM), anywhere] + [pl.BlockSpec(memory_space=pl.ANY)] * len(earlier),
        out_specs=[anywhere] * len(shapes),
        scratch_shapes=[
            pltpu.VMEM((2,) + shapes[0], BF16),
            pltpu.SemaphoreType.DMA((2, pieces)),
            pltpu.SemaphoreType.DMA((1 + pols, pieces)),
        ],
        compiler_params=pltpu.CompilerParams(vmem_limit_bytes=VMEM_LIMIT),
        cost_estimate=cost(4),
        name="cut",
    )(place, voltages, *earlier)


def weighted(taps, window, count, lanes, part, rows, sums):
    tap_count = taps.shape[0]
    tap_rows = [taps[k, :, lanes][None] for k in range(tap_count)]
    for j, ref, index in window:
        value = ref[index, part, rows, lanes].astype(F32).reshape(SB // 8, 8, LANES)
        for f in range(count):
            k = f - j
            if 0 <= k < tap_count:
                term = tap_rows[k] * value
                sums[f] = term if sums[f] is None else sums[f] + term
    return sums


def over_tiles(stations, samples, step):
    tiles, lane_tiles = stations // SB, samples // LANES

    def body(i, carry):
        lanes = pl.ds(pl.multiple_of(i % lane_tiles * LANES, LANES), LANES)
        rows = pl.ds(pl.multiple_of(i // (2 * lane_tiles) * SB, SB), SB)
        step(lanes, i // lane_tiles % 2, rows)
        return carry

    lax.fori_loop(0, 2 * tiles * lane_tiles, body, 0, unroll=2)


def near_kernel(place, taps, own, other, own_back, other_back, *rest):
    partial = rest[-1]
    frames = own.shape[0]
    count = 2 * frames

    def run(first, second, first_back, second_back):
        window = []
        for start, ref in ((-count, first_back), (frames - count, second_back), (0, first), (frames, second)):
            window += [(start + i, ref, i) for i in range(frames)]

        def step(lanes, part, rows):
            sums = weighted(taps, window, count, lanes, part, rows, [None] * count)
            for f in range(count):
                partial[f, part, rows, lanes] = sums[f].reshape(SB, LANES)

        over_tiles(*own.shape[2:], step)

    @pl.when(place[0] == 0)
    def _():
        run(own, other, own_back, other_back)

    @pl.when(place[0] == 1)
    def _():
        run(other, own, other_back, own_back)


def far_kernel(place, taps, partial, far, *rest):
    keep, send = rest[-2:]
    frames = keep.shape[0]
    count = 2 * frames
    window = [(i + 1 - 2 * count, far, i) for i in range(far.shape[0])]

    def run(first_out, second_out):
        def step(lanes, part, rows):
            sums = [partial[f, part, rows, lanes].reshape(SB // 8, 8, LANES) for f in range(count)]
            sums = weighted(taps, window, count, lanes, part, rows, sums)
            for f in range(count):
                out = first_out if f < frames else second_out
                out[f % frames, part, rows, lanes] = sums[f].reshape(SB, LANES).astype(BF16)

        over_tiles(*keep.shape[2:], step)

    @pl.when(place[0] == 0)
    def _():
        run(keep, send)

    @pl.when(place[0] == 1)
    def _():
        run(send, keep)


def near_filter(place, taps, own, other, own_back, other_back, pol, earlier):
    frames, parts, stations, samples = other.shape
    block = 512
    both = pl.BlockSpec((None, frames, parts, stations, block), lambda i, place: (pol, 0, 0, 0, i))
    one = pl.BlockSpec((frames, parts, stations, block), lambda i, place: (0, 0, 0, i))
    return pl.pallas_call(
        near_kernel,
        out_shape=jax.ShapeDtypeStruct((2 * frames, parts, stations, samples), F32),
        grid_spec=pltpu.PrefetchScalarGridSpec(
            num_scalar_prefetch=1,
            grid=(samples // block,),
            in_specs=[pl.BlockSpec((taps.shape[0], 8, block), lambda i, place: (0, 0, i)), both, one, both, one]
            + [pl.BlockSpec(memory_space=pl.ANY)] * len(earlier),
            out_specs=pl.BlockSpec((2 * frames, parts, stations, block), lambda i, place: (0, 0, 0, i)),
        ),
        compiler_params=pltpu.CompilerParams(vmem_limit_bytes=VMEM_LIMIT),
        cost_estimate=cost(8 * stations / 32),
        name="near",
    )(place, taps, own, other, own_back, other_back, *earlier)


def far_filter(place, taps, partial, far, low, size, earlier):
    count, parts, stations, _ = partial.shape
    frames = count // 2
    block = size // 2

    def spec(depth, start):
        shape = (pl.Element(depth), pl.Element(parts), pl.Element(stations), pl.Element(block))
        return pl.BlockSpec(shape, lambda i, place: (0, 0, 0, pl.multiple_of(start + i * block, LANES)))

    shape = jax.ShapeDtypeStruct((frames, parts, stations, size), BF16)
    return pl.pallas_call(
        far_kernel,
        out_shape=(shape, shape),
        grid_spec=pltpu.PrefetchScalarGridSpec(
            num_scalar_prefetch=1,
            grid=(size // block,),
            in_specs=[
                pl.BlockSpec(
                    (pl.Element(taps.shape[0]), pl.Element(8), pl.Element(block)),
                    lambda i, place: (0, 0, pl.multiple_of(low + i * block, LANES)),
                )
            ]
            + [spec(count, low), spec(far.shape[0], 0)]
            + [pl.BlockSpec(memory_space=pl.ANY)] * len(earlier),
            out_specs=[spec(frames, 0)] * 2,
        ),
        compiler_params=pltpu.CompilerParams(vmem_limit_bytes=VMEM_LIMIT),
        cost_estimate=cost(1),
        name="far",
    )(place, taps, partial, far, *earlier)


def onward_kernel(place, own_back, other_back, far):
    frames = other_back.shape[0]
    own_back = own_back.at[0]

    def run(first, second):
        far[: frames - 1] = first[1:]
        far[frames - 1 :] = second[...]

    @pl.when(place[0] == 0)
    def _():
        run(own_back, other_back)

    @pl.when(place[0] == 1)
    def _():
        run(other_back, own_back)


def onward(place, own_back, other_back, pol, low, size):
    frames, parts, stations, _ = other_back.shape
    depth = 2 * frames - 1

    def spec(depth, *before):
        shape = tuple(pl.Element(n) for n in (1,) * len(before) + (depth, 1, stations, size))
        return pl.BlockSpec(shape, lambda i, place: before + (0, i, 0, low))

    return pl.pallas_call(
        onward_kernel,
        out_shape=jax.ShapeDtypeStruct((depth, parts, stations, size), BF16),
        grid_spec=pltpu.PrefetchScalarGridSpec(
            num_scalar_prefetch=1,
            grid=(parts,),
            in_specs=[spec(frames, pol), spec(frames)],
            out_specs=pl.BlockSpec((depth, 1, stations, size), lambda i, place: (0, i, 0, 0)),
        ),
        compiler_params=pltpu.CompilerParams(vmem_limit_bytes=VMEM_LIMIT),
        cost_estimate=cost(3),
        name="onward",
    )(place, own_back, other_back)


def weight_kernel(table, index, mask, *rest):
    out = rest[-1]
    groups, depth, width = out.shape
    beams = width // 2
    half = depth // 2
    rows = lax.broadcasted_iota(jnp.int32, (table.shape[0], beams), 0)
    for q in range(index.shape[0]):
        hit = jnp.where((rows == index[q : q + 1, :]) & (mask[q : q + 1, :] != 0), 1.0, 0.0).astype(BF16)
        picked = lax.dot_general(table[...], hit, (((0,), (0,)), ((), ())), preferred_element_type=F32)
        picked = picked.reshape(groups, 2, SB, beams)
        low = q * SB
        re, im = picked[:, 0], picked[:, 1]
        out[:, low : low + SB, :beams] = re.astype(BF16)
        out[:, low : low + SB, beams:] = im.astype(BF16)
        low += half
        out[:, low : low + SB, :beams] = (-im).astype(BF16)
        out[:, low : low + SB, beams:] = re.astype(BF16)


def beam_weights(table, index, mask, earlier):
    blocks, beams = index.shape
    groups = table.shape[1] // (2 * SB)
    shape = (groups, 2 * blocks * SB, 2 * beams)
    return pl.pallas_call(
        weight_kernel,
        out_shape=jax.ShapeDtypeStruct(shape, BF16),
        in_specs=[pl.BlockSpec(memory_space=pltpu.VMEM)] * 3 + [pl.BlockSpec(memory_space=pl.ANY)] * len(earlier),
        compiler_params=pltpu.CompilerParams(vmem_limit_bytes=VMEM_LIMIT),
        cost_estimate=cost(4),
        name="weights",
    )(table, index, mask, *earlier)


def beam_kernel(source_count, ranges, later_count, has_earlier, *refs):
    refs = list(refs)
    refs.pop(0)
    sources = [refs.pop(0) for _ in range(source_count)]
    table, weights = refs.pop(0), refs.pop(0)
    earlier = refs.pop(0) if has_earlier else None
    refs = refs[later_count:]
    out, mixed, spectra, sems, *refs = refs
    held = refs
    step = pl.program_id(0)
    frames = sources[0].shape[0]
    stations = sources[0].shape[2]
    tiles = stations // SB
    station_count = stations * (source_count // ranges)
    groups = spectra.shape[0]
    beams = weights.shape[2] // 2
    rows_of = table.shape[2] // 2 // groups
    pair = 2
    lane_tiles = beams // LANES

    @pl.when(step == 0)
    def _():
        copies = [pltpu.make_async_copy(ref, to, sems.at[k]) for k, (ref, to) in enumerate(zip(sources, held))]
        for copy in copies:
            copy.start()
        for k in range(0, source_count, ranges):
            for copy in copies[k : k + ranges]:
                copy.wait()
            pieces = []
            for ref in held[k : k + ranges]:
                pieces += [(ref, slice(n, n + LANES)) for n in range(0, ref.shape[3], LANES)]

            def radix(i, carry, pieces=pieces, low=k // ranges * stations):
                f, rows = i // tiles, pl.ds(pl.multiple_of(i % tiles * SB, SB), SB)
                values = [tuple(ref[f, part, rows, lanes].astype(F32) for part in range(2)) for ref, lanes in pieces]
                target = pl.ds(pl.multiple_of(f * station_count + low + i % tiles * SB, SB), SB)
                for b, (re, im) in enumerate(sixteen_points(values)):
                    mixed[b, target, :LANES] = re.astype(BF16)
                    mixed[b, target, LANES:] = im.astype(BF16)
                return carry

            lax.fori_loop(0, frames * tiles, radix, 0)

        def transform(b, carry):
            for start in range(0, frames, pair):
                product = lax.dot_general(
                    table[0, b],
                    mixed[b, start * station_count : (start + pair) * station_count],
                    (((1,), (1,)), ((), ())),
                    preferred_element_type=F32,
                )
                product = product.reshape(2, groups, rows_of, pair * station_count)
                rows = slice(start * rows_of, (start + pair) * rows_of)
                for part in range(2):
                    value = jnp.concatenate(
                        [product[part, :, :, f * station_count : (f + 1) * station_count] for f in range(pair)], axis=1
                    )
                    columns = slice(part * station_count, (part + 1) * station_count)
                    spectra[:, b, rows, columns] = value.astype(BF16)
            return carry

        lax.fori_loop(0, RADIX, transform, 0, unroll=4)

    for k in range(weights.shape[0]):
        rows = spectra[step * weights.shape[0] + k].reshape(RADIX * frames * rows_of, 2 * station_count)
        beam = jnp.dot(rows, weights[k], preferred_element_type=F32)
        re, im = beam[:, :beams], beam[:, beams:]
        power = re * re + im * im
        if not has_earlier:
            out[k] = power
            continue
        power = power + earlier[k]
        for b in range(RADIX):
            for f in range(frames):
                at = (b * frames + f) * rows_of
                channels = pl.ds(k * rows_of * RADIX + b, rows_of, stride=RADIX)
                for t in range(lane_tiles):
                    out[channels, t, f, :] = power[at : at + rows_of, t * LANES : (t + 1) * LANES]


def beam_power(place, sources, ranges, table, weights, earlier, channels, later=()):
    frames = sources[0].shape[0]
    groups, depth, width = weights.shape
    beams = width // 2
    station_count = sum(s.shape[2] for s in sources) // ranges
    at_once = 2
    flat = (groups, channels // groups * frames, beams)
    flat_spec = pl.BlockSpec((at_once,) + flat[1:], lambda i, place: (i, 0, 0))
    in_specs = [pl.BlockSpec(memory_space=pltpu.HBM) for s in sources]
    in_specs += [
        pl.BlockSpec((1,) + table.shape[1:], lambda i, place: (place[1], 0, 0, 0)),
        pl.BlockSpec((at_once, depth, width), lambda i, place: (i, 0, 0)),
    ]
    operands = list(sources) + [table, weights]
    free = [pl.BlockSpec(memory_space=pl.ANY)] * len(later)
    scratch = [
        pltpu.VMEM((RADIX, frames * station_count, 2 * LANES), BF16),
        pltpu.VMEM((groups, RADIX, frames * channels // groups // RADIX, 2 * station_count), BF16),
        pltpu.SemaphoreType.DMA((len(sources),)),
    ]
    scratch += [pltpu.VMEM(s.shape, BF16) for s in sources]
    if earlier is None:
        out_shape = jax.ShapeDtypeStruct(flat, F32)
        out_spec = flat_spec
    else:
        out_shape = jax.ShapeDtypeStruct((channels, beams // LANES, frames, LANES), F32)
        out_spec = pl.BlockSpec((channels // groups * at_once,) + out_shape.shape[1:], lambda i, place: (i, 0, 0, 0))
        operands.append(earlier)
        in_specs.append(flat_spec)
    return pl.pallas_call(
        functools.partial(beam_kernel, len(sources), ranges, len(later), earlier is not None),
        out_shape=out_shape,
        grid_spec=pltpu.PrefetchScalarGridSpec(
            num_scalar_prefetch=1,
            grid=(groups // at_once,),
            in_specs=in_specs + free,
            out_specs=out_spec,
            scratch_shapes=scratch,
        ),
        compiler_params=pltpu.CompilerParams(vmem_limit_bytes=VMEM_LIMIT),
        cost_estimate=cost(0),
        name="beams",
    )(place, *operands, *later)


def flipped(rows, bit):
    return jnp.where(bit == 1, rows[::-1], rows)


def body(voltages, filter_taps, use_mask, block_index, weight_blocks):
    stations, pols, frames, parts, samples = voltages.shape
    history = filter_taps.shape[0] - 1
    half = stations // 2
    time_devices = lax.axis_size("tm")
    side = lax.axis_index("tm") % 2
    core = lax.axis_index("stn")
    place = jnp.stack([side, core]).astype(jnp.int32)

    def pair(block):
        return lax.ppermute(block, "tm", [(i, i ^ 1) for i in range(time_devices)])

    def hop(block, skip=0):
        return lax.ppermute(block, "tm", [(i, i + 2) for i in range(skip, time_devices - 2)])

    def swap(block):
        return lax.ppermute(block, "stn", [(0, 1), (1, 0)])

    def laid(block):
        return jnp.moveaxis(block, 0, -2)

    columns = weight_blocks.shape[1] // CORES
    shard = lax.dynamic_slice_in_dim(weight_blocks, core * columns, columns, 1)
    shards = [shard] + [
        lax.ppermute(shard, "tm", [(i, i ^ far) for i in range(time_devices)]) for far in range(2, time_devices, 2)
    ]
    own, *other = cut(place, voltages, [(pol, 0, half) for pol in range(pols)], [])
    own = after(own, *shards[1:])
    own_back = laid(after(hop(own)))
    own = laid(own)
    other = [laid(after(pair(block))) for block in other]
    shards = jnp.concatenate(shards)
    shards = jnp.concatenate([shards, pair(shards)])

    def ordered(rows):
        rows = rows.T.reshape(2, 2, 2, -1)
        rows = flipped(rows, core)
        rows = flipped(rows.swapaxes(0, 1), side).swapaxes(0, 1)
        return rows.reshape(8, -1)

    each = weight_blocks.shape[0]
    apart = block_index // each ^ lax.axis_index("tm")
    index = (apart % 2 * (time_devices // 2) + apart // 2) * each + block_index % each
    weights = beam_weights(shards, ordered(index), ordered(use_mask), other)
    table = jnp.asarray(dft_tables(samples))
    taps = jnp.broadcast_to(filter_taps[:, None, :], (history + 1, 8, samples))

    parts_of = [(samples // 2, samples // 2), (5 * samples // 8, 3 * samples // 8)]
    chunks = [(pol, sum(sizes[:i]), size) for pol, sizes in enumerate(parts_of) for i, size in enumerate(sizes)]
    other_back = [hop(block) for block in other]
    further = [onward(place, own_back, other_back[pol], pol, low, size) for pol, low, size in chunks]
    far = [hop(block, 2) for block in further]
    partial = []
    for pol in range(pols):
        gates = further[: 2 * pol + 2] + [weights]
        partial.append(near_filter(place, taps, own, other[pol], own_back, other_back[pol], pol, gates))
    keeps, sents, power = [], [], None

    def power_of(pol, earlier, later=()):
        mine, pairs = keeps[2 * pol : 2 * pol + 2], sents[2 * pol : 2 * pol + 2]
        sources = mine + pairs + [swap(block) for block in mine + pairs]
        return beam_power(place, sources, 2, table, weights, earlier, samples // CORES, later)

    for k, (pol, low, size) in enumerate(chunks):
        gates = {0: [], 1: [*sents[:1], partial[1]], 2: sents[1:2], 3: [power]}[k]
        keep, send = far_filter(place, taps, partial[pol], far[k], low, size, gates)
        keeps.append(keep)
        sents.append(pair(send))
        if k == 2:
            power = power_of(0, None, [keep])
    power = power_of(1, power)
    return jnp.moveaxis(power, 1, 2).reshape(power.shape[0], power.shape[2], -1)


def solution(mesh):
    in_specs = (
        P(("parts", "stn"), None, "tm", None, None),
        P(),
        P("parts", None),
        P("parts", None),
        P("tm", None),
    )
    out_specs = P("stn", "tm", "parts")
    return jax.shard_map(body, mesh=mesh, in_specs=in_specs, out_specs=out_specs, check_vma=False)
```

```python
import functools
import math

import jax
import jax.numpy as jnp
import ml_dtypes
import numpy as np
from jax import lax
from jax.experimental import pallas as pl
from jax.experimental.pallas import tpu as pltpu
from jax.sharding import PartitionSpec as P

SB = 16
G = 16
RADIX = 16
LANES = 128
CORES = 2
VMEM_LIMIT = 63 * 1024 * 1024
F32 = jnp.float32
BF16 = jnp.bfloat16


def cost(microseconds):
    return pl.CostEstimate(flops=0, bytes_accessed=int(microseconds * 3.3e6), transcendentals=0)


def dft_tables(channels):
    per_half = channels // RADIX // CORES
    b = np.arange(RADIX)[None, :, None, None]
    e = np.arange(LANES)[None, None, None, :]
    d = np.arange(CORES * per_half).reshape(CORES, 1, per_half, 1)
    angle = (e * (RADIX * d + b) % channels) * (2.0 * math.pi / channels)
    cosine, sine = np.cos(angle), np.sin(angle)
    real_rows = np.concatenate([cosine, sine], axis=3)
    imag_rows = np.concatenate([-sine, cosine], axis=3)
    table = np.concatenate([real_rows, imag_rows], axis=2) / math.sqrt(channels)
    return table.astype(ml_dtypes.bfloat16)


def turned(value, step, size):
    re, im = value
    step %= size
    if step == 0:
        return re, im
    if 4 * step == size:
        return im, -re
    if 2 * step == size:
        return -re, -im
    if 4 * step == 3 * size:
        return -im, re
    cosine, sine = math.cos(2 * math.pi * step / size), math.sin(2 * math.pi * step / size)
    if 8 * step == size:
        return (re + im) * cosine, (im - re) * cosine
    if 8 * step == 3 * size:
        return (im - re) * sine, -(re + im) * sine
    return re * cosine + im * sine, im * cosine - re * sine


def four_points(values):
    (r0, i0), (r1, i1), (r2, i2), (r3, i3) = values
    sr, si, dr, di = r0 + r2, i0 + i2, r0 - r2, i0 - i2
    tr, ti, er, ei = r1 + r3, i1 + i3, r1 - r3, i1 - i3
    return [(sr + tr, si + ti), (dr + ei, di - er), (sr - tr, si - ti), (dr - ei, di + er)]


def sixteen_points(values):
    inner = [four_points([values[4 * a1 + a0] for a1 in range(4)]) for a0 in range(4)]
    result = [None] * 16
    for b0 in range(4):
        outer = four_points([turned(inner[a0][b0], a0 * b0, 16) for a0 in range(4)])
        for b1 in range(4):
            result[4 * b1 + b0] = outer[b1]
    return result


def after(block, *earlier):
    return pl.pallas_call(
        lambda *refs: None,
        out_shape=jax.ShapeDtypeStruct(block.shape, block.dtype),
        in_specs=[pl.BlockSpec(memory_space=pl.ANY)] * (1 + len(earlier)),
        out_specs=pl.BlockSpec(memory_space=pl.ANY),
        input_output_aliases={0: 0},
        cost_estimate=cost(0),
        name="after",
    )(block, *earlier)


def cut_kernel(cuts, place, voltages, *rest):
    (own, *outs), (buffer, loads, stores) = rest[-4 - len(cuts) : -3], rest[-3:]
    half = own.shape[0]
    pieces = loads.shape[1]
    size = half // pieces
    side = place[0]

    def load(h, k):
        start = jnp.where(side == h, 0, half) + k * size
        return pltpu.make_async_copy(
            voltages.at[pl.ds(start, size)], buffer.at[h, pl.ds(k * size, size)], loads.at[h, k]
        )

    def store(h, k):
        copies = []
        if h == 0:
            copies.append(pltpu.make_async_copy(buffer.at[0, pl.ds(k * size, size)], own.at[pl.ds(k * size, size)], stores.at[0, k]))
        else:
            for pol in range(voltages.shape[1]):
                for out, (which, low, count) in zip(outs, cuts):
                    if which == pol and low <= k * size < low + count:
                        copies.append(
                            pltpu.make_async_copy(
                                buffer.at[1, pl.ds(k * size, size), pol],
                                out.at[pl.ds(k * size - low, size)],
                                stores.at[1 + pol, k],
                            )
                        )
        return copies

    order = [(h, k) for h in range(2) for k in range(pieces)]
    for h, k in order:
        load(h, k).start()
    for h, k in order:
        load(h, k).wait()
        for copy in store(h, k):
            copy.start()
    for h, k in order:
        for copy in store(h, k):
            copy.wait()


def cut(place, voltages, cuts, earlier):
    stations, pols, frames, parts, samples = voltages.shape
    half = stations // 2
    pieces = 4
    shapes = [(half, pols, frames, parts, samples)] + [(size, frames, parts, samples) for _, _, size in cuts]
    anywhere = pl.BlockSpec(memory_space=pltpu.HBM)
    return pl.pallas_call(
        functools.partial(cut_kernel, cuts),
        out_shape=[jax.ShapeDtypeStruct(shape, BF16) for shape in shapes],
        in_specs=[pl.BlockSpec(memory_space=pltpu.SMEM), anywhere] + [pl.BlockSpec(memory_space=pl.ANY)] * len(earlier),
        out_specs=[anywhere] * len(shapes),
        scratch_shapes=[
            pltpu.VMEM((2,) + shapes[0], BF16),
            pltpu.SemaphoreType.DMA((2, pieces)),
            pltpu.SemaphoreType.DMA((1 + pols, pieces)),
        ],
        compiler_params=pltpu.CompilerParams(vmem_limit_bytes=VMEM_LIMIT),
        cost_estimate=cost(4),
        name="cut",
    )(place, voltages, *earlier)


def weighted(taps, window, count, lanes, part, rows, sums):
    tap_count = taps.shape[0]
    tap_rows = [taps[k, :, lanes][None] for k in range(tap_count)]
    for j, ref, index in window:
        value = ref[index, part, rows, lanes].astype(F32).reshape(SB // 8, 8, LANES)
        for f in range(count):
            k = f - j
            if 0 <= k < tap_count:
                term = tap_rows[k] * value
                sums[f] = term if sums[f] is None else sums[f] + term
    return sums


def over_tiles(stations, samples, step):
    tiles, lane_tiles = stations // SB, samples // LANES

    def body(i, carry):
        lanes = pl.ds(pl.multiple_of(i % lane_tiles * LANES, LANES), LANES)
        rows = pl.ds(pl.multiple_of(i // (2 * lane_tiles) * SB, SB), SB)
        step(lanes, i // lane_tiles % 2, rows)
        return carry

    lax.fori_loop(0, 2 * tiles * lane_tiles, body, 0, unroll=2)


def near_kernel(place, taps, own, other, own_back, other_back, *rest):
    partial = rest[-1]
    frames = own.shape[0]
    count = 2 * frames

    def run(first, second, first_back, second_back):
        window = []
        for start, ref in ((-count, first_back), (frames - count, second_back), (0, first), (frames, second)):
            window += [(start + i, ref, i) for i in range(frames)]

        def step(lanes, part, rows):
            sums = weighted(taps, window, count, lanes, part, rows, [None] * count)
            for f in range(count):
                partial[f, part, rows, lanes] = sums[f].reshape(SB, LANES)

        over_tiles(*own.shape[2:], step)

    @pl.when(place[0] == 0)
    def _():
        run(own, other, own_back, other_back)

    @pl.when(place[0] == 1)
    def _():
        run(other, own, other_back, own_back)


def far_kernel(place, taps, partial, far, *rest):
    keep, send = rest[-2:]
    frames = keep.shape[0]
    count = 2 * frames
    window = [(i + 1 - 2 * count, far, i) for i in range(far.shape[0])]

    def run(first_out, second_out):
        def step(lanes, part, rows):
            sums = [partial[f, part, rows, lanes].reshape(SB // 8, 8, LANES) for f in range(count)]
            sums = weighted(taps, window, count, lanes, part, rows, sums)
            for f in range(count):
                out = first_out if f < frames else second_out
                out[f % frames, part, rows, lanes] = sums[f].reshape(SB, LANES).astype(BF16)

        over_tiles(*keep.shape[2:], step)

    @pl.when(place[0] == 0)
    def _():
        run(keep, send)

    @pl.when(place[0] == 1)
    def _():
        run(send, keep)


def near_filter(place, taps, own, other, own_back, other_back, pol, earlier):
    frames, parts, stations, samples = other.shape
    block = 512
    both = pl.BlockSpec((None, frames, parts, stations, block), lambda i, place: (pol, 0, 0, 0, i))
    one = pl.BlockSpec((frames, parts, stations, block), lambda i, place: (0, 0, 0, i))
    return pl.pallas_call(
        near_kernel,
        out_shape=jax.ShapeDtypeStruct((2 * frames, parts, stations, samples), F32),
        grid_spec=pltpu.PrefetchScalarGridSpec(
            num_scalar_prefetch=1,
            grid=(samples // block,),
            in_specs=[pl.BlockSpec((taps.shape[0], 8, block), lambda i, place: (0, 0, i)), both, one, both, one]
            + [pl.BlockSpec(memory_space=pl.ANY)] * len(earlier),
            out_specs=pl.BlockSpec((2 * frames, parts, stations, block), lambda i, place: (0, 0, 0, i)),
        ),
        compiler_params=pltpu.CompilerParams(vmem_limit_bytes=VMEM_LIMIT),
        cost_estimate=cost(8 * stations / 32),
        name="near",
    )(place, taps, own, other, own_back, other_back, *earlier)


def far_filter(place, taps, partial, far, low, size, earlier):
    count, parts, stations, _ = partial.shape
    frames = count // 2
    block = size // 2

    def spec(depth, start):
        shape = (pl.Element(depth), pl.Element(parts), pl.Element(stations), pl.Element(block))
        return pl.BlockSpec(shape, lambda i, place: (0, 0, 0, pl.multiple_of(start + i * block, LANES)))

    shape = jax.ShapeDtypeStruct((frames, parts, stations, size), BF16)
    return pl.pallas_call(
        far_kernel,
        out_shape=(shape, shape),
        grid_spec=pltpu.PrefetchScalarGridSpec(
            num_scalar_prefetch=1,
            grid=(size // block,),
            in_specs=[
                pl.BlockSpec(
                    (pl.Element(taps.shape[0]), pl.Element(8), pl.Element(block)),
                    lambda i, place: (0, 0, pl.multiple_of(low + i * block, LANES)),
                )
            ]
            + [spec(count, low), spec(far.shape[0], 0)]
            + [pl.BlockSpec(memory_space=pl.ANY)] * len(earlier),
            out_specs=[spec(frames, 0)] * 2,
        ),
        compiler_params=pltpu.CompilerParams(vmem_limit_bytes=VMEM_LIMIT),
        cost_estimate=cost(1),
        name="far",
    )(place, taps, partial, far, *earlier)


def onward_kernel(place, own_back, other_back, far):
    frames = other_back.shape[0]
    own_back = own_back.at[0]

    def run(first, second):
        far[: frames - 1] = first[1:]
        far[frames - 1 :] = second[...]

    @pl.when(place[0] == 0)
    def _():
        run(own_back, other_back)

    @pl.when(place[0] == 1)
    def _():
        run(other_back, own_back)


def onward(place, own_back, other_back, pol, low, size):
    frames, parts, stations, _ = other_back.shape
    depth = 2 * frames - 1

    def spec(depth, *before):
        shape = tuple(pl.Element(n) for n in (1,) * len(before) + (depth, 1, stations, size))
        return pl.BlockSpec(shape, lambda i, place: before + (0, i, 0, low))

    return pl.pallas_call(
        onward_kernel,
        out_shape=jax.ShapeDtypeStruct((depth, parts, stations, size), BF16),
        grid_spec=pltpu.PrefetchScalarGridSpec(
            num_scalar_prefetch=1,
            grid=(parts,),
            in_specs=[spec(frames, pol), spec(frames)],
            out_specs=pl.BlockSpec((depth, 1, stations, size), lambda i, place: (0, i, 0, 0)),
        ),
        compiler_params=pltpu.CompilerParams(vmem_limit_bytes=VMEM_LIMIT),
        cost_estimate=cost(3),
        name="onward",
    )(place, own_back, other_back)


def weight_kernel(table, index, mask, *rest):
    out = rest[-1]
    groups, depth, width = out.shape
    beams = width // 2
    half = depth // 2
    rows = lax.broadcasted_iota(jnp.int32, (table.shape[0], beams), 0)
    for q in range(index.shape[0]):
        hit = jnp.where((rows == index[q : q + 1, :]) & (mask[q : q + 1, :] != 0), 1.0, 0.0).astype(BF16)
        picked = lax.dot_general(table[...], hit, (((0,), (0,)), ((), ())), preferred_element_type=F32)
        picked = picked.reshape(groups, 2, SB, beams)
        low = q * SB
        re, im = picked[:, 0], picked[:, 1]
        out[:, low : low + SB, :beams] = re.astype(BF16)
        out[:, low : low + SB, beams:] = im.astype(BF16)
        low += half
        out[:, low : low + SB, :beams] = (-im).astype(BF16)
        out[:, low : low + SB, beams:] = re.astype(BF16)


def beam_weights(table, index, mask, earlier):
    blocks, beams = index.shape
    groups = table.shape[1] // (2 * SB)
    shape = (groups, 2 * blocks * SB, 2 * beams)
    return pl.pallas_call(
        weight_kernel,
        out_shape=jax.ShapeDtypeStruct(shape, BF16),
        in_specs=[pl.BlockSpec(memory_space=pltpu.VMEM)] * 3 + [pl.BlockSpec(memory_space=pl.ANY)] * len(earlier),
        compiler_params=pltpu.CompilerParams(vmem_limit_bytes=VMEM_LIMIT),
        cost_estimate=cost(4),
        name="weights",
    )(table, index, mask, *earlier)


def beam_kernel(source_count, ranges, later_count, has_earlier, place, *refs):
    refs = list(refs)
    inputs = [refs.pop(0) for _ in range(source_count + 2 + has_earlier)]
    refs = refs[later_count:]
    out, mixed, spectra, sems, *held = refs
    inputs[source_count] = inputs[source_count].at[pl.ds(place[1], 1)]
    copies = [pltpu.make_async_copy(ref, to, sems.at[k]) for k, (ref, to) in enumerate(zip(inputs, held))]
    table, weights = held[source_count : source_count + 2]
    step = pl.program_id(0)
    frames, _, stations, _ = held[0].shape
    tiles = stations // SB
    station_count = stations * (source_count // ranges)
    groups = spectra.shape[0]
    beams = weights.shape[2] // 2
    rows_of = table.shape[2] // 2 // groups
    pair = 2
    lane_tiles = beams // LANES
    at_once = groups // pl.num_programs(0)

    @pl.when(step == 0)
    def _():
        for copy in copies:
            copy.start()
        for k in range(0, source_count, ranges):
            for copy in copies[k : k + ranges]:
                copy.wait()
            pieces = []
            for ref in held[k : k + ranges]:
                pieces += [(ref, slice(n, n + LANES)) for n in range(0, ref.shape[3], LANES)]

            def radix(i, carry, pieces=pieces, low=k // ranges * stations):
                f, rows = i // tiles, pl.ds(pl.multiple_of(i % tiles * SB, SB), SB)
                values = [tuple(ref[f, part, rows, lanes].astype(F32) for part in range(2)) for ref, lanes in pieces]
                target = pl.ds(pl.multiple_of(f * station_count + low + i % tiles * SB, SB), SB)
                for b, (re, im) in enumerate(sixteen_points(values)):
                    mixed[b, target, :LANES] = re.astype(BF16)
                    mixed[b, target, LANES:] = im.astype(BF16)
                return carry

            lax.fori_loop(0, frames * tiles, radix, 0)
        copies[source_count].wait()

        def transform(b, carry):
            for start in range(0, frames, pair):
                product = lax.dot_general(
                    table[0, b],
                    mixed[b, start * station_count : (start + pair) * station_count],
                    (((1,), (1,)), ((), ())),
                    preferred_element_type=F32,
                )
                product = product.reshape(2, groups, rows_of, pair * station_count)
                rows = slice(start * rows_of, (start + pair) * rows_of)
                for part in range(2):
                    value = jnp.concatenate(
                        [product[part, :, :, f * station_count : (f + 1) * station_count] for f in range(pair)], axis=1
                    )
                    columns = slice(part * station_count, (part + 1) * station_count)
                    spectra[:, b, rows, columns] = value.astype(BF16)
            return carry

        lax.fori_loop(0, RADIX, transform, 0, unroll=4)
        for copy in copies[source_count + 1 :]:
            copy.wait()

    for k in range(at_once):
        group = step * at_once + k
        rows = spectra[group].reshape(RADIX * frames * rows_of, 2 * station_count)
        beam = jnp.dot(rows, weights[group], preferred_element_type=F32)
        re, im = beam[:, :beams], beam[:, beams:]
        power = re * re + im * im
        if not has_earlier:
            out[k] = power
            continue
        power = power + held[-1][group]
        for b in range(RADIX):
            for f in range(frames):
                at = (b * frames + f) * rows_of
                channels = pl.ds(k * rows_of * RADIX + b, rows_of, stride=RADIX)
                for t in range(lane_tiles):
                    out[channels, t, f, :] = power[at : at + rows_of, t * LANES : (t + 1) * LANES]


def beam_power(place, sources, ranges, table, weights, earlier, channels, later=()):
    frames = sources[0].shape[0]
    groups, depth, width = weights.shape
    beams = width // 2
    station_count = sum(s.shape[2] for s in sources) // ranges
    at_once = 2
    flat = (groups, channels // groups * frames, beams)
    flat_spec = pl.BlockSpec((at_once,) + flat[1:], lambda i, place: (i, 0, 0))
    operands = list(sources) + [table, weights] + ([] if earlier is None else [earlier])
    in_specs = [pl.BlockSpec(memory_space=pltpu.HBM)] * len(operands) + [pl.BlockSpec(memory_space=pl.ANY)] * len(later)
    scratch = [
        pltpu.VMEM((RADIX, frames * station_count, 2 * LANES), BF16),
        pltpu.VMEM((groups, RADIX, frames * channels // groups // RADIX, 2 * station_count), BF16),
        pltpu.SemaphoreType.DMA((len(operands),)),
    ]
    for k, block in enumerate(operands):
        scratch.append(pltpu.VMEM(((1,) if k == len(sources) else block.shape[:1]) + block.shape[1:], block.dtype))
    if earlier is None:
        out_shape = jax.ShapeDtypeStruct(flat, F32)
        out_spec = flat_spec
    else:
        out_shape = jax.ShapeDtypeStruct((channels, beams // LANES, frames, LANES), F32)
        out_spec = pl.BlockSpec((channels // groups * at_once,) + out_shape.shape[1:], lambda i, place: (i, 0, 0, 0))
    return pl.pallas_call(
        functools.partial(beam_kernel, len(sources), ranges, len(later), earlier is not None),
        out_shape=out_shape,
        grid_spec=pltpu.PrefetchScalarGridSpec(
            num_scalar_prefetch=1,
            grid=(groups // at_once,),
            in_specs=in_specs,
            out_specs=out_spec,
            scratch_shapes=scratch,
        ),
        compiler_params=pltpu.CompilerParams(vmem_limit_bytes=VMEM_LIMIT),
        cost_estimate=cost(0),
        name="beams",
    )(place, *operands, *later)


def flipped(rows, bit):
    return jnp.where(bit == 1, rows[::-1], rows)


def body(voltages, filter_taps, use_mask, block_index, weight_blocks):
    stations, pols, frames, parts, samples = voltages.shape
    history = filter_taps.shape[0] - 1
    half = stations // 2
    time_devices = lax.axis_size("tm")
    side = lax.axis_index("tm") % 2
    core = lax.axis_index("stn")
    place = jnp.stack([side, core]).astype(jnp.int32)

    def pair(block):
        return lax.ppermute(block, "tm", [(i, i ^ 1) for i in range(time_devices)])

    def hop(block, skip=0):
        return lax.ppermute(block, "tm", [(i, i + 2) for i in range(skip, time_devices - 2)])

    def swap(block):
        return lax.ppermute(block, "stn", [(0, 1), (1, 0)])

    def laid(block):
        return jnp.moveaxis(block, 0, -2)

    own, *other = cut(place, voltages, [(pol, 0, half) for pol in range(pols)], [])
    columns = weight_blocks.shape[1] // CORES
    shard = lax.dynamic_slice_in_dim(weight_blocks, core * columns, columns, 1)
    shards = [shard] + [
        lax.ppermute(shard, "tm", [(i, i ^ apart) for i in range(time_devices)]) for apart in range(2, time_devices, 2)
    ]
    own_back = laid(after(hop(own), *shards[1:]))
    shards = jnp.concatenate(shards)
    own = laid(own)
    other = [laid(after(pair(block))) for block in other]

    def ordered(rows):
        rows = rows.T.reshape(2, 2, 2, -1)
        rows = flipped(rows, core)
        rows = flipped(rows.swapaxes(0, 1), side).swapaxes(0, 1)
        return rows.reshape(8, -1)

    each = weight_blocks.shape[0]
    apart = block_index // each ^ lax.axis_index("tm")
    index = (apart % 2 * (time_devices // 2) + apart // 2) * each + block_index % each
    table = jnp.asarray(dft_tables(samples))
    taps = jnp.broadcast_to(filter_taps[:, None, :], (history + 1, 8, samples))

    chunks = [(pol, low, samples // 2) for pol in range(pols) for low in (0, samples // 2)]
    other_back = [hop(block) for block in other]
    further = [onward(place, own_back, other_back[pol], pol, low, size) for pol, low, size in chunks]
    far = [hop(block, 2) for block in further]
    weights = beam_weights(jnp.concatenate([shards, pair(shards)]), ordered(index), ordered(use_mask), [])
    partial = []
    for pol in range(pols):
        gates = further[: 2 * pol + 2] + [weights]
        partial.append(near_filter(place, taps, own, other[pol], own_back, other_back[pol], pol, gates))
    keeps, sents, power = [], [], None

    def power_of(pol, earlier, later=()):
        mine, pairs = keeps[2 * pol : 2 * pol + 2], sents[2 * pol : 2 * pol + 2]
        sources = mine + pairs + [swap(block) for block in mine + pairs]
        return beam_power(place, sources, 2, table, weights, earlier, samples // CORES, later)

    for k, (pol, low, size) in enumerate(chunks):
        gates = {0: [], 1: [*sents[:1], partial[1]], 2: sents[1:2], 3: sents[2:3]}[k]
        keep, send = far_filter(place, taps, partial[pol], far[k], low, size, gates)
        keeps.append(keep)
        sents.append(pair(send))
    power = power_of(0, None, keeps[-1:])
    sents[-1] = after(sents[-1], power)
    power = power_of(1, power)
    return jnp.moveaxis(power, 1, 2).reshape(power.shape[0], power.shape[2], -1)


def solution(mesh):
    in_specs = (
        P(("parts", "stn"), None, "tm", None, None),
        P(),
        P("parts", None),
        P("parts", None),
        P("tm", None),
    )
    out_specs = P("stn", "tm", "parts")
    return jax.shard_map(body, mesh=mesh, in_specs=in_specs, out_specs=out_specs, check_vma=False)
```

```python
import functools
import math

import jax
import jax.numpy as jnp
import ml_dtypes
import numpy as np
from jax import lax
from jax.experimental import pallas as pl
from jax.experimental.pallas import tpu as pltpu
from jax.sharding import PartitionSpec as P

SB = 16
G = 16
RADIX = 16
LANES = 128
CORES = 2
VMEM_LIMIT = 63 * 1024 * 1024
F32 = jnp.float32
BF16 = jnp.bfloat16


def cost(microseconds):
    return pl.CostEstimate(flops=0, bytes_accessed=int(microseconds * 3.3e6), transcendentals=0)


def dft_tables(channels):
    per_half = channels // RADIX // CORES
    b = np.arange(RADIX)[None, :, None, None]
    e = np.arange(LANES)[None, None, None, :]
    d = np.arange(CORES * per_half).reshape(CORES, 1, per_half, 1)
    angle = (e * (RADIX * d + b) % channels) * (2.0 * math.pi / channels)
    cosine, sine = np.cos(angle), np.sin(angle)
    real_rows = np.concatenate([cosine, sine], axis=3)
    imag_rows = np.concatenate([-sine, cosine], axis=3)
    table = np.concatenate([real_rows, imag_rows], axis=2) / math.sqrt(channels)
    return table.astype(ml_dtypes.bfloat16)


def turned(value, step, size):
    re, im = value
    step %= size
    if step == 0:
        return re, im
    if 4 * step == size:
        return im, -re
    if 2 * step == size:
        return -re, -im
    if 4 * step == 3 * size:
        return -im, re
    cosine, sine = math.cos(2 * math.pi * step / size), math.sin(2 * math.pi * step / size)
    if 8 * step == size:
        return (re + im) * cosine, (im - re) * cosine
    if 8 * step == 3 * size:
        return (im - re) * sine, -(re + im) * sine
    return re * cosine + im * sine, im * cosine - re * sine


def four_points(values):
    (r0, i0), (r1, i1), (r2, i2), (r3, i3) = values
    sr, si, dr, di = r0 + r2, i0 + i2, r0 - r2, i0 - i2
    tr, ti, er, ei = r1 + r3, i1 + i3, r1 - r3, i1 - i3
    return [(sr + tr, si + ti), (dr + ei, di - er), (sr - tr, si - ti), (dr - ei, di + er)]


def sixteen_points(values):
    inner = [four_points([values[4 * a1 + a0] for a1 in range(4)]) for a0 in range(4)]
    result = [None] * 16
    for b0 in range(4):
        outer = four_points([turned(inner[a0][b0], a0 * b0, 16) for a0 in range(4)])
        for b1 in range(4):
            result[4 * b1 + b0] = outer[b1]
    return result


def after(block, *earlier):
    return pl.pallas_call(
        lambda *refs: None,
        out_shape=jax.ShapeDtypeStruct(block.shape, block.dtype),
        in_specs=[pl.BlockSpec(memory_space=pl.ANY)] * (1 + len(earlier)),
        out_specs=pl.BlockSpec(memory_space=pl.ANY),
        input_output_aliases={0: 0},
        cost_estimate=cost(0),
        name="after",
    )(block, *earlier)


def cut_kernel(cuts, place, voltages, *rest):
    (own, *outs), (buffer, loads, stores) = rest[-4 - len(cuts) : -3], rest[-3:]
    half = own.shape[0]
    pieces = loads.shape[1]
    size = half // pieces
    side = place[0]

    def load(h, k):
        start = jnp.where(side == h, 0, half) + k * size
        return pltpu.make_async_copy(
            voltages.at[pl.ds(start, size)], buffer.at[h, pl.ds(k * size, size)], loads.at[h, k]
        )

    def store(h, k):
        copies = []
        if h == 0:
            copies.append(pltpu.make_async_copy(buffer.at[0, pl.ds(k * size, size)], own.at[pl.ds(k * size, size)], stores.at[0, k]))
        else:
            for pol in range(voltages.shape[1]):
                for out, (which, low, count) in zip(outs, cuts):
                    if which == pol and low <= k * size < low + count:
                        copies.append(
                            pltpu.make_async_copy(
                                buffer.at[1, pl.ds(k * size, size), pol],
                                out.at[pl.ds(k * size - low, size)],
                                stores.at[1 + pol, k],
                            )
                        )
        return copies

    order = [(h, k) for h in range(2) for k in range(pieces)]
    for h, k in order:
        load(h, k).start()
    for h, k in order:
        load(h, k).wait()
        for copy in store(h, k):
            copy.start()
    for h, k in order:
        for copy in store(h, k):
            copy.wait()


def cut(place, voltages, cuts, earlier):
    stations, pols, frames, parts, samples = voltages.shape
    half = stations // 2
    pieces = 4
    shapes = [(half, pols, frames, parts, samples)] + [(size, frames, parts, samples) for _, _, size in cuts]
    anywhere = pl.BlockSpec(memory_space=pltpu.HBM)
    return pl.pallas_call(
        functools.partial(cut_kernel, cuts),
        out_shape=[jax.ShapeDtypeStruct(shape, BF16) for shape in shapes],
        in_specs=[pl.BlockSpec(memory_space=pltpu.SMEM), anywhere] + [pl.BlockSpec(memory_space=pl.ANY)] * len(earlier),
        out_specs=[anywhere] * len(shapes),
        scratch_shapes=[
            pltpu.VMEM((2,) + shapes[0], BF16),
            pltpu.SemaphoreType.DMA((2, pieces)),
            pltpu.SemaphoreType.DMA((1 + pols, pieces)),
        ],
        compiler_params=pltpu.CompilerParams(vmem_limit_bytes=VMEM_LIMIT),
        cost_estimate=cost(4),
        name="cut",
    )(place, voltages, *earlier)


def weighted(taps, window, count, lanes, part, rows, sums):
    tap_count = taps.shape[0]
    tap_rows = [taps[k, :, lanes][None] for k in range(tap_count)]
    for j, ref, index in window:
        value = ref[index, part, rows, lanes].astype(F32).reshape(SB // 8, 8, LANES)
        for f in range(count):
            k = f - j
            if 0 <= k < tap_count:
                term = tap_rows[k] * value
                sums[f] = term if sums[f] is None else sums[f] + term
    return sums


def over_tiles(stations, samples, step):
    tiles, lane_tiles = stations // SB, samples // LANES

    def body(i, carry):
        lanes = pl.ds(pl.multiple_of(i % lane_tiles * LANES, LANES), LANES)
        rows = pl.ds(pl.multiple_of(i // (2 * lane_tiles) * SB, SB), SB)
        step(lanes, i // lane_tiles % 2, rows)
        return carry

    lax.fori_loop(0, 2 * tiles * lane_tiles, body, 0, unroll=2)


def near_kernel(place, taps, own, other, own_back, other_back, *rest):
    partial = rest[-1]
    frames = own.shape[0]
    count = 2 * frames

    def run(first, second, first_back, second_back):
        window = []
        for start, ref in ((-count, first_back), (frames - count, second_back), (0, first), (frames, second)):
            window += [(start + i, ref, i) for i in range(frames)]

        def step(lanes, part, rows):
            sums = weighted(taps, window, count, lanes, part, rows, [None] * count)
            for f in range(count):
                partial[f, part, rows, lanes] = sums[f].reshape(SB, LANES)

        over_tiles(*own.shape[2:], step)

    @pl.when(place[0] == 0)
    def _():
        run(own, other, own_back, other_back)

    @pl.when(place[0] == 1)
    def _():
        run(other, own, other_back, own_back)


def far_kernel(place, taps, partial, far, *rest):
    keep, send = rest[-2:]
    frames = keep.shape[0]
    count = 2 * frames
    window = [(i + 1 - 2 * count, far, i) for i in range(far.shape[0])]

    def run(first_out, second_out):
        def step(lanes, part, rows):
            sums = [partial[f, part, rows, lanes].reshape(SB // 8, 8, LANES) for f in range(count)]
            sums = weighted(taps, window, count, lanes, part, rows, sums)
            for f in range(count):
                out = first_out if f < frames else second_out
                out[f % frames, part, rows, lanes] = sums[f].reshape(SB, LANES).astype(BF16)

        over_tiles(*keep.shape[2:], step)

    @pl.when(place[0] == 0)
    def _():
        run(keep, send)

    @pl.when(place[0] == 1)
    def _():
        run(send, keep)


def near_filter(place, taps, own, other, own_back, other_back, pol, earlier):
    frames, parts, stations, samples = other.shape
    block = 512
    both = pl.BlockSpec((None, frames, parts, stations, block), lambda i, place: (pol, 0, 0, 0, i))
    one = pl.BlockSpec((frames, parts, stations, block), lambda i, place: (0, 0, 0, i))
    return pl.pallas_call(
        near_kernel,
        out_shape=jax.ShapeDtypeStruct((2 * frames, parts, stations, samples), F32),
        grid_spec=pltpu.PrefetchScalarGridSpec(
            num_scalar_prefetch=1,
            grid=(samples // block,),
            in_specs=[pl.BlockSpec((taps.shape[0], 8, block), lambda i, place: (0, 0, i)), both, one, both, one]
            + [pl.BlockSpec(memory_space=pl.ANY)] * len(earlier),
            out_specs=pl.BlockSpec((2 * frames, parts, stations, block), lambda i, place: (0, 0, 0, i)),
        ),
        compiler_params=pltpu.CompilerParams(vmem_limit_bytes=VMEM_LIMIT),
        cost_estimate=cost(8 * stations / 32),
        name="near",
    )(place, taps, own, other, own_back, other_back, *earlier)


def far_filter(place, taps, partial, far, low, size, earlier):
    count, parts, stations, _ = partial.shape
    frames = count // 2
    block = size // 2

    def spec(depth, start):
        shape = (pl.Element(depth), pl.Element(parts), pl.Element(stations), pl.Element(block))
        return pl.BlockSpec(shape, lambda i, place: (0, 0, 0, pl.multiple_of(start + i * block, LANES)))

    shape = jax.ShapeDtypeStruct((frames, parts, stations, size), BF16)
    return pl.pallas_call(
        far_kernel,
        out_shape=(shape, shape),
        grid_spec=pltpu.PrefetchScalarGridSpec(
            num_scalar_prefetch=1,
            grid=(size // block,),
            in_specs=[
                pl.BlockSpec(
                    (pl.Element(taps.shape[0]), pl.Element(8), pl.Element(block)),
                    lambda i, place: (0, 0, pl.multiple_of(low + i * block, LANES)),
                )
            ]
            + [spec(count, low), spec(far.shape[0], 0)]
            + [pl.BlockSpec(memory_space=pl.ANY)] * len(earlier),
            out_specs=[spec(frames, 0)] * 2,
        ),
        compiler_params=pltpu.CompilerParams(vmem_limit_bytes=VMEM_LIMIT),
        cost_estimate=cost(1),
        name="far",
    )(place, taps, partial, far, *earlier)


def onward_kernel(place, own_back, other_back, *rest):
    far = rest[-1]
    frames = other_back.shape[0]
    own_back = own_back.at[0]

    def run(first, second):
        far[: frames - 1] = first[1:]
        far[frames - 1 :] = second[...]

    @pl.when(place[0] == 0)
    def _():
        run(own_back, other_back)

    @pl.when(place[0] == 1)
    def _():
        run(other_back, own_back)


def onward(place, own_back, other_back, pol, low, size, earlier):
    frames, parts, stations, _ = other_back.shape
    depth = 2 * frames - 1

    def spec(depth, *before):
        shape = tuple(pl.Element(n) for n in (1,) * len(before) + (depth, 1, stations, size))
        return pl.BlockSpec(shape, lambda i, place: before + (0, i, 0, low))

    return pl.pallas_call(
        onward_kernel,
        out_shape=jax.ShapeDtypeStruct((depth, parts, stations, size), BF16),
        grid_spec=pltpu.PrefetchScalarGridSpec(
            num_scalar_prefetch=1,
            grid=(parts,),
            in_specs=[spec(frames, pol), spec(frames)] + [pl.BlockSpec(memory_space=pl.ANY)] * len(earlier),
            out_specs=pl.BlockSpec((depth, 1, stations, size), lambda i, place: (0, i, 0, 0)),
        ),
        compiler_params=pltpu.CompilerParams(vmem_limit_bytes=VMEM_LIMIT),
        cost_estimate=cost(3),
        name="onward",
    )(place, own_back, other_back, *earlier)


def weight_kernel(table, index, mask, *rest):
    out = rest[-1]
    groups, depth, width = out.shape
    beams = width // 2
    half = depth // 2
    rows = lax.broadcasted_iota(jnp.int32, (table.shape[0], beams), 0)
    for q in range(index.shape[0]):
        hit = jnp.where((rows == index[q : q + 1, :]) & (mask[q : q + 1, :] != 0), 1.0, 0.0).astype(BF16)
        picked = lax.dot_general(table[...], hit, (((0,), (0,)), ((), ())), preferred_element_type=F32)
        picked = picked.reshape(groups, 2, SB, beams)
        low = q * SB
        re, im = picked[:, 0], picked[:, 1]
        out[:, low : low + SB, :beams] = re.astype(BF16)
        out[:, low : low + SB, beams:] = im.astype(BF16)
        low += half
        out[:, low : low + SB, :beams] = (-im).astype(BF16)
        out[:, low : low + SB, beams:] = re.astype(BF16)


def beam_weights(table, index, mask, earlier):
    blocks, beams = index.shape
    groups = table.shape[1] // (2 * SB)
    shape = (groups, 2 * blocks * SB, 2 * beams)
    return pl.pallas_call(
        weight_kernel,
        out_shape=jax.ShapeDtypeStruct(shape, BF16),
        in_specs=[pl.BlockSpec(memory_space=pltpu.VMEM)] * 3 + [pl.BlockSpec(memory_space=pl.ANY)] * len(earlier),
        compiler_params=pltpu.CompilerParams(vmem_limit_bytes=VMEM_LIMIT),
        cost_estimate=cost(4),
        name="weights",
    )(table, index, mask, *earlier)


def beam_kernel(source_count, ranges, later_count, has_earlier, place, *refs):
    refs = list(refs)
    inputs = [refs.pop(0) for _ in range(source_count + 2 + has_earlier)]
    refs = refs[later_count:]
    out, mixed, spectra, sems, *held = refs
    inputs[source_count] = inputs[source_count].at[pl.ds(place[1], 1)]
    copies = [pltpu.make_async_copy(ref, to, sems.at[k]) for k, (ref, to) in enumerate(zip(inputs, held))]
    table, weights = held[source_count : source_count + 2]
    step = pl.program_id(0)
    frames, _, stations, _ = held[0].shape
    tiles = stations // SB
    station_count = stations * (source_count // ranges)
    groups = spectra.shape[0]
    beams = weights.shape[2] // 2
    rows_of = table.shape[2] // 2 // groups
    pair = 2
    lane_tiles = beams // LANES
    at_once = groups // pl.num_programs(0)

    @pl.when(step == 0)
    def _():
        for copy in copies:
            copy.start()
        for k in range(0, source_count, ranges):
            for copy in copies[k : k + ranges]:
                copy.wait()
            pieces = []
            for ref in held[k : k + ranges]:
                pieces += [(ref, slice(n, n + LANES)) for n in range(0, ref.shape[3], LANES)]

            def radix(i, carry, pieces=pieces, low=k // ranges * stations):
                f, rows = i // tiles, pl.ds(pl.multiple_of(i % tiles * SB, SB), SB)
                values = [tuple(ref[f, part, rows, lanes].astype(F32) for part in range(2)) for ref, lanes in pieces]
                target = pl.ds(pl.multiple_of(f * station_count + low + i % tiles * SB, SB), SB)
                for b, (re, im) in enumerate(sixteen_points(values)):
                    mixed[b, target, :LANES] = re.astype(BF16)
                    mixed[b, target, LANES:] = im.astype(BF16)
                return carry

            lax.fori_loop(0, frames * tiles, radix, 0)
        copies[source_count].wait()

        def transform(b, carry):
            for start in range(0, frames, pair):
                product = lax.dot_general(
                    table[0, b],
                    mixed[b, start * station_count : (start + pair) * station_count],
                    (((1,), (1,)), ((), ())),
                    preferred_element_type=F32,
                )
                product = product.reshape(2, groups, rows_of, pair * station_count)
                rows = slice(start * rows_of, (start + pair) * rows_of)
                for part in range(2):
                    value = jnp.concatenate(
                        [product[part, :, :, f * station_count : (f + 1) * station_count] for f in range(pair)], axis=1
                    )
                    columns = slice(part * station_count, (part + 1) * station_count)
                    spectra[:, b, rows, columns] = value.astype(BF16)
            return carry

        lax.fori_loop(0, RADIX, transform, 0, unroll=4)
        for copy in copies[source_count + 1 :]:
            copy.wait()

    for k in range(at_once):
        group = step * at_once + k
        rows = spectra[group].reshape(RADIX * frames * rows_of, 2 * station_count)
        beam = jnp.dot(rows, weights[group], preferred_element_type=F32)
        re, im = beam[:, :beams], beam[:, beams:]
        power = re * re + im * im
        if not has_earlier:
            out[k] = power
            continue
        power = power + held[-1][group]
        for b in range(RADIX):
            for f in range(frames):
                at = (b * frames + f) * rows_of
                channels = pl.ds(k * rows_of * RADIX + b, rows_of, stride=RADIX)
                for t in range(lane_tiles):
                    out[channels, t, f, :] = power[at : at + rows_of, t * LANES : (t + 1) * LANES]


def beam_power(place, sources, ranges, table, weights, earlier, channels, later=()):
    frames = sources[0].shape[0]
    groups, depth, width = weights.shape
    beams = width // 2
    station_count = sum(s.shape[2] for s in sources) // ranges
    at_once = 2
    flat = (groups, channels // groups * frames, beams)
    flat_spec = pl.BlockSpec((at_once,) + flat[1:], lambda i, place: (i, 0, 0))
    operands = list(sources) + [table, weights] + ([] if earlier is None else [earlier])
    in_specs = [pl.BlockSpec(memory_space=pltpu.HBM)] * len(operands) + [pl.BlockSpec(memory_space=pl.ANY)] * len(later)
    scratch = [
        pltpu.VMEM((RADIX, frames * station_count, 2 * LANES), BF16),
        pltpu.VMEM((groups, RADIX, frames * channels // groups // RADIX, 2 * station_count), BF16),
        pltpu.SemaphoreType.DMA((len(operands),)),
    ]
    for k, block in enumerate(operands):
        scratch.append(pltpu.VMEM(((1,) if k == len(sources) else block.shape[:1]) + block.shape[1:], block.dtype))
    if earlier is None:
        out_shape = jax.ShapeDtypeStruct(flat, F32)
        out_spec = flat_spec
    else:
        out_shape = jax.ShapeDtypeStruct((channels, beams // LANES, frames, LANES), F32)
        out_spec = pl.BlockSpec((channels // groups * at_once,) + out_shape.shape[1:], lambda i, place: (i, 0, 0, 0))
    return pl.pallas_call(
        functools.partial(beam_kernel, len(sources), ranges, len(later), earlier is not None),
        out_shape=out_shape,
        grid_spec=pltpu.PrefetchScalarGridSpec(
            num_scalar_prefetch=1,
            grid=(groups // at_once,),
            in_specs=in_specs,
            out_specs=out_spec,
            scratch_shapes=scratch,
        ),
        compiler_params=pltpu.CompilerParams(vmem_limit_bytes=VMEM_LIMIT),
        cost_estimate=cost(0),
        name="beams",
    )(place, *operands, *later)


def flipped(rows, bit):
    return jnp.where(bit == 1, rows[::-1], rows)


def body(voltages, filter_taps, use_mask, block_index, weight_blocks):
    stations, pols, frames, parts, samples = voltages.shape
    history = filter_taps.shape[0] - 1
    half = stations // 2
    time_devices = lax.axis_size("tm")
    side = lax.axis_index("tm") % 2
    core = lax.axis_index("stn")
    place = jnp.stack([side, core]).astype(jnp.int32)

    def pair(block):
        return lax.ppermute(block, "tm", [(i, i ^ 1) for i in range(time_devices)])

    def hop(block, skip=0):
        return lax.ppermute(block, "tm", [(i, i + 2) for i in range(skip, time_devices - 2)])

    def swap(block):
        return lax.ppermute(block, "stn", [(0, 1), (1, 0)])

    def laid(block):
        return jnp.moveaxis(block, 0, -2)

    own, *other = cut(place, voltages, [(pol, 0, half) for pol in range(pols)], [])
    columns = weight_blocks.shape[1] // CORES
    shard = lax.dynamic_slice_in_dim(weight_blocks, core * columns, columns, 1)
    shards = [shard] + [
        lax.ppermute(shard, "tm", [(i, i ^ apart) for i in range(time_devices)]) for apart in range(2, time_devices, 2)
    ]
    own_back = laid(after(hop(own)))
    own = laid(own)
    other = [laid(after(pair(block))) for block in other]

    def ordered(rows):
        rows = rows.T.reshape(2, 2, 2, -1)
        rows = flipped(rows, core)
        rows = flipped(rows.swapaxes(0, 1), side).swapaxes(0, 1)
        return rows.reshape(8, -1)

    each = weight_blocks.shape[0]
    apart = block_index // each ^ lax.axis_index("tm")
    index = (apart % 2 * (time_devices // 2) + apart // 2) * each + block_index % each
    table = jnp.asarray(dft_tables(samples))
    taps = jnp.broadcast_to(filter_taps[:, None, :], (history + 1, 8, samples))

    parts_of = [(samples // 2, samples // 2), (5 * samples // 8, 3 * samples // 8)]
    chunks = [(pol, sum(sizes[:i]), size) for pol, sizes in enumerate(parts_of) for i, size in enumerate(sizes)]
    other_back = [hop(block) for block in other]
    further = []
    for pol, low, size in chunks:
        gates = [] if further else shards[1:]
        further.append(onward(place, own_back, other_back[pol], pol, low, size, gates))
    shards = jnp.concatenate(shards)
    far = [hop(block, 2) for block in further]
    weights = beam_weights(jnp.concatenate([shards, pair(shards)]), ordered(index), ordered(use_mask), [])
    partial = []
    for pol in range(pols):
        gates = further[: 2 * pol + 2] + [weights] + other_back[1:]
        partial.append(near_filter(place, taps, own, other[pol], own_back, other_back[pol], pol, gates))
    keeps, sents, power = [], [], None

    def power_of(pol, earlier, later=()):
        mine, pairs = keeps[2 * pol : 2 * pol + 2], sents[2 * pol : 2 * pol + 2]
        sources = mine + pairs + [swap(block) for block in mine + pairs]
        return beam_power(place, sources, 2, table, weights, earlier, samples // CORES, later)

    for k, (pol, low, size) in enumerate(chunks):
        gates = {0: [], 1: [*sents[:1], partial[1]], 2: sents[1:2], 3: [power]}[k]
        keep, send = far_filter(place, taps, partial[pol], far[k], low, size, gates)
        keeps.append(keep)
        sents.append(pair(send))
        if k == 2:
            power = power_of(0, None, [keep])
    power = power_of(1, power)
    return jnp.moveaxis(power, 1, 2).reshape(power.shape[0], power.shape[2], -1)


def solution(mesh):
    in_specs = (
        P(("parts", "stn"), None, "tm", None, None),
        P(),
        P("parts", None),
        P("parts", None),
        P("tm", None),
    )
    out_specs = P("stn", "tm", "parts")
    return jax.shard_map(body, mesh=mesh, in_specs=in_specs, out_specs=out_specs, check_vma=False)
```

```python
import functools
import math

import jax
import jax.numpy as jnp
import ml_dtypes
import numpy as np
from jax import lax
from jax.experimental import pallas as pl
from jax.experimental.pallas import tpu as pltpu
from jax.sharding import PartitionSpec as P

SB = 16
G = 16
RADIX = 16
LANES = 128
CORES = 2
VMEM_LIMIT = 63 * 1024 * 1024
F32 = jnp.float32
BF16 = jnp.bfloat16


def cost(microseconds):
    return pl.CostEstimate(flops=0, bytes_accessed=int(microseconds * 3.3e6), transcendentals=0)


def dft_tables(channels):
    per_half = channels // RADIX // CORES
    b = np.arange(RADIX)[None, :, None, None]
    e = np.arange(LANES)[None, None, None, :]
    d = np.arange(CORES * per_half).reshape(CORES, 1, per_half, 1)
    angle = (e * (RADIX * d + b) % channels) * (2.0 * math.pi / channels)
    cosine, sine = np.cos(angle), np.sin(angle)
    real_rows = np.concatenate([cosine, sine], axis=3)
    imag_rows = np.concatenate([-sine, cosine], axis=3)
    table = np.concatenate([real_rows, imag_rows], axis=2) / math.sqrt(channels)
    return table.astype(ml_dtypes.bfloat16)


def turned(value, step, size):
    re, im = value
    step %= size
    if step == 0:
        return re, im
    if 4 * step == size:
        return im, -re
    if 2 * step == size:
        return -re, -im
    if 4 * step == 3 * size:
        return -im, re
    cosine, sine = math.cos(2 * math.pi * step / size), math.sin(2 * math.pi * step / size)
    if 8 * step == size:
        return (re + im) * cosine, (im - re) * cosine
    if 8 * step == 3 * size:
        return (im - re) * sine, -(re + im) * sine
    return re * cosine + im * sine, im * cosine - re * sine


def four_points(values):
    (r0, i0), (r1, i1), (r2, i2), (r3, i3) = values
    sr, si, dr, di = r0 + r2, i0 + i2, r0 - r2, i0 - i2
    tr, ti, er, ei = r1 + r3, i1 + i3, r1 - r3, i1 - i3
    return [(sr + tr, si + ti), (dr + ei, di - er), (sr - tr, si - ti), (dr - ei, di + er)]


def sixteen_points(values):
    inner = [four_points([values[4 * a1 + a0] for a1 in range(4)]) for a0 in range(4)]
    result = [None] * 16
    for b0 in range(4):
        outer = four_points([turned(inner[a0][b0], a0 * b0, 16) for a0 in range(4)])
        for b1 in range(4):
            result[4 * b1 + b0] = outer[b1]
    return result


def after(block, *earlier):
    return pl.pallas_call(
        lambda *refs: None,
        out_shape=jax.ShapeDtypeStruct(block.shape, block.dtype),
        in_specs=[pl.BlockSpec(memory_space=pl.ANY)] * (1 + len(earlier)),
        out_specs=pl.BlockSpec(memory_space=pl.ANY),
        input_output_aliases={0: 0},
        cost_estimate=cost(0),
        name="after",
    )(block, *earlier)


def cut_kernel(mine, voltages, *rest):
    count = len(mine)
    outs, (buffer, loads, stores) = rest[-3 - count : -3], rest[-3:]
    half = buffer.shape[0]
    pieces = loads.shape[0]
    size = half // pieces
    side = lax.rem(lax.axis_index("tm"), 2)
    start = half * (side if mine[0] is None else 1 - side)

    def load(k):
        return pltpu.make_async_copy(
            voltages.at[pl.ds(start + k * size, size)], buffer.at[pl.ds(k * size, size)], loads.at[k]
        )

    def store(k, i):
        block = buffer.at[pl.ds(k * size, size)]
        block = block if mine[i] is None else block.at[:, mine[i]]
        return pltpu.make_async_copy(block, outs[i].at[pl.ds(k * size, size)], stores.at[i, k])

    for k in range(pieces):
        load(k).start()
    for k in range(pieces):
        load(k).wait()
        for i in range(count):
            store(k, i).start()
    for k in range(pieces):
        for i in range(count):
            store(k, i).wait()


def cut(voltages, mine, earlier):
    stations, pols, frames, parts, samples = voltages.shape
    whole = (stations // 2, pols, frames, parts, samples)
    shapes = [whole if pol is None else whole[:1] + whole[2:] for pol in mine]
    pieces = 4
    there = pl.BlockSpec(memory_space=pltpu.HBM)
    return pl.pallas_call(
        functools.partial(cut_kernel, mine),
        out_shape=[jax.ShapeDtypeStruct(shape, BF16) for shape in shapes],
        in_specs=[there] + [pl.BlockSpec(memory_space=pl.ANY)] * len(earlier),
        out_specs=[there] * len(shapes),
        scratch_shapes=[
            pltpu.VMEM(whole, BF16),
            pltpu.SemaphoreType.DMA((pieces,)),
            pltpu.SemaphoreType.DMA((len(mine), pieces)),
        ],
        compiler_params=pltpu.CompilerParams(vmem_limit_bytes=VMEM_LIMIT),
        cost_estimate=cost(2),
        name="cut",
    )(voltages, *earlier)


def weighted(taps, window, count, lanes, part, rows, sums):
    tap_count = taps.shape[0]
    tap_rows = [taps[k, :, lanes][None] for k in range(tap_count)]
    for j, ref, index in window:
        value = ref[index, part, rows, lanes].astype(F32).reshape(SB // 8, 8, LANES)
        for f in range(count):
            k = f - j
            if 0 <= k < tap_count:
                term = tap_rows[k] * value
                sums[f] = term if sums[f] is None else sums[f] + term
    return sums


def over_tiles(stations, samples, step):
    tiles, lane_tiles = stations // SB, samples // LANES

    def body(i, carry):
        lanes = pl.ds(pl.multiple_of(i % lane_tiles * LANES, LANES), LANES)
        rows = pl.ds(pl.multiple_of(i // (2 * lane_tiles) * SB, SB), SB)
        step(lanes, i // lane_tiles % 2, rows)
        return carry

    lax.fori_loop(0, 2 * tiles * lane_tiles, body, 0, unroll=2)


def near_kernel(place, taps, own, other, own_back, other_back, *rest):
    partial = rest[-1]
    frames = own.shape[0]
    count = 2 * frames

    def run(first, second, first_back, second_back):
        window = []
        for start, ref in ((-count, first_back), (frames - count, second_back), (0, first), (frames, second)):
            window += [(start + i, ref, i) for i in range(frames)]

        def step(lanes, part, rows):
            sums = weighted(taps, window, count, lanes, part, rows, [None] * count)
            for f in range(count):
                partial[f, part, rows, lanes] = sums[f].reshape(SB, LANES)

        over_tiles(*own.shape[2:], step)

    @pl.when(place[0] == 0)
    def _():
        run(own, other, own_back, other_back)

    @pl.when(place[0] == 1)
    def _():
        run(other, own, other_back, own_back)


def far_kernel(place, taps, partial, far, *rest):
    keep, send = rest[-2:]
    frames = keep.shape[0]
    count = 2 * frames
    window = [(i + 1 - 2 * count, far, i) for i in range(far.shape[0])]

    def run(first_out, second_out):
        def step(lanes, part, rows):
            sums = [partial[f, part, rows, lanes].reshape(SB // 8, 8, LANES) for f in range(count)]
            sums = weighted(taps, window, count, lanes, part, rows, sums)
            for f in range(count):
                out = first_out if f < frames else second_out
                out[f % frames, part, rows, lanes] = sums[f].reshape(SB, LANES).astype(BF16)

        over_tiles(*keep.shape[2:], step)

    @pl.when(place[0] == 0)
    def _():
        run(keep, send)

    @pl.when(place[0] == 1)
    def _():
        run(send, keep)


def near_filter(place, taps, own, other, own_back, other_back, pol, earlier):
    frames, parts, stations, samples = other.shape
    block = 512
    both = pl.BlockSpec((None, frames, parts, stations, block), lambda i, place: (pol, 0, 0, 0, i))
    one = pl.BlockSpec((frames, parts, stations, block), lambda i, place: (0, 0, 0, i))
    return pl.pallas_call(
        near_kernel,
        out_shape=jax.ShapeDtypeStruct((2 * frames, parts, stations, samples), F32),
        grid_spec=pltpu.PrefetchScalarGridSpec(
            num_scalar_prefetch=1,
            grid=(samples // block,),
            in_specs=[pl.BlockSpec((taps.shape[0], 8, block), lambda i, place: (0, 0, i)), both, one, both, one]
            + [pl.BlockSpec(memory_space=pl.ANY)] * len(earlier),
            out_specs=pl.BlockSpec((2 * frames, parts, stations, block), lambda i, place: (0, 0, 0, i)),
        ),
        compiler_params=pltpu.CompilerParams(vmem_limit_bytes=VMEM_LIMIT),
        cost_estimate=cost(8 * stations / 32),
        name="near",
    )(place, taps, own, other, own_back, other_back, *earlier)


def far_filter(place, taps, partial, far, low, size, earlier):
    count, parts, stations, _ = partial.shape
    frames = count // 2
    block = size // 2

    def spec(depth, start):
        shape = (pl.Element(depth), pl.Element(parts), pl.Element(stations), pl.Element(block))
        return pl.BlockSpec(shape, lambda i, place: (0, 0, 0, pl.multiple_of(start + i * block, LANES)))

    shape = jax.ShapeDtypeStruct((frames, parts, stations, size), BF16)
    return pl.pallas_call(
        far_kernel,
        out_shape=(shape, shape),
        grid_spec=pltpu.PrefetchScalarGridSpec(
            num_scalar_prefetch=1,
            grid=(size // block,),
            in_specs=[
                pl.BlockSpec(
                    (pl.Element(taps.shape[0]), pl.Element(8), pl.Element(block)),
                    lambda i, place: (0, 0, pl.multiple_of(low + i * block, LANES)),
                )
            ]
            + [spec(count, low), spec(far.shape[0], 0)]
            + [pl.BlockSpec(memory_space=pl.ANY)] * len(earlier),
            out_specs=[spec(frames, 0)] * 2,
        ),
        compiler_params=pltpu.CompilerParams(vmem_limit_bytes=VMEM_LIMIT),
        cost_estimate=cost(1),
        name="far",
    )(place, taps, partial, far, *earlier)


def onward_kernel(place, own_back, other_back, *rest):
    far = rest[-1]
    frames = other_back.shape[0]
    own_back = own_back.at[0]

    def run(first, second):
        far[: frames - 1] = first[1:]
        far[frames - 1 :] = second[...]

    @pl.when(place[0] == 0)
    def _():
        run(own_back, other_back)

    @pl.when(place[0] == 1)
    def _():
        run(other_back, own_back)


def onward(place, own_back, other_back, pol, low, size, earlier):
    frames, parts, stations, _ = other_back.shape
    depth = 2 * frames - 1

    def spec(depth, *before):
        shape = tuple(pl.Element(n) for n in (1,) * len(before) + (depth, 1, stations, size))
        return pl.BlockSpec(shape, lambda i, place: before + (0, i, 0, low))

    return pl.pallas_call(
        onward_kernel,
        out_shape=jax.ShapeDtypeStruct((depth, parts, stations, size), BF16),
        grid_spec=pltpu.PrefetchScalarGridSpec(
            num_scalar_prefetch=1,
            grid=(parts,),
            in_specs=[spec(frames, pol), spec(frames)] + [pl.BlockSpec(memory_space=pl.ANY)] * len(earlier),
            out_specs=pl.BlockSpec((depth, 1, stations, size), lambda i, place: (0, i, 0, 0)),
        ),
        compiler_params=pltpu.CompilerParams(vmem_limit_bytes=VMEM_LIMIT),
        cost_estimate=cost(3),
        name="onward",
    )(place, own_back, other_back, *earlier)


def weight_kernel(table, index, mask, *rest):
    out = rest[-1]
    groups, depth, width = out.shape
    beams = width // 2
    half = depth // 2
    rows = lax.broadcasted_iota(jnp.int32, (table.shape[0], beams), 0)
    for q in range(index.shape[0]):
        hit = jnp.where((rows == index[q : q + 1, :]) & (mask[q : q + 1, :] != 0), 1.0, 0.0).astype(BF16)
        picked = lax.dot_general(table[...], hit, (((0,), (0,)), ((), ())), preferred_element_type=F32)
        picked = picked.reshape(groups, 2, SB, beams)
        low = q * SB
        re, im = picked[:, 0], picked[:, 1]
        out[:, low : low + SB, :beams] = re.astype(BF16)
        out[:, low : low + SB, beams:] = im.astype(BF16)
        low += half
        out[:, low : low + SB, :beams] = (-im).astype(BF16)
        out[:, low : low + SB, beams:] = re.astype(BF16)


def beam_weights(table, index, mask, earlier):
    blocks, beams = index.shape
    groups = table.shape[1] // (2 * SB)
    shape = (groups, 2 * blocks * SB, 2 * beams)
    return pl.pallas_call(
        weight_kernel,
        out_shape=jax.ShapeDtypeStruct(shape, BF16),
        in_specs=[pl.BlockSpec(memory_space=pltpu.VMEM)] * 3 + [pl.BlockSpec(memory_space=pl.ANY)] * len(earlier),
        compiler_params=pltpu.CompilerParams(vmem_limit_bytes=VMEM_LIMIT),
        cost_estimate=cost(4),
        name="weights",
    )(table, index, mask, *earlier)


def beam_kernel(source_count, ranges, later_count, has_earlier, place, *refs):
    refs = list(refs)
    sources = [refs.pop(0) for _ in range(source_count)]
    others = [refs.pop(0) for _ in range(2 + has_earlier)]
    others[0] = others[0].at[pl.ds(place[1], 1)]
    refs = refs[later_count:]
    out, spectra, source_sems, other_sems = refs[:4]
    mixed, held, kept = refs[4:6], refs[6 : 6 + ranges], refs[6 + ranges :]
    table, weights = kept[:2]
    step = pl.program_id(0)
    members, frames, _, stations, _ = held[0].shape
    tiles = stations // SB
    station_count = stations * members
    groups = spectra.shape[0]
    beams = weights.shape[2] // 2
    rows_of = table.shape[2] // 2 // groups
    pair = frames // 2
    lane_tiles = beams // LANES
    at_once = groups // pl.num_programs(0)

    def arrival(p, k):
        frames_of = pl.ds(p * pair, pair)
        return pltpu.make_async_copy(
            sources[k].at[frames_of], held[k % ranges].at[k // ranges, frames_of], source_sems.at[p, k]
        )

    other_copies = [pltpu.make_async_copy(ref, to, other_sems.at[k]) for k, (ref, to) in enumerate(zip(others, kept))]
    pieces = []
    for ref in held:
        pieces += [(ref, slice(n, n + LANES)) for n in range(0, ref.shape[4], LANES)]

    def radix(p, member, i):
        f, tile = i // tiles, i % tiles
        rows = pl.ds(pl.multiple_of(tile * SB, SB), SB)
        values = [
            tuple(ref[member, p * pair + f, part, rows, lanes].astype(F32) for part in range(2)) for ref, lanes in pieces
        ]
        target = pl.ds(pl.multiple_of(f * station_count + member * stations + tile * SB, SB), SB)
        for b, (re, im) in enumerate(sixteen_points(values)):
            mixed[p][b, target, :LANES] = re.astype(BF16)
            mixed[p][b, target, LANES:] = im.astype(BF16)

    def transform(p, b):
        product = lax.dot_general(table[0, b], mixed[p][b], (((1,), (1,)), ((), ())), preferred_element_type=F32)
        product = product.reshape(2, groups, rows_of, pair * station_count)
        rows = slice(p * pair * rows_of, (p + 1) * pair * rows_of)
        for part in range(2):
            value = jnp.concatenate(
                [product[part, :, :, f * station_count : (f + 1) * station_count] for f in range(pair)], axis=1
            )
            columns = slice(part * station_count, (part + 1) * station_count)
            spectra[:, b, rows, columns] = value.astype(BF16)

    def loop(count, body, unroll):
        def step(i, carry):
            body(i)
            return carry

        lax.fori_loop(0, count, step, 0, unroll=unroll)

    @pl.when(step == 0)
    def _():
        for k in range(source_count):
            arrival(0, k).start()
        other_copies[0].start()
        for k in range(source_count):
            arrival(1, k).start()
        for copy in other_copies[1:]:
            copy.start()
        for member in range(members):
            for k in range(ranges):
                arrival(0, member * ranges + k).wait()
            loop(pair * tiles, lambda i: radix(0, member, i), 1)
        for k in range(source_count):
            arrival(1, k).wait()
        other_copies[0].wait()
        each = pair * tiles
        if members * each == RADIX:

            def both(b):
                radix(1, b // each, b % each)
                transform(0, b)

            loop(RADIX, both, 1)
        else:
            for member in range(members):
                loop(each, lambda i: radix(1, member, i), 1)
            loop(RADIX, lambda b: transform(0, b), 4)
        loop(RADIX, lambda b: transform(1, b), 4)
        for copy in other_copies[1:]:
            copy.wait()

    for k in range(at_once):
        group = step * at_once + k
        rows = spectra[group].reshape(RADIX * frames * rows_of, 2 * station_count)
        beam = jnp.dot(rows, weights[group], preferred_element_type=F32)
        re, im = beam[:, :beams], beam[:, beams:]
        power = re * re + im * im
        if not has_earlier:
            out[k] = power
            continue
        power = power + kept[2][group]
        for b in range(RADIX):
            for f in range(frames):
                at = (b * frames + f) * rows_of
                channels = pl.ds(k * rows_of * RADIX + b, rows_of, stride=RADIX)
                for t in range(lane_tiles):
                    out[channels, t, f, :] = power[at : at + rows_of, t * LANES : (t + 1) * LANES]


def beam_power(place, sources, ranges, table, weights, earlier, channels, later=()):
    frames = sources[0].shape[0]
    groups, depth, width = weights.shape
    beams = width // 2
    station_count = sum(s.shape[2] for s in sources) // ranges
    at_once = 2
    flat = (groups, channels // groups * frames, beams)
    flat_spec = pl.BlockSpec((at_once,) + flat[1:], lambda i, place: (i, 0, 0))
    operands = list(sources) + [table, weights] + ([] if earlier is None else [earlier])
    in_specs = [pl.BlockSpec(memory_space=pltpu.HBM)] * len(operands) + [pl.BlockSpec(memory_space=pl.ANY)] * len(later)
    members = len(sources) // ranges
    mixed = pltpu.VMEM((RADIX, frames // 2 * station_count, 2 * LANES), BF16)
    scratch = [
        pltpu.VMEM((groups, RADIX, frames * channels // groups // RADIX, 2 * station_count), BF16),
        pltpu.SemaphoreType.DMA((2, len(sources))),
        pltpu.SemaphoreType.DMA((3,)),
        mixed,
        mixed,
    ]
    scratch += [pltpu.VMEM((members,) + block.shape, BF16) for block in sources[:ranges]]
    scratch += [pltpu.VMEM((1,) + table.shape[1:], BF16), pltpu.VMEM(weights.shape, BF16)]
    scratch += [] if earlier is None else [pltpu.VMEM(flat, F32)]
    if earlier is None:
        out_shape = jax.ShapeDtypeStruct(flat, F32)
        out_spec = flat_spec
    else:
        out_shape = jax.ShapeDtypeStruct((channels, beams // LANES, frames, LANES), F32)
        out_spec = pl.BlockSpec((channels // groups * at_once,) + out_shape.shape[1:], lambda i, place: (i, 0, 0, 0))
    return pl.pallas_call(
        functools.partial(beam_kernel, len(sources), ranges, len(later), earlier is not None),
        out_shape=out_shape,
        grid_spec=pltpu.PrefetchScalarGridSpec(
            num_scalar_prefetch=1,
            grid=(groups // at_once,),
            in_specs=in_specs,
            out_specs=out_spec,
            scratch_shapes=scratch,
        ),
        compiler_params=pltpu.CompilerParams(vmem_limit_bytes=VMEM_LIMIT),
        cost_estimate=cost(0),
        name="beams",
    )(place, *operands, *later)


def flipped(rows, bit):
    return jnp.where(bit == 1, rows[::-1], rows)


def body(voltages, filter_taps, use_mask, block_index, weight_blocks):
    stations, pols, frames, parts, samples = voltages.shape
    history = filter_taps.shape[0] - 1
    half = stations // 2
    time_devices = lax.axis_size("tm")
    side = lax.axis_index("tm") % 2
    core = lax.axis_index("stn")
    place = jnp.stack([side, core]).astype(jnp.int32)

    def pair(block):
        return lax.ppermute(block, "tm", [(i, i ^ 1) for i in range(time_devices)])

    def hop(block, skip=0):
        return lax.ppermute(block, "tm", [(i, i + 2) for i in range(skip, time_devices - 2)])

    def swap(block):
        return lax.ppermute(block, "stn", [(0, 1), (1, 0)])

    def laid(block):
        return jnp.moveaxis(block, 0, -2)

    (own,) = cut(voltages, [None], [])
    other = cut(voltages, list(range(pols)), [own, place])
    columns = weight_blocks.shape[1] // CORES
    shard = lax.dynamic_slice_in_dim(weight_blocks, core * columns, columns, 1)
    shards = [shard] + [
        lax.ppermute(shard, "tm", [(i, i ^ apart) for i in range(time_devices)]) for apart in range(2, time_devices, 2)
    ]
    own_back = laid(after(hop(own)))
    own = laid(own)
    other = [laid(after(pair(block))) for block in other]

    def ordered(rows):
        rows = rows.T.reshape(2, 2, 2, -1)
        rows = flipped(rows, core)
        rows = flipped(rows.swapaxes(0, 1), side).swapaxes(0, 1)
        return rows.reshape(8, -1)

    each = weight_blocks.shape[0]
    apart = block_index // each ^ lax.axis_index("tm")
    index = (apart % 2 * (time_devices // 2) + apart // 2) * each + block_index % each
    table = jnp.asarray(dft_tables(samples))
    taps = jnp.broadcast_to(filter_taps[:, None, :], (history + 1, 8, samples))

    parts_of = [(samples // 2, samples // 2), (5 * samples // 8, 3 * samples // 8)]
    chunks = [(pol, sum(sizes[:i]), size) for pol, sizes in enumerate(parts_of) for i, size in enumerate(sizes)]
    other_back = [hop(block) for block in other]
    further = []
    for pol, low, size in chunks:
        gates = [] if further else shards[1:]
        further.append(onward(place, own_back, other_back[pol], pol, low, size, gates))
    shards = jnp.concatenate(shards)
    far = [hop(block, 2) for block in further]
    weights = beam_weights(jnp.concatenate([shards, pair(shards)]), ordered(index), ordered(use_mask), [])
    partial = []
    for pol in range(pols):
        gates = further[: 2 * pol + 2] + [weights] + other_back[1:]
        partial.append(near_filter(place, taps, own, other[pol], own_back, other_back[pol], pol, gates))
    keeps, sents, power = [], [], None

    def power_of(pol, earlier, later=()):
        mine, pairs = keeps[2 * pol : 2 * pol + 2], sents[2 * pol : 2 * pol + 2]
        sources = mine + pairs + [swap(block) for block in mine + pairs]
        return beam_power(place, sources, 2, table, weights, earlier, samples // CORES, later)

    for k, (pol, low, size) in enumerate(chunks):
        gates = {0: [], 1: [*sents[:1], partial[1]], 2: sents[1:2], 3: [power]}[k]
        keep, send = far_filter(place, taps, partial[pol], far[k], low, size, gates)
        keeps.append(keep)
        sents.append(pair(send))
        if k == 2:
            power = power_of(0, None, [keep])
    power = power_of(1, power)
    return jnp.moveaxis(power, 1, 2).reshape(power.shape[0], power.shape[2], -1)


def solution(mesh):
    in_specs = (
        P(("parts", "stn"), None, "tm", None, None),
        P(),
        P("parts", None),
        P("parts", None),
        P("tm", None),
    )
    out_specs = P("stn", "tm", "parts")
    return jax.shard_map(body, mesh=mesh, in_specs=in_specs, out_specs=out_specs, check_vma=False)
```

```python
import functools
import math

import jax
import jax.numpy as jnp
import ml_dtypes
import numpy as np
from jax import lax
from jax.experimental import pallas as pl
from jax.experimental.pallas import tpu as pltpu
from jax.sharding import PartitionSpec as P

SB = 16
G = 16
RADIX = 16
LANES = 128
CORES = 2
VMEM_LIMIT = 63 * 1024 * 1024
F32 = jnp.float32
BF16 = jnp.bfloat16


def cost(microseconds):
    return pl.CostEstimate(flops=0, bytes_accessed=int(microseconds * 3.3e6), transcendentals=0)


def dft_tables(channels):
    per_half = channels // RADIX // CORES
    b = np.arange(RADIX)[None, :, None, None]
    e = np.arange(LANES)[None, None, None, :]
    d = np.arange(CORES * per_half).reshape(CORES, 1, per_half, 1)
    angle = (e * (RADIX * d + b) % channels) * (2.0 * math.pi / channels)
    cosine, sine = np.cos(angle), np.sin(angle)
    real_rows = np.concatenate([cosine, sine], axis=3)
    imag_rows = np.concatenate([-sine, cosine], axis=3)
    table = np.concatenate([real_rows, imag_rows], axis=2) / math.sqrt(channels)
    return table.astype(ml_dtypes.bfloat16)


def turned(value, step, size):
    re, im = value
    step %= size
    if step == 0:
        return re, im
    if 4 * step == size:
        return im, -re
    if 2 * step == size:
        return -re, -im
    if 4 * step == 3 * size:
        return -im, re
    cosine, sine = math.cos(2 * math.pi * step / size), math.sin(2 * math.pi * step / size)
    if 8 * step == size:
        return (re + im) * cosine, (im - re) * cosine
    if 8 * step == 3 * size:
        return (im - re) * sine, -(re + im) * sine
    return re * cosine + im * sine, im * cosine - re * sine


def four_points(values):
    (r0, i0), (r1, i1), (r2, i2), (r3, i3) = values
    sr, si, dr, di = r0 + r2, i0 + i2, r0 - r2, i0 - i2
    tr, ti, er, ei = r1 + r3, i1 + i3, r1 - r3, i1 - i3
    return [(sr + tr, si + ti), (dr + ei, di - er), (sr - tr, si - ti), (dr - ei, di + er)]


def sixteen_points(values):
    inner = [four_points([values[4 * a1 + a0] for a1 in range(4)]) for a0 in range(4)]
    result = [None] * 16
    for b0 in range(4):
        outer = four_points([turned(inner[a0][b0], a0 * b0, 16) for a0 in range(4)])
        for b1 in range(4):
            result[4 * b1 + b0] = outer[b1]
    return result


def after(block, *earlier):
    return pl.pallas_call(
        lambda *refs: None,
        out_shape=jax.ShapeDtypeStruct(block.shape, block.dtype),
        in_specs=[pl.BlockSpec(memory_space=pl.ANY)] * (1 + len(earlier)),
        out_specs=pl.BlockSpec(memory_space=pl.ANY),
        input_output_aliases={0: 0},
        cost_estimate=cost(0),
        name="after",
    )(block, *earlier)


def cut_kernel(mine, voltages, *rest):
    count = len(mine)
    outs, (buffer, loads, stores) = rest[-3 - count : -3], rest[-3:]
    half = buffer.shape[0]
    pieces = loads.shape[0]
    size = half // pieces
    side = lax.rem(lax.axis_index("tm"), 2)
    start = half * (side if mine[0] is None else 1 - side)

    def load(k):
        return pltpu.make_async_copy(
            voltages.at[pl.ds(start + k * size, size)], buffer.at[pl.ds(k * size, size)], loads.at[k]
        )

    def store(k, i):
        block = buffer.at[pl.ds(k * size, size)]
        block = block if mine[i] is None else block.at[:, mine[i]]
        return pltpu.make_async_copy(block, outs[i].at[pl.ds(k * size, size)], stores.at[i, k])

    for k in range(pieces):
        load(k).start()
    for k in range(pieces):
        load(k).wait()
        for i in range(count):
            store(k, i).start()
    for k in range(pieces):
        for i in range(count):
            store(k, i).wait()


def cut(voltages, mine, earlier):
    stations, pols, frames, parts, samples = voltages.shape
    whole = (stations // 2, pols, frames, parts, samples)
    shapes = [whole if pol is None else whole[:1] + whole[2:] for pol in mine]
    pieces = 4
    there = pl.BlockSpec(memory_space=pltpu.HBM)
    return pl.pallas_call(
        functools.partial(cut_kernel, mine),
        out_shape=[jax.ShapeDtypeStruct(shape, BF16) for shape in shapes],
        in_specs=[there] + [pl.BlockSpec(memory_space=pl.ANY)] * len(earlier),
        out_specs=[there] * len(shapes),
        scratch_shapes=[
            pltpu.VMEM(whole, BF16),
            pltpu.SemaphoreType.DMA((pieces,)),
            pltpu.SemaphoreType.DMA((len(mine), pieces)),
        ],
        compiler_params=pltpu.CompilerParams(vmem_limit_bytes=VMEM_LIMIT),
        cost_estimate=cost(2),
        name="cut",
    )(voltages, *earlier)


def weighted(taps, window, count, lanes, part, rows, sums):
    tap_count = taps.shape[0]
    tap_rows = [taps[k, :, lanes][None] for k in range(tap_count)]
    for j, ref, index in window:
        value = ref[index, part, rows, lanes].astype(F32).reshape(SB // 8, 8, LANES)
        for f in range(count):
            k = f - j
            if 0 <= k < tap_count:
                term = tap_rows[k] * value
                sums[f] = term if sums[f] is None else sums[f] + term
    return sums


def over_tiles(stations, samples, step):
    tiles, lane_tiles = stations // SB, samples // LANES

    def body(i, carry):
        lanes = pl.ds(pl.multiple_of(i % lane_tiles * LANES, LANES), LANES)
        rows = pl.ds(pl.multiple_of(i // (2 * lane_tiles) * SB, SB), SB)
        step(lanes, i // lane_tiles % 2, rows)
        return carry

    lax.fori_loop(0, 2 * tiles * lane_tiles, body, 0, unroll=2)


def near_kernel(place, taps, own, other, own_back, other_back, *rest):
    partial = rest[-1]
    frames = own.shape[0]
    count = 2 * frames

    def run(first, second, first_back, second_back):
        window = []
        for start, ref in ((-count, first_back), (frames - count, second_back), (0, first), (frames, second)):
            window += [(start + i, ref, i) for i in range(frames)]

        def step(lanes, part, rows):
            sums = weighted(taps, window, count, lanes, part, rows, [None] * count)
            for f in range(count):
                partial[f, part, rows, lanes] = sums[f].reshape(SB, LANES)

        over_tiles(*own.shape[2:], step)

    @pl.when(place[0] == 0)
    def _():
        run(own, other, own_back, other_back)

    @pl.when(place[0] == 1)
    def _():
        run(other, own, other_back, own_back)


def far_kernel(place, taps, partial, far, *rest):
    keep, send = rest[-2:]
    frames = keep.shape[0]
    count = 2 * frames
    window = [(i + 1 - 2 * count, far, i) for i in range(far.shape[0])]

    def run(first_out, second_out):
        def step(lanes, part, rows):
            sums = [partial[f, part, rows, lanes].reshape(SB // 8, 8, LANES) for f in range(count)]
            sums = weighted(taps, window, count, lanes, part, rows, sums)
            for f in range(count):
                out = first_out if f < frames else second_out
                out[f % frames, part, rows, lanes] = sums[f].reshape(SB, LANES).astype(BF16)

        over_tiles(*keep.shape[2:], step)

    @pl.when(place[0] == 0)
    def _():
        run(keep, send)

    @pl.when(place[0] == 1)
    def _():
        run(send, keep)


def near_filter(place, taps, own, other, own_back, other_back, pol, earlier):
    frames, parts, stations, samples = other.shape
    block = 512
    both = pl.BlockSpec((None, frames, parts, stations, block), lambda i, place: (pol, 0, 0, 0, i))
    one = pl.BlockSpec((frames, parts, stations, block), lambda i, place: (0, 0, 0, i))
    return pl.pallas_call(
        near_kernel,
        out_shape=jax.ShapeDtypeStruct((2 * frames, parts, stations, samples), F32),
        grid_spec=pltpu.PrefetchScalarGridSpec(
            num_scalar_prefetch=1,
            grid=(samples // block,),
            in_specs=[pl.BlockSpec((taps.shape[0], 8, block), lambda i, place: (0, 0, i)), both, one, both, one]
            + [pl.BlockSpec(memory_space=pl.ANY)] * len(earlier),
            out_specs=pl.BlockSpec((2 * frames, parts, stations, block), lambda i, place: (0, 0, 0, i)),
        ),
        compiler_params=pltpu.CompilerParams(vmem_limit_bytes=VMEM_LIMIT),
        cost_estimate=cost(8 * stations / 32),
        name="near",
    )(place, taps, own, other, own_back, other_back, *earlier)


def far_filter(place, taps, partial, far, low, size, earlier):
    count, parts, stations, _ = partial.shape
    frames = count // 2
    block = size // 2

    def spec(depth, start):
        shape = (pl.Element(depth), pl.Element(parts), pl.Element(stations), pl.Element(block))
        return pl.BlockSpec(shape, lambda i, place: (0, 0, 0, pl.multiple_of(start + i * block, LANES)))

    shape = jax.ShapeDtypeStruct((frames, parts, stations, size), BF16)
    return pl.pallas_call(
        far_kernel,
        out_shape=(shape, shape),
        grid_spec=pltpu.PrefetchScalarGridSpec(
            num_scalar_prefetch=1,
            grid=(size // block,),
            in_specs=[
                pl.BlockSpec(
                    (pl.Element(taps.shape[0]), pl.Element(8), pl.Element(block)),
                    lambda i, place: (0, 0, pl.multiple_of(low + i * block, LANES)),
                )
            ]
            + [spec(count, low), spec(far.shape[0], 0)]
            + [pl.BlockSpec(memory_space=pl.ANY)] * len(earlier),
            out_specs=[spec(frames, 0)] * 2,
        ),
        compiler_params=pltpu.CompilerParams(vmem_limit_bytes=VMEM_LIMIT),
        cost_estimate=cost(1),
        name="far",
    )(place, taps, partial, far, *earlier)


def onward_kernel(place, own_back, other_back, *rest):
    far = rest[-1]
    frames = other_back.shape[0]
    own_back = own_back.at[0]

    def run(first, second):
        far[: frames - 1] = first[1:]
        far[frames - 1 :] = second[...]

    @pl.when(place[0] == 0)
    def _():
        run(own_back, other_back)

    @pl.when(place[0] == 1)
    def _():
        run(other_back, own_back)


def onward(place, own_back, other_back, pol, low, size, earlier):
    frames, parts, stations, _ = other_back.shape
    depth = 2 * frames - 1

    def spec(depth, *before):
        shape = tuple(pl.Element(n) for n in (1,) * len(before) + (depth, 1, stations, size))
        return pl.BlockSpec(shape, lambda i, place: before + (0, i, 0, low))

    return pl.pallas_call(
        onward_kernel,
        out_shape=jax.ShapeDtypeStruct((depth, parts, stations, size), BF16),
        grid_spec=pltpu.PrefetchScalarGridSpec(
            num_scalar_prefetch=1,
            grid=(parts,),
            in_specs=[spec(frames, pol), spec(frames)] + [pl.BlockSpec(memory_space=pl.ANY)] * len(earlier),
            out_specs=pl.BlockSpec((depth, 1, stations, size), lambda i, place: (0, i, 0, 0)),
        ),
        compiler_params=pltpu.CompilerParams(vmem_limit_bytes=VMEM_LIMIT),
        cost_estimate=cost(3),
        name="onward",
    )(place, own_back, other_back, *earlier)


def weight_kernel(table, index, mask, *rest):
    out = rest[-1]
    groups, depth, width = out.shape
    beams = width // 2
    half = depth // 2
    rows = lax.broadcasted_iota(jnp.int32, (table.shape[0], beams), 0)
    for q in range(index.shape[0]):
        hit = jnp.where((rows == index[q : q + 1, :]) & (mask[q : q + 1, :] != 0), 1.0, 0.0).astype(BF16)
        picked = lax.dot_general(table[...], hit, (((0,), (0,)), ((), ())), preferred_element_type=F32)
        picked = picked.reshape(groups, 2, SB, beams)
        low = q * SB
        re, im = picked[:, 0], picked[:, 1]
        out[:, low : low + SB, :beams] = re.astype(BF16)
        out[:, low : low + SB, beams:] = im.astype(BF16)
        low += half
        out[:, low : low + SB, :beams] = (-im).astype(BF16)
        out[:, low : low + SB, beams:] = re.astype(BF16)


def beam_weights(table, index, mask, earlier):
    blocks, beams = index.shape
    groups = table.shape[1] // (2 * SB)
    shape = (groups, 2 * blocks * SB, 2 * beams)
    return pl.pallas_call(
        weight_kernel,
        out_shape=jax.ShapeDtypeStruct(shape, BF16),
        in_specs=[pl.BlockSpec(memory_space=pltpu.VMEM)] * 3 + [pl.BlockSpec(memory_space=pl.ANY)] * len(earlier),
        compiler_params=pltpu.CompilerParams(vmem_limit_bytes=VMEM_LIMIT),
        cost_estimate=cost(4),
        name="weights",
    )(table, index, mask, *earlier)


def beam_kernel(source_count, ranges, later_count, has_earlier, place, *refs):
    refs = list(refs)
    inputs = [refs.pop(0) for _ in range(source_count + 2 + has_earlier)]
    refs = refs[later_count:]
    out, mixed, spectra, sems, *held = refs
    inputs[source_count] = inputs[source_count].at[pl.ds(place[1], 1)]
    copies = [pltpu.make_async_copy(ref, to, sems.at[k]) for k, (ref, to) in enumerate(zip(inputs, held))]
    table, weights = held[source_count : source_count + 2]
    step = pl.program_id(0)
    frames, _, stations, _ = held[0].shape
    tiles = stations // SB
    station_count = stations * (source_count // ranges)
    groups = spectra.shape[0]
    beams = weights.shape[2] // 2
    rows_of = table.shape[2] // 2 // groups
    pair = 2
    lane_tiles = beams // LANES
    at_once = groups // pl.num_programs(0)

    @pl.when(step == 0)
    def _():
        for copy in copies:
            copy.start()
        for k in range(0, source_count, ranges):
            for copy in copies[k : k + ranges]:
                copy.wait()
            pieces = []
            for ref in held[k : k + ranges]:
                pieces += [(ref, slice(n, n + LANES)) for n in range(0, ref.shape[3], LANES)]

            def radix(i, carry, pieces=pieces, low=k // ranges * stations):
                f, rows = i // tiles, pl.ds(pl.multiple_of(i % tiles * SB, SB), SB)
                values = [tuple(ref[f, part, rows, lanes].astype(F32) for part in range(2)) for ref, lanes in pieces]
                target = pl.ds(pl.multiple_of(f * station_count + low + i % tiles * SB, SB), SB)
                for b, (re, im) in enumerate(sixteen_points(values)):
                    mixed[b, target, :LANES] = re.astype(BF16)
                    mixed[b, target, LANES:] = im.astype(BF16)
                return carry

            lax.fori_loop(0, frames * tiles, radix, 0, unroll=2)
        copies[source_count].wait()

        def transform(b, carry):
            for start in range(0, frames, pair):
                product = lax.dot_general(
                    table[0, b],
                    mixed[b, start * station_count : (start + pair) * station_count],
                    (((1,), (1,)), ((), ())),
                    preferred_element_type=F32,
                )
                product = product.reshape(2, groups, rows_of, pair * station_count)
                rows = slice(start * rows_of, (start + pair) * rows_of)
                for part in range(2):
                    value = jnp.concatenate(
                        [product[part, :, :, f * station_count : (f + 1) * station_count] for f in range(pair)], axis=1
                    )
                    columns = slice(part * station_count, (part + 1) * station_count)
                    spectra[:, b, rows, columns] = value.astype(BF16)
            return carry

        lax.fori_loop(0, RADIX, transform, 0, unroll=True)
        for copy in copies[source_count + 1 :]:
            copy.wait()

    for k in range(at_once):
        group = step * at_once + k
        rows = spectra[group].reshape(RADIX * frames * rows_of, 2 * station_count)
        beam = jnp.dot(rows, weights[group], preferred_element_type=F32)
        re, im = beam[:, :beams], beam[:, beams:]
        power = re * re + im * im
        if not has_earlier:
            out[k] = power
            continue
        power = power + held[-1][group]
        for b in range(RADIX):
            for f in range(frames):
                at = (b * frames + f) * rows_of
                channels = pl.ds(k * rows_of * RADIX + b, rows_of, stride=RADIX)
                for t in range(lane_tiles):
                    out[channels, t, f, :] = power[at : at + rows_of, t * LANES : (t + 1) * LANES]


def beam_power(place, sources, ranges, table, weights, earlier, channels, later=()):
    frames = sources[0].shape[0]
    groups, depth, width = weights.shape
    beams = width // 2
    station_count = sum(s.shape[2] for s in sources) // ranges
    at_once = 2
    flat = (groups, channels // groups * frames, beams)
    flat_spec = pl.BlockSpec((at_once,) + flat[1:], lambda i, place: (i, 0, 0))
    operands = list(sources) + [table, weights] + ([] if earlier is None else [earlier])
    in_specs = [pl.BlockSpec(memory_space=pltpu.HBM)] * len(operands) + [pl.BlockSpec(memory_space=pl.ANY)] * len(later)
    scratch = [
        pltpu.VMEM((RADIX, frames * station_count, 2 * LANES), BF16),
        pltpu.VMEM((groups, RADIX, frames * channels // groups // RADIX, 2 * station_count), BF16),
        pltpu.SemaphoreType.DMA((len(operands),)),
    ]
    for k, block in enumerate(operands):
        scratch.append(pltpu.VMEM(((1,) if k == len(sources) else block.shape[:1]) + block.shape[1:], block.dtype))
    if earlier is None:
        out_shape = jax.ShapeDtypeStruct(flat, F32)
        out_spec = flat_spec
    else:
        out_shape = jax.ShapeDtypeStruct((channels, beams // LANES, frames, LANES), F32)
        out_spec = pl.BlockSpec((channels // groups * at_once,) + out_shape.shape[1:], lambda i, place: (i, 0, 0, 0))
    return pl.pallas_call(
        functools.partial(beam_kernel, len(sources), ranges, len(later), earlier is not None),
        out_shape=out_shape,
        grid_spec=pltpu.PrefetchScalarGridSpec(
            num_scalar_prefetch=1,
            grid=(groups // at_once,),
            in_specs=in_specs,
            out_specs=out_spec,
            scratch_shapes=scratch,
        ),
        compiler_params=pltpu.CompilerParams(vmem_limit_bytes=VMEM_LIMIT),
        cost_estimate=cost(0),
        name="beams",
    )(place, *operands, *later)


def flipped(rows, bit):
    return jnp.where(bit == 1, rows[::-1], rows)


def body(voltages, filter_taps, use_mask, block_index, weight_blocks):
    stations, pols, frames, parts, samples = voltages.shape
    history = filter_taps.shape[0] - 1
    half = stations // 2
    time_devices = lax.axis_size("tm")
    side = lax.axis_index("tm") % 2
    core = lax.axis_index("stn")
    place = jnp.stack([side, core]).astype(jnp.int32)

    def pair(block):
        return lax.ppermute(block, "tm", [(i, i ^ 1) for i in range(time_devices)])

    def hop(block, skip=0):
        return lax.ppermute(block, "tm", [(i, i + 2) for i in range(skip, time_devices - 2)])

    def swap(block):
        return lax.ppermute(block, "stn", [(0, 1), (1, 0)])

    def laid(block):
        return jnp.moveaxis(block, 0, -2)

    (own,) = cut(voltages, [None], [])
    other = cut(voltages, list(range(pols)), [own, place])
    columns = weight_blocks.shape[1] // CORES
    shard = lax.dynamic_slice_in_dim(weight_blocks, core * columns, columns, 1)
    shards = [shard] + [
        lax.ppermute(shard, "tm", [(i, i ^ apart) for i in range(time_devices)]) for apart in range(2, time_devices, 2)
    ]
    own_back = laid(after(hop(own)))
    own = laid(own)
    other = [laid(after(pair(block))) for block in other]

    def ordered(rows):
        rows = rows.T.reshape(2, 2, 2, -1)
        rows = flipped(rows, core)
        rows = flipped(rows.swapaxes(0, 1), side).swapaxes(0, 1)
        return rows.reshape(8, -1)

    each = weight_blocks.shape[0]
    apart = block_index // each ^ lax.axis_index("tm")
    index = (apart % 2 * (time_devices // 2) + apart // 2) * each + block_index % each
    table = jnp.asarray(dft_tables(samples))
    taps = jnp.broadcast_to(filter_taps[:, None, :], (history + 1, 8, samples))

    parts_of = [(samples // 2, samples // 2), (5 * samples // 8, 3 * samples // 8)]
    chunks = [(pol, sum(sizes[:i]), size) for pol, sizes in enumerate(parts_of) for i, size in enumerate(sizes)]
    other_back = [hop(block) for block in other]
    further = []
    for pol, low, size in chunks:
        gates = [] if further else shards[1:]
        further.append(onward(place, own_back, other_back[pol], pol, low, size, gates))
    shards = jnp.concatenate(shards)
    far = [hop(block, 2) for block in further]
    weights = beam_weights(jnp.concatenate([shards, pair(shards)]), ordered(index), ordered(use_mask), [])
    partial = []
    for pol in range(pols):
        gates = further[: 2 * pol + 2] + [weights] + other_back[1:]
        partial.append(near_filter(place, taps, own, other[pol], own_back, other_back[pol], pol, gates))
    keeps, sents, power = [], [], None

    def power_of(pol, earlier, later=()):
        mine, pairs = keeps[2 * pol : 2 * pol + 2], sents[2 * pol : 2 * pol + 2]
        sources = mine + pairs + [swap(block) for block in mine + pairs]
        return beam_power(place, sources, 2, table, weights, earlier, samples // CORES, later)

    for k, (pol, low, size) in enumerate(chunks):
        gates = {0: [], 1: [*sents[:1], partial[1]], 2: sents[1:2], 3: [power]}[k]
        keep, send = far_filter(place, taps, partial[pol], far[k], low, size, gates)
        keeps.append(keep)
        sents.append(pair(send))
        if k == 2:
            power = power_of(0, None, [keep])
    power = power_of(1, power)
    return jnp.moveaxis(power, 1, 2).reshape(power.shape[0], power.shape[2], -1)


def solution(mesh):
    in_specs = (
        P(("parts", "stn"), None, "tm", None, None),
        P(),
        P("parts", None),
        P("parts", None),
        P("tm", None),
    )
    out_specs = P("stn", "tm", "parts")
    return jax.shard_map(body, mesh=mesh, in_specs=in_specs, out_specs=out_specs, check_vma=False)
```

```python
import functools
import math

import jax
import jax.numpy as jnp
import ml_dtypes
import numpy as np
from jax import lax
from jax.experimental import pallas as pl
from jax.experimental.pallas import tpu as pltpu
from jax.sharding import PartitionSpec as P

SB = 16
G = 16
RADIX = 16
LANES = 128
CORES = 2
VMEM_LIMIT = 63 * 1024 * 1024
F32 = jnp.float32
BF16 = jnp.bfloat16


def cost(microseconds):
    return pl.CostEstimate(flops=0, bytes_accessed=int(microseconds * 3.3e6), transcendentals=0)


def dft_tables(channels):
    per_half = channels // RADIX // CORES
    b = np.arange(RADIX)[None, :, None, None]
    e = np.arange(LANES)[None, None, None, :]
    d = np.arange(CORES * per_half).reshape(CORES, 1, per_half, 1)
    angle = (e * (RADIX * d + b) % channels) * (2.0 * math.pi / channels)
    cosine, sine = np.cos(angle), np.sin(angle)
    real_rows = np.concatenate([cosine, sine], axis=3)
    imag_rows = np.concatenate([-sine, cosine], axis=3)
    table = np.concatenate([real_rows, imag_rows], axis=2) / math.sqrt(channels)
    return table.astype(ml_dtypes.bfloat16)


def turned(value, step, size):
    re, im = value
    step %= size
    if step == 0:
        return re, im
    if 4 * step == size:
        return im, -re
    if 2 * step == size:
        return -re, -im
    if 4 * step == 3 * size:
        return -im, re
    cosine, sine = math.cos(2 * math.pi * step / size), math.sin(2 * math.pi * step / size)
    if 8 * step == size:
        return (re + im) * cosine, (im - re) * cosine
    if 8 * step == 3 * size:
        return (im - re) * sine, -(re + im) * sine
    return re * cosine + im * sine, im * cosine - re * sine


def four_points(values):
    (r0, i0), (r1, i1), (r2, i2), (r3, i3) = values
    sr, si, dr, di = r0 + r2, i0 + i2, r0 - r2, i0 - i2
    tr, ti, er, ei = r1 + r3, i1 + i3, r1 - r3, i1 - i3
    return [(sr + tr, si + ti), (dr + ei, di - er), (sr - tr, si - ti), (dr - ei, di + er)]


def sixteen_points(values):
    inner = [four_points([values[4 * a1 + a0] for a1 in range(4)]) for a0 in range(4)]
    result = [None] * 16
    for b0 in range(4):
        outer = four_points([turned(inner[a0][b0], a0 * b0, 16) for a0 in range(4)])
        for b1 in range(4):
            result[4 * b1 + b0] = outer[b1]
    return result


def after(block, *earlier):
    return pl.pallas_call(
        lambda *refs: None,
        out_shape=jax.ShapeDtypeStruct(block.shape, block.dtype),
        in_specs=[pl.BlockSpec(memory_space=pl.ANY)] * (1 + len(earlier)),
        out_specs=pl.BlockSpec(memory_space=pl.ANY),
        input_output_aliases={0: 0},
        cost_estimate=cost(0),
        name="after",
    )(block, *earlier)


def cut_kernel(mine, voltages, *rest):
    count = len(mine)
    outs, (buffer, loads, stores) = rest[-3 - count : -3], rest[-3:]
    half = buffer.shape[0]
    pieces = loads.shape[0]
    size = half // pieces
    side = lax.rem(lax.axis_index("tm"), 2)
    start = half * (side if mine[0] is None else 1 - side)

    def load(k):
        return pltpu.make_async_copy(
            voltages.at[pl.ds(start + k * size, size)], buffer.at[pl.ds(k * size, size)], loads.at[k]
        )

    def store(k, i):
        block = buffer.at[pl.ds(k * size, size)]
        block = block if mine[i] is None else block.at[:, mine[i]]
        return pltpu.make_async_copy(block, outs[i].at[pl.ds(k * size, size)], stores.at[i, k])

    for k in range(pieces):
        load(k).start()
    for k in range(pieces):
        load(k).wait()
        for i in range(count):
            store(k, i).start()
    for k in range(pieces):
        for i in range(count):
            store(k, i).wait()


def cut(voltages, mine, earlier):
    stations, pols, frames, parts, samples = voltages.shape
    whole = (stations // 2, pols, frames, parts, samples)
    shapes = [whole if pol is None else whole[:1] + whole[2:] for pol in mine]
    pieces = 4
    there = pl.BlockSpec(memory_space=pltpu.HBM)
    return pl.pallas_call(
        functools.partial(cut_kernel, mine),
        out_shape=[jax.ShapeDtypeStruct(shape, BF16) for shape in shapes],
        in_specs=[there] + [pl.BlockSpec(memory_space=pl.ANY)] * len(earlier),
        out_specs=[there] * len(shapes),
        scratch_shapes=[
            pltpu.VMEM(whole, BF16),
            pltpu.SemaphoreType.DMA((pieces,)),
            pltpu.SemaphoreType.DMA((len(mine), pieces)),
        ],
        compiler_params=pltpu.CompilerParams(vmem_limit_bytes=VMEM_LIMIT),
        cost_estimate=cost(2),
        name="cut",
    )(voltages, *earlier)


def weighted(taps, window, count, lanes, part, rows, sums):
    tap_count = taps.shape[0]
    tap_rows = [taps[k, :, lanes][None] for k in range(tap_count)]
    for j, ref, index in window:
        value = ref[index, part, rows, lanes].astype(F32).reshape(SB // 8, 8, LANES)
        for f in range(count):
            k = f - j
            if 0 <= k < tap_count:
                term = tap_rows[k] * value
                sums[f] = term if sums[f] is None else sums[f] + term
    return sums


def over_tiles(stations, samples, step):
    tiles, lane_tiles = stations // SB, samples // LANES

    def body(i, carry):
        lanes = pl.ds(pl.multiple_of(i % lane_tiles * LANES, LANES), LANES)
        rows = pl.ds(pl.multiple_of(i // (2 * lane_tiles) * SB, SB), SB)
        step(lanes, i // lane_tiles % 2, rows)
        return carry

    lax.fori_loop(0, 2 * tiles * lane_tiles, body, 0, unroll=2)


def near_kernel(place, taps, own, other, own_back, other_back, *rest):
    partial = rest[-1]
    frames = own.shape[0]
    count = 2 * frames

    def run(first, second, first_back, second_back):
        window = []
        for start, ref in ((-count, first_back), (frames - count, second_back), (0, first), (frames, second)):
            window += [(start + i, ref, i) for i in range(frames)]

        def step(lanes, part, rows):
            sums = weighted(taps, window, count, lanes, part, rows, [None] * count)
            for f in range(count):
                partial[f, part, rows, lanes] = sums[f].reshape(SB, LANES)

        over_tiles(*own.shape[2:], step)

    @pl.when(place[0] == 0)
    def _():
        run(own, other, own_back, other_back)

    @pl.when(place[0] == 1)
    def _():
        run(other, own, other_back, own_back)


def far_kernel(place, taps, partial, far, *rest):
    keep, send = rest[-2:]
    frames = keep.shape[0]
    count = 2 * frames
    window = [(i + 1 - 2 * count, far, i) for i in range(far.shape[0])]

    def run(first_out, second_out):
        def step(lanes, part, rows):
            sums = [partial[f, part, rows, lanes].reshape(SB // 8, 8, LANES) for f in range(count)]
            sums = weighted(taps, window, count, lanes, part, rows, sums)
            for f in range(count):
                out = first_out if f < frames else second_out
                out[f % frames, part, rows, lanes] = sums[f].reshape(SB, LANES).astype(BF16)

        over_tiles(*keep.shape[2:], step)

    @pl.when(place[0] == 0)
    def _():
        run(keep, send)

    @pl.when(place[0] == 1)
    def _():
        run(send, keep)


def near_filter(place, taps, own, other, own_back, other_back, pol, earlier):
    frames, parts, stations, samples = other.shape
    block = 512
    both = pl.BlockSpec((None, frames, parts, stations, block), lambda i, place: (pol, 0, 0, 0, i))
    one = pl.BlockSpec((frames, parts, stations, block), lambda i, place: (0, 0, 0, i))
    return pl.pallas_call(
        near_kernel,
        out_shape=jax.ShapeDtypeStruct((2 * frames, parts, stations, samples), F32),
        grid_spec=pltpu.PrefetchScalarGridSpec(
            num_scalar_prefetch=1,
            grid=(samples // block,),
            in_specs=[pl.BlockSpec((taps.shape[0], 8, block), lambda i, place: (0, 0, i)), both, one, both, one]
            + [pl.BlockSpec(memory_space=pl.ANY)] * len(earlier),
            out_specs=pl.BlockSpec((2 * frames, parts, stations, block), lambda i, place: (0, 0, 0, i)),
        ),
        compiler_params=pltpu.CompilerParams(vmem_limit_bytes=VMEM_LIMIT),
        cost_estimate=cost(8 * stations / 32),
        name="near",
    )(place, taps, own, other, own_back, other_back, *earlier)


def far_filter(place, taps, partial, far, low, size, earlier):
    count, parts, stations, _ = partial.shape
    frames = count // 2
    block = size // 2

    def spec(depth, start):
        shape = (pl.Element(depth), pl.Element(parts), pl.Element(stations), pl.Element(block))
        return pl.BlockSpec(shape, lambda i, place: (0, 0, 0, pl.multiple_of(start + i * block, LANES)))

    shape = jax.ShapeDtypeStruct((frames, parts, stations, size), BF16)
    return pl.pallas_call(
        far_kernel,
        out_shape=(shape, shape),
        grid_spec=pltpu.PrefetchScalarGridSpec(
            num_scalar_prefetch=1,
            grid=(size // block,),
            in_specs=[
                pl.BlockSpec(
                    (pl.Element(taps.shape[0]), pl.Element(8), pl.Element(block)),
                    lambda i, place: (0, 0, pl.multiple_of(low + i * block, LANES)),
                )
            ]
            + [spec(count, low), spec(far.shape[0], 0)]
            + [pl.BlockSpec(memory_space=pl.ANY)] * len(earlier),
            out_specs=[spec(frames, 0)] * 2,
        ),
        compiler_params=pltpu.CompilerParams(vmem_limit_bytes=VMEM_LIMIT),
        cost_estimate=cost(1),
        name="far",
    )(place, taps, partial, far, *earlier)


def onward_kernel(place, own_back, other_back, *rest):
    far = rest[-1]
    frames = other_back.shape[0]
    own_back = own_back.at[0]

    def run(first, second):
        far[: frames - 1] = first[1:]
        far[frames - 1 :] = second[...]

    @pl.when(place[0] == 0)
    def _():
        run(own_back, other_back)

    @pl.when(place[0] == 1)
    def _():
        run(other_back, own_back)


def onward(place, own_back, other_back, pol, low, size, earlier):
    frames, parts, stations, _ = other_back.shape
    depth = 2 * frames - 1

    def spec(depth, *before):
        shape = tuple(pl.Element(n) for n in (1,) * len(before) + (depth, 1, stations, size))
        return pl.BlockSpec(shape, lambda i, place: before + (0, i, 0, low))

    return pl.pallas_call(
        onward_kernel,
        out_shape=jax.ShapeDtypeStruct((depth, parts, stations, size), BF16),
        grid_spec=pltpu.PrefetchScalarGridSpec(
            num_scalar_prefetch=1,
            grid=(parts,),
            in_specs=[spec(frames, pol), spec(frames)] + [pl.BlockSpec(memory_space=pl.ANY)] * len(earlier),
            out_specs=pl.BlockSpec((depth, 1, stations, size), lambda i, place: (0, i, 0, 0)),
        ),
        compiler_params=pltpu.CompilerParams(vmem_limit_bytes=VMEM_LIMIT),
        cost_estimate=cost(3),
        name="onward",
    )(place, own_back, other_back, *earlier)


def weight_kernel(table, index, mask, *rest):
    out = rest[-1]
    groups, depth, width = out.shape
    beams = width // 2
    half = depth // 2
    rows = lax.broadcasted_iota(jnp.int32, (table.shape[0], beams), 0)
    for q in range(index.shape[0]):
        hit = jnp.where((rows == index[q : q + 1, :]) & (mask[q : q + 1, :] != 0), 1.0, 0.0).astype(BF16)
        picked = lax.dot_general(table[...], hit, (((0,), (0,)), ((), ())), preferred_element_type=F32)
        picked = picked.reshape(groups, 2, SB, beams)
        low = q * SB
        re, im = picked[:, 0], picked[:, 1]
        out[:, low : low + SB, :beams] = re.astype(BF16)
        out[:, low : low + SB, beams:] = im.astype(BF16)
        low += half
        out[:, low : low + SB, :beams] = (-im).astype(BF16)
        out[:, low : low + SB, beams:] = re.astype(BF16)


def beam_weights(table, index, mask, earlier):
    blocks, beams = index.shape
    groups = table.shape[1] // (2 * SB)
    shape = (groups, 2 * blocks * SB, 2 * beams)
    return pl.pallas_call(
        weight_kernel,
        out_shape=jax.ShapeDtypeStruct(shape, BF16),
        in_specs=[pl.BlockSpec(memory_space=pltpu.VMEM)] * 3 + [pl.BlockSpec(memory_space=pl.ANY)] * len(earlier),
        compiler_params=pltpu.CompilerParams(vmem_limit_bytes=VMEM_LIMIT),
        cost_estimate=cost(4),
        name="weights",
    )(table, index, mask, *earlier)


def beam_kernel(source_count, ranges, later_count, has_earlier, place, *refs):
    refs = list(refs)
    inputs = [refs.pop(0) for _ in range(source_count + 2 + has_earlier)]
    refs = refs[later_count:]
    out, mixed, spectra, sems, *held = refs
    inputs[source_count] = inputs[source_count].at[pl.ds(place[1], 1)]
    copies = [pltpu.make_async_copy(ref, to, sems.at[k]) for k, (ref, to) in enumerate(zip(inputs, held))]
    table, weights = held[source_count : source_count + 2]
    step = pl.program_id(0)
    frames, _, stations, _ = held[0].shape
    tiles = stations // SB
    station_count = stations * (source_count // ranges)
    groups = spectra.shape[0]
    beams = weights.shape[2] // 2
    rows_of = table.shape[2] // 2 // groups
    pair = 2
    lane_tiles = beams // LANES
    at_once = groups // pl.num_programs(0)

    @pl.when(step == 0)
    def _():
        for copy in copies:
            copy.start()
        for k in range(0, source_count, ranges):
            for copy in copies[k : k + ranges]:
                copy.wait()
            pieces = []
            for ref in held[k : k + ranges]:
                pieces += [(ref, slice(n, n + LANES)) for n in range(0, ref.shape[3], LANES)]

            def radix(i, carry, pieces=pieces, low=k // ranges * stations):
                f, rows = i // tiles, pl.ds(pl.multiple_of(i % tiles * SB, SB), SB)
                values = [tuple(ref[f, part, rows, lanes].astype(F32) for part in range(2)) for ref, lanes in pieces]
                target = pl.ds(pl.multiple_of(f * station_count + low + i % tiles * SB, SB), SB)
                for b, (re, im) in enumerate(sixteen_points(values)):
                    mixed[b, target, :LANES] = re.astype(BF16)
                    mixed[b, target, LANES:] = im.astype(BF16)
                return carry

            lax.fori_loop(0, frames * tiles, radix, 0, unroll=2)
        copies[source_count].wait()

        def transform(b, carry):
            for start in range(0, frames, pair):
                product = lax.dot_general(
                    table[0, b],
                    mixed[b, start * station_count : (start + pair) * station_count],
                    (((1,), (1,)), ((), ())),
                    preferred_element_type=F32,
                )
                product = product.reshape(2, groups, rows_of, pair * station_count)
                rows = slice(start * rows_of, (start + pair) * rows_of)
                for part in range(2):
                    value = jnp.concatenate(
                        [product[part, :, :, f * station_count : (f + 1) * station_count] for f in range(pair)], axis=1
                    )
                    columns = slice(part * station_count, (part + 1) * station_count)
                    spectra[:, b, rows, columns] = value.astype(BF16)
            return carry

        lax.fori_loop(0, RADIX, transform, 0, unroll=True)
        for copy in copies[source_count + 1 :]:
            copy.wait()

    for k in range(at_once):
        group = step * at_once + k
        rows = spectra[group].reshape(RADIX * frames * rows_of, 2 * station_count)
        beam = jnp.dot(rows, weights[group], preferred_element_type=F32)
        re, im = beam[:, :beams], beam[:, beams:]
        power = re * re + im * im
        if not has_earlier:
            out[k] = power
            continue
        power = power + held[-1][group]
        for b in range(RADIX):
            for f in range(frames):
                at = (b * frames + f) * rows_of
                channels = pl.ds(k * rows_of * RADIX + b, rows_of, stride=RADIX)
                for t in range(lane_tiles):
                    out[channels, t, f, :] = power[at : at + rows_of, t * LANES : (t + 1) * LANES]


def beam_power(place, sources, ranges, table, weights, earlier, channels, later=()):
    frames = sources[0].shape[0]
    groups, depth, width = weights.shape
    beams = width // 2
    station_count = sum(s.shape[2] for s in sources) // ranges
    at_once = 2
    flat = (groups, channels // groups * frames, beams)
    flat_spec = pl.BlockSpec((at_once,) + flat[1:], lambda i, place: (i, 0, 0))
    operands = list(sources) + [table, weights] + ([] if earlier is None else [earlier])
    in_specs = [pl.BlockSpec(memory_space=pltpu.HBM)] * len(operands) + [pl.BlockSpec(memory_space=pl.ANY)] * len(later)
    scratch = [
        pltpu.VMEM((RADIX, frames * station_count, 2 * LANES), BF16),
        pltpu.VMEM((groups, RADIX, frames * channels // groups // RADIX, 2 * station_count), BF16),
        pltpu.SemaphoreType.DMA((len(operands),)),
    ]
    for k, block in enumerate(operands):
        scratch.append(pltpu.VMEM(((1,) if k == len(sources) else block.shape[:1]) + block.shape[1:], block.dtype))
    if earlier is None:
        out_shape = jax.ShapeDtypeStruct(flat, F32)
        out_spec = flat_spec
    else:
        out_shape = jax.ShapeDtypeStruct((channels, beams // LANES, frames, LANES), F32)
        out_spec = pl.BlockSpec((channels // groups * at_once,) + out_shape.shape[1:], lambda i, place: (i, 0, 0, 0))
    return pl.pallas_call(
        functools.partial(beam_kernel, len(sources), ranges, len(later), earlier is not None),
        out_shape=out_shape,
        grid_spec=pltpu.PrefetchScalarGridSpec(
            num_scalar_prefetch=1,
            grid=(groups // at_once,),
            in_specs=in_specs,
            out_specs=out_spec,
            scratch_shapes=scratch,
        ),
        compiler_params=pltpu.CompilerParams(vmem_limit_bytes=VMEM_LIMIT),
        cost_estimate=cost(0),
        name="beams",
    )(place, *operands, *later)


def flipped(rows, bit):
    return jnp.where(bit == 1, rows[::-1], rows)


def body(voltages, filter_taps, use_mask, block_index, weight_blocks):
    stations, pols, frames, parts, samples = voltages.shape
    history = filter_taps.shape[0] - 1
    half = stations // 2
    time_devices = lax.axis_size("tm")
    side = lax.axis_index("tm") % 2
    core = lax.axis_index("stn")
    place = jnp.stack([side, core]).astype(jnp.int32)

    def pair(block):
        return lax.ppermute(block, "tm", [(i, i ^ 1) for i in range(time_devices)])

    def hop(block, skip=0):
        return lax.ppermute(block, "tm", [(i, i + 2) for i in range(skip, time_devices - 2)])

    def swap(block):
        return lax.ppermute(block, "stn", [(0, 1), (1, 0)])

    def laid(block):
        return jnp.moveaxis(block, 0, -2)

    (own,) = cut(voltages, [None], [])
    other = cut(voltages, list(range(pols)), [own, place])
    columns = weight_blocks.shape[1] // CORES
    shard = lax.dynamic_slice_in_dim(weight_blocks, core * columns, columns, 1)
    shards = [shard] + [
        lax.ppermute(shard, "tm", [(i, i ^ apart) for i in range(time_devices)]) for apart in range(2, time_devices, 2)
    ]
    own_back = laid(after(hop(own)))
    own = laid(own)
    other = [laid(after(pair(block))) for block in other]

    def ordered(rows):
        rows = rows.T.reshape(2, 2, 2, -1)
        rows = flipped(rows, core)
        rows = flipped(rows.swapaxes(0, 1), side).swapaxes(0, 1)
        return rows.reshape(8, -1)

    each = weight_blocks.shape[0]
    apart = block_index // each ^ lax.axis_index("tm")
    index = (apart % 2 * (time_devices // 2) + apart // 2) * each + block_index % each
    table = jnp.asarray(dft_tables(samples))
    taps = jnp.broadcast_to(filter_taps[:, None, :], (history + 1, 8, samples))

    large, small = 5 * samples // 8, 3 * samples // 8
    chunks = [(0, 0, large), (1, 0, large), (0, large, small), (1, large, small)]
    other_back = [hop(block) for block in other]
    further = []
    for pol, low, size in chunks:
        gates = shards[1:] if len(further) == 1 else further[-1:]
        further.append(onward(place, own_back, other_back[pol], pol, low, size, gates))
    shards = jnp.concatenate(shards)
    far = [hop(block, 2) for block in further]
    weights = beam_weights(jnp.concatenate([shards, pair(shards)]), ordered(index), ordered(use_mask), [])
    partial = []
    for pol in range(pols):
        gates = further[: 2 * pol + 2] + [weights]
        partial.append(near_filter(place, taps, own, other[pol], own_back, other_back[pol], pol, gates))
    keeps, sents, power = [], [], None

    def power_of(pol, earlier, later=()):
        mine, pairs = keeps[pol::2], sents[pol::2]
        sources = mine + pairs + [swap(block) for block in mine + pairs]
        return beam_power(place, sources, 2, table, weights, earlier, samples // CORES, later)

    for k, (pol, low, size) in enumerate(chunks):
        gates = {0: [], 1: [*sents[:1], partial[1]], 2: keeps[1:2], 3: [*keeps[2:3], *sents[1:2]]}[k]
        keep, send = far_filter(place, taps, partial[pol], far[k], low, size, gates)
        keeps.append(keep)
        sents.append(pair(send))
    power = power_of(0, None, keeps[-1:])
    sents[-1] = after(sents[-1], power)
    power = power_of(1, power)
    return jnp.moveaxis(power, 1, 2).reshape(power.shape[0], power.shape[2], -1)


def solution(mesh):
    in_specs = (
        P(("parts", "stn"), None, "tm", None, None),
        P(),
        P("parts", None),
        P("parts", None),
        P("tm", None),
    )
    out_specs = P("stn", "tm", "parts")
    return jax.shard_map(body, mesh=mesh, in_specs=in_specs, out_specs=out_specs, check_vma=False)
```

```python
import functools
import math

import jax
import jax.numpy as jnp
import ml_dtypes
import numpy as np
from jax import lax
from jax.experimental import pallas as pl
from jax.experimental.pallas import tpu as pltpu
from jax.sharding import PartitionSpec as P

SB = 16
G = 16
RADIX = 16
LANES = 128
CORES = 2
VMEM_LIMIT = 63 * 1024 * 1024
F32 = jnp.float32
BF16 = jnp.bfloat16


def cost(microseconds):
    return pl.CostEstimate(flops=0, bytes_accessed=int(microseconds * 3.3e6), transcendentals=0)


def dft_tables(channels):
    per_half = channels // RADIX // CORES
    b = np.arange(RADIX)[None, :, None, None]
    e = np.arange(LANES)[None, None, None, :]
    d = np.arange(CORES * per_half).reshape(CORES, 1, per_half, 1)
    angle = (e * (RADIX * d + b) % channels) * (2.0 * math.pi / channels)
    cosine, sine = np.cos(angle), np.sin(angle)
    real_rows = np.concatenate([cosine, sine], axis=3)
    imag_rows = np.concatenate([-sine, cosine], axis=3)
    table = np.concatenate([real_rows, imag_rows], axis=2) / math.sqrt(channels)
    return table.astype(ml_dtypes.bfloat16)


def turned(value, step, size):
    re, im = value
    step %= size
    if step == 0:
        return re, im
    if 4 * step == size:
        return im, -re
    if 2 * step == size:
        return -re, -im
    if 4 * step == 3 * size:
        return -im, re
    cosine, sine = math.cos(2 * math.pi * step / size), math.sin(2 * math.pi * step / size)
    if 8 * step == size:
        return (re + im) * cosine, (im - re) * cosine
    if 8 * step == 3 * size:
        return (im - re) * sine, -(re + im) * sine
    return re * cosine + im * sine, im * cosine - re * sine


def four_points(values):
    (r0, i0), (r1, i1), (r2, i2), (r3, i3) = values
    sr, si, dr, di = r0 + r2, i0 + i2, r0 - r2, i0 - i2
    tr, ti, er, ei = r1 + r3, i1 + i3, r1 - r3, i1 - i3
    return [(sr + tr, si + ti), (dr + ei, di - er), (sr - tr, si - ti), (dr - ei, di + er)]


def sixteen_points(values):
    inner = [four_points([values[4 * a1 + a0] for a1 in range(4)]) for a0 in range(4)]
    result = [None] * 16
    for b0 in range(4):
        outer = four_points([turned(inner[a0][b0], a0 * b0, 16) for a0 in range(4)])
        for b1 in range(4):
            result[4 * b1 + b0] = outer[b1]
    return result


def after(block, *earlier):
    return pl.pallas_call(
        lambda *refs: None,
        out_shape=jax.ShapeDtypeStruct(block.shape, block.dtype),
        in_specs=[pl.BlockSpec(memory_space=pl.ANY)] * (1 + len(earlier)),
        out_specs=pl.BlockSpec(memory_space=pl.ANY),
        input_output_aliases={0: 0},
        cost_estimate=cost(0),
        name="after",
    )(block, *earlier)


def cut_kernel(mine, voltages, *rest):
    count = len(mine)
    outs, (buffer, loads, stores) = rest[-3 - count : -3], rest[-3:]
    half = buffer.shape[0]
    pieces = loads.shape[0]
    size = half // pieces
    side = lax.rem(lax.axis_index("tm"), 2)
    start = half * (side if mine[0] is None else 1 - side)

    def load(k):
        return pltpu.make_async_copy(
            voltages.at[pl.ds(start + k * size, size)], buffer.at[pl.ds(k * size, size)], loads.at[k]
        )

    def store(k, i):
        block = buffer.at[pl.ds(k * size, size)]
        block = block if mine[i] is None else block.at[:, mine[i]]
        return pltpu.make_async_copy(block, outs[i].at[pl.ds(k * size, size)], stores.at[i, k])

    for k in range(pieces):
        load(k).start()
    for k in range(pieces):
        load(k).wait()
        for i in range(count):
            store(k, i).start()
    for k in range(pieces):
        for i in range(count):
            store(k, i).wait()


def cut(voltages, mine, earlier):
    stations, pols, frames, parts, samples = voltages.shape
    whole = (stations // 2, pols, frames, parts, samples)
    shapes = [whole if pol is None else whole[:1] + whole[2:] for pol in mine]
    pieces = 4
    there = pl.BlockSpec(memory_space=pltpu.HBM)
    return pl.pallas_call(
        functools.partial(cut_kernel, mine),
        out_shape=[jax.ShapeDtypeStruct(shape, BF16) for shape in shapes],
        in_specs=[there] + [pl.BlockSpec(memory_space=pl.ANY)] * len(earlier),
        out_specs=[there] * len(shapes),
        scratch_shapes=[
            pltpu.VMEM(whole, BF16),
            pltpu.SemaphoreType.DMA((pieces,)),
            pltpu.SemaphoreType.DMA((len(mine), pieces)),
        ],
        compiler_params=pltpu.CompilerParams(vmem_limit_bytes=VMEM_LIMIT),
        cost_estimate=cost(2),
        name="cut",
    )(voltages, *earlier)


def weighted(taps, window, count, lanes, part, rows, sums):
    tap_count = taps.shape[0]
    tap_rows = [taps[k, :, lanes][None] for k in range(tap_count)]
    for j, ref, index in window:
        value = ref[index, part, rows, lanes].astype(F32).reshape(SB // 8, 8, LANES)
        for f in range(count):
            k = f - j
            if 0 <= k < tap_count:
                term = tap_rows[k] * value
                sums[f] = term if sums[f] is None else sums[f] + term
    return sums


def over_tiles(stations, samples, step):
    tiles, lane_tiles = stations // SB, samples // LANES

    def body(i, carry):
        lanes = pl.ds(pl.multiple_of(i % lane_tiles * LANES, LANES), LANES)
        rows = pl.ds(pl.multiple_of(i // (2 * lane_tiles) * SB, SB), SB)
        step(lanes, i // lane_tiles % 2, rows)
        return carry

    lax.fori_loop(0, 2 * tiles * lane_tiles, body, 0, unroll=2)


def near_kernel(place, taps, own, other, own_back, other_back, *rest):
    partial = rest[-1]
    frames = own.shape[0]
    count = 2 * frames

    def run(first, second, first_back, second_back):
        window = []
        for start, ref in ((-count, first_back), (frames - count, second_back), (0, first), (frames, second)):
            window += [(start + i, ref, i) for i in range(frames)]

        def step(lanes, part, rows):
            sums = weighted(taps, window, count, lanes, part, rows, [None] * count)
            for f in range(count):
                partial[f, part, rows, lanes] = sums[f].reshape(SB, LANES)

        over_tiles(*own.shape[2:], step)

    @pl.when(place[0] == 0)
    def _():
        run(own, other, own_back, other_back)

    @pl.when(place[0] == 1)
    def _():
        run(other, own, other_back, own_back)


def far_kernel(place, taps, partial, far, *rest):
    keep, send = rest[-2:]
    frames = keep.shape[0]
    count = 2 * frames
    window = [(i + 1 - 2 * count, far, i) for i in range(far.shape[0])]

    def run(first_out, second_out):
        def step(lanes, part, rows):
            sums = [partial[f, part, rows, lanes].reshape(SB // 8, 8, LANES) for f in range(count)]
            sums = weighted(taps, window, count, lanes, part, rows, sums)
            for f in range(count):
                out = first_out if f < frames else second_out
                out[f % frames, part, rows, lanes] = sums[f].reshape(SB, LANES).astype(BF16)

        over_tiles(*keep.shape[2:], step)

    @pl.when(place[0] == 0)
    def _():
        run(keep, send)

    @pl.when(place[0] == 1)
    def _():
        run(send, keep)


def near_filter(place, taps, own, other, own_back, other_back, pol, earlier):
    frames, parts, stations, samples = other.shape
    block = 512
    both = pl.BlockSpec((None, frames, parts, stations, block), lambda i, place: (pol, 0, 0, 0, i))
    one = pl.BlockSpec((frames, parts, stations, block), lambda i, place: (0, 0, 0, i))
    return pl.pallas_call(
        near_kernel,
        out_shape=jax.ShapeDtypeStruct((2 * frames, parts, stations, samples), F32),
        grid_spec=pltpu.PrefetchScalarGridSpec(
            num_scalar_prefetch=1,
            grid=(samples // block,),
            in_specs=[pl.BlockSpec((taps.shape[0], 8, block), lambda i, place: (0, 0, i)), both, one, both, one]
            + [pl.BlockSpec(memory_space=pl.ANY)] * len(earlier),
            out_specs=pl.BlockSpec((2 * frames, parts, stations, block), lambda i, place: (0, 0, 0, i)),
        ),
        compiler_params=pltpu.CompilerParams(vmem_limit_bytes=VMEM_LIMIT),
        cost_estimate=cost(8 * stations / 32),
        name="near",
    )(place, taps, own, other, own_back, other_back, *earlier)


def far_filter(place, taps, partial, far, low, size, earlier):
    count, parts, stations, _ = partial.shape
    frames = count // 2
    block = next(size // n for n in (2, 3, 1) if size // n % LANES == 0)

    def spec(depth, start):
        shape = (pl.Element(depth), pl.Element(parts), pl.Element(stations), pl.Element(block))
        return pl.BlockSpec(shape, lambda i, place: (0, 0, 0, pl.multiple_of(start + i * block, LANES)))

    shape = jax.ShapeDtypeStruct((frames, parts, stations, size), BF16)
    return pl.pallas_call(
        far_kernel,
        out_shape=(shape, shape),
        grid_spec=pltpu.PrefetchScalarGridSpec(
            num_scalar_prefetch=1,
            grid=(size // block,),
            in_specs=[
                pl.BlockSpec(
                    (pl.Element(taps.shape[0]), pl.Element(8), pl.Element(block)),
                    lambda i, place: (0, 0, pl.multiple_of(low + i * block, LANES)),
                )
            ]
            + [spec(count, low), spec(far.shape[0], 0)]
            + [pl.BlockSpec(memory_space=pl.ANY)] * len(earlier),
            out_specs=[spec(frames, 0)] * 2,
        ),
        compiler_params=pltpu.CompilerParams(vmem_limit_bytes=VMEM_LIMIT),
        cost_estimate=cost(1),
        name="far",
    )(place, taps, partial, far, *earlier)


def onward_kernel(place, own_back, other_back, *rest):
    far = rest[-1]
    frames = other_back.shape[0]
    own_back = own_back.at[0]

    def run(first, second):
        far[: frames - 1] = first[1:]
        far[frames - 1 :] = second[...]

    @pl.when(place[0] == 0)
    def _():
        run(own_back, other_back)

    @pl.when(place[0] == 1)
    def _():
        run(other_back, own_back)


def onward(place, own_back, other_back, pol, low, size, earlier):
    frames, parts, stations, _ = other_back.shape
    depth = 2 * frames - 1

    def spec(depth, *before):
        shape = tuple(pl.Element(n) for n in (1,) * len(before) + (depth, 1, stations, size))
        return pl.BlockSpec(shape, lambda i, place: before + (0, i, 0, low))

    return pl.pallas_call(
        onward_kernel,
        out_shape=jax.ShapeDtypeStruct((depth, parts, stations, size), BF16),
        grid_spec=pltpu.PrefetchScalarGridSpec(
            num_scalar_prefetch=1,
            grid=(parts,),
            in_specs=[spec(frames, pol), spec(frames)] + [pl.BlockSpec(memory_space=pl.ANY)] * len(earlier),
            out_specs=pl.BlockSpec((depth, 1, stations, size), lambda i, place: (0, i, 0, 0)),
        ),
        compiler_params=pltpu.CompilerParams(vmem_limit_bytes=VMEM_LIMIT),
        cost_estimate=cost(3),
        name="onward",
    )(place, own_back, other_back, *earlier)


def weight_kernel(table, index, mask, *rest):
    out = rest[-1]
    groups, depth, width = out.shape
    beams = width // 2
    half = depth // 2
    rows = lax.broadcasted_iota(jnp.int32, (table.shape[0], beams), 0)
    for q in range(index.shape[0]):
        hit = jnp.where((rows == index[q : q + 1, :]) & (mask[q : q + 1, :] != 0), 1.0, 0.0).astype(BF16)
        picked = lax.dot_general(table[...], hit, (((0,), (0,)), ((), ())), preferred_element_type=F32)
        picked = picked.reshape(groups, 2, SB, beams)
        low = q * SB
        re, im = picked[:, 0], picked[:, 1]
        out[:, low : low + SB, :beams] = re.astype(BF16)
        out[:, low : low + SB, beams:] = im.astype(BF16)
        low += half
        out[:, low : low + SB, :beams] = (-im).astype(BF16)
        out[:, low : low + SB, beams:] = re.astype(BF16)


def beam_weights(table, index, mask, earlier):
    blocks, beams = index.shape
    groups = table.shape[1] // (2 * SB)
    shape = (groups, 2 * blocks * SB, 2 * beams)
    return pl.pallas_call(
        weight_kernel,
        out_shape=jax.ShapeDtypeStruct(shape, BF16),
        in_specs=[pl.BlockSpec(memory_space=pltpu.VMEM)] * 3 + [pl.BlockSpec(memory_space=pl.ANY)] * len(earlier),
        compiler_params=pltpu.CompilerParams(vmem_limit_bytes=VMEM_LIMIT),
        cost_estimate=cost(4),
        name="weights",
    )(table, index, mask, *earlier)


def beam_kernel(source_count, ranges, later_count, has_earlier, place, *refs):
    refs = list(refs)
    inputs = [refs.pop(0) for _ in range(source_count + 2 + has_earlier)]
    refs = refs[later_count:]
    out, mixed, spectra, sems, *held = refs
    inputs[source_count] = inputs[source_count].at[pl.ds(place[1], 1)]
    copies = [pltpu.make_async_copy(ref, to, sems.at[k]) for k, (ref, to) in enumerate(zip(inputs, held))]
    table, weights = held[source_count : source_count + 2]
    step = pl.program_id(0)
    frames, _, stations, _ = held[0].shape
    tiles = stations // SB
    station_count = stations * (source_count // ranges)
    groups = spectra.shape[0]
    beams = weights.shape[2] // 2
    rows_of = table.shape[2] // 2 // groups
    pair = 2
    lane_tiles = beams // LANES
    at_once = groups // pl.num_programs(0)

    @pl.when(step == 0)
    def _():
        for copy in copies:
            copy.start()
        for k in range(0, source_count, ranges):
            for copy in copies[k : k + ranges]:
                copy.wait()
            pieces = []
            for ref in held[k : k + ranges]:
                pieces += [(ref, slice(n, n + LANES)) for n in range(0, ref.shape[3], LANES)]

            def radix(i, carry, pieces=pieces, low=k // ranges * stations):
                f, rows = i // tiles, pl.ds(pl.multiple_of(i % tiles * SB, SB), SB)
                values = [tuple(ref[f, part, rows, lanes].astype(F32) for part in range(2)) for ref, lanes in pieces]
                target = pl.ds(pl.multiple_of(f * station_count + low + i % tiles * SB, SB), SB)
                for b, (re, im) in enumerate(sixteen_points(values)):
                    mixed[b, target, :LANES] = re.astype(BF16)
                    mixed[b, target, LANES:] = im.astype(BF16)
                return carry

            lax.fori_loop(0, frames * tiles, radix, 0, unroll=4 if has_earlier else 2)
        copies[source_count].wait()

        def transform(b, carry):
            for start in range(0, frames, pair):
                product = lax.dot_general(
                    table[0, b],
                    mixed[b, start * station_count : (start + pair) * station_count],
                    (((1,), (1,)), ((), ())),
                    preferred_element_type=F32,
                )
                product = product.reshape(2, groups, rows_of, pair * station_count)
                rows = slice(start * rows_of, (start + pair) * rows_of)
                for part in range(2):
                    value = jnp.concatenate(
                        [product[part, :, :, f * station_count : (f + 1) * station_count] for f in range(pair)], axis=1
                    )
                    columns = slice(part * station_count, (part + 1) * station_count)
                    spectra[:, b, rows, columns] = value.astype(BF16)
            return carry

        lax.fori_loop(0, RADIX, transform, 0, unroll=True)
        for copy in copies[source_count + 1 :]:
            copy.wait()

    for k in range(at_once):
        group = step * at_once + k
        rows = spectra[group].reshape(RADIX * frames * rows_of, 2 * station_count)
        beam = jnp.dot(rows, weights[group], preferred_element_type=F32)
        re, im = beam[:, :beams], beam[:, beams:]
        power = re * re + im * im
        if not has_earlier:
            out[k] = power
            continue
        power = power + held[-1][group]
        for b in range(RADIX):
            for f in range(frames):
                at = (b * frames + f) * rows_of
                channels = pl.ds(k * rows_of * RADIX + b, rows_of, stride=RADIX)
                for t in range(lane_tiles):
                    out[channels, t, f, :] = power[at : at + rows_of, t * LANES : (t + 1) * LANES]


def beam_power(place, sources, ranges, table, weights, earlier, channels, later=()):
    frames = sources[0].shape[0]
    groups, depth, width = weights.shape
    beams = width // 2
    station_count = sum(s.shape[2] for s in sources) // ranges
    at_once = 4 if earlier is None else 2
    flat = (groups, channels // groups * frames, beams)
    flat_spec = pl.BlockSpec((at_once,) + flat[1:], lambda i, place: (i, 0, 0))
    operands = list(sources) + [table, weights] + ([] if earlier is None else [earlier])
    in_specs = [pl.BlockSpec(memory_space=pltpu.HBM)] * len(operands) + [pl.BlockSpec(memory_space=pl.ANY)] * len(later)
    scratch = [
        pltpu.VMEM((RADIX, frames * station_count, 2 * LANES), BF16),
        pltpu.VMEM((groups, RADIX, frames * channels // groups // RADIX, 2 * station_count), BF16),
        pltpu.SemaphoreType.DMA((len(operands),)),
    ]
    for k, block in enumerate(operands):
        scratch.append(pltpu.VMEM(((1,) if k == len(sources) else block.shape[:1]) + block.shape[1:], block.dtype))
    if earlier is None:
        out_shape = jax.ShapeDtypeStruct(flat, F32)
        out_spec = flat_spec
    else:
        out_shape = jax.ShapeDtypeStruct((channels, beams // LANES, frames, LANES), F32)
        out_spec = pl.BlockSpec((channels // groups * at_once,) + out_shape.shape[1:], lambda i, place: (i, 0, 0, 0))
    return pl.pallas_call(
        functools.partial(beam_kernel, len(sources), ranges, len(later), earlier is not None),
        out_shape=out_shape,
        grid_spec=pltpu.PrefetchScalarGridSpec(
            num_scalar_prefetch=1,
            grid=(groups // at_once,),
            in_specs=in_specs,
            out_specs=out_spec,
            scratch_shapes=scratch,
        ),
        compiler_params=pltpu.CompilerParams(vmem_limit_bytes=VMEM_LIMIT),
        cost_estimate=cost(0),
        name="beams",
    )(place, *operands, *later)


def flipped(rows, bit):
    return jnp.where(bit == 1, rows[::-1], rows)


def body(voltages, filter_taps, use_mask, block_index, weight_blocks):
    stations, pols, frames, parts, samples = voltages.shape
    history = filter_taps.shape[0] - 1
    half = stations // 2
    time_devices = lax.axis_size("tm")
    side = lax.axis_index("tm") % 2
    core = lax.axis_index("stn")
    place = jnp.stack([side, core]).astype(jnp.int32)

    def pair(block):
        return lax.ppermute(block, "tm", [(i, i ^ 1) for i in range(time_devices)])

    def hop(block, skip=0):
        return lax.ppermute(block, "tm", [(i, i + 2) for i in range(skip, time_devices - 2)])

    def swap(block):
        return lax.ppermute(block, "stn", [(0, 1), (1, 0)])

    def laid(block):
        return jnp.moveaxis(block, 0, -2)

    (own,) = cut(voltages, [None], [])
    other = cut(voltages, list(range(pols)), [own, place])
    columns = weight_blocks.shape[1] // CORES
    shard = lax.dynamic_slice_in_dim(weight_blocks, core * columns, columns, 1)
    shards = [shard] + [
        lax.ppermute(shard, "tm", [(i, i ^ apart) for i in range(time_devices)]) for apart in range(2, time_devices, 2)
    ]
    own_back = laid(after(hop(own)))
    own = laid(own)
    other = [laid(after(pair(block))) for block in other]

    def ordered(rows):
        rows = rows.T.reshape(2, 2, 2, -1)
        rows = flipped(rows, core)
        rows = flipped(rows.swapaxes(0, 1), side).swapaxes(0, 1)
        return rows.reshape(8, -1)

    each = weight_blocks.shape[0]
    apart = block_index // each ^ lax.axis_index("tm")
    index = (apart % 2 * (time_devices // 2) + apart // 2) * each + block_index % each
    table = jnp.asarray(dft_tables(samples))
    taps = jnp.broadcast_to(filter_taps[:, None, :], (history + 1, 8, samples))

    parts_of = [(samples // 2, samples // 2), (9 * samples // 16, 7 * samples // 16)]
    chunks = [(pol, sum(sizes[:i]), size) for pol, sizes in enumerate(parts_of) for i, size in enumerate(sizes)]
    other_back = [hop(block) for block in other]
    further = []
    for pol, low, size in chunks:
        gates = [] if further else shards[1:]
        further.append(onward(place, own_back, other_back[pol], pol, low, size, gates))
    shards = jnp.concatenate(shards)
    far = [hop(block, 2) for block in further]
    weights = beam_weights(jnp.concatenate([shards, pair(shards)]), ordered(index), ordered(use_mask), [])
    partial = []
    for pol in range(pols):
        gates = further[: 2 * pol + 2] + [weights] + other_back[1:]
        partial.append(near_filter(place, taps, own, other[pol], own_back, other_back[pol], pol, gates))
    keeps, sents, power = [], [], None

    def power_of(pol, earlier, later=()):
        mine, pairs = keeps[2 * pol : 2 * pol + 2], sents[2 * pol : 2 * pol + 2]
        sources = mine + pairs + [swap(block) for block in mine + pairs]
        return beam_power(place, sources, 2, table, weights, earlier, samples // CORES, later)

    for k, (pol, low, size) in enumerate(chunks):
        gates = {0: [], 1: [*sents[:1], partial[1]], 2: sents[1:2], 3: [power]}[k]
        keep, send = far_filter(place, taps, partial[pol], far[k], low, size, gates)
        keeps.append(keep)
        sents.append(pair(send))
        if k == 2:
            power = power_of(0, None, [keep])
    power = power_of(1, power)
    return jnp.moveaxis(power, 1, 2).reshape(power.shape[0], power.shape[2], -1)


def solution(mesh):
    in_specs = (
        P(("parts", "stn"), None, "tm", None, None),
        P(),
        P("parts", None),
        P("parts", None),
        P("tm", None),
    )
    out_specs = P("stn", "tm", "parts")
    return jax.shard_map(body, mesh=mesh, in_specs=in_specs, out_specs=out_specs, check_vma=False)
```

```python
import functools
import math

import jax
import jax.numpy as jnp
import ml_dtypes
import numpy as np
from jax import lax
from jax.experimental import pallas as pl
from jax.experimental.pallas import tpu as pltpu
from jax.sharding import PartitionSpec as P

SB = 16
G = 16
RADIX = 16
LANES = 128
CORES = 2
VMEM_LIMIT = 63 * 1024 * 1024
F32 = jnp.float32
BF16 = jnp.bfloat16


def cost(microseconds):
    return pl.CostEstimate(flops=0, bytes_accessed=int(microseconds * 3.3e6), transcendentals=0)


def dft_tables(channels):
    per_half = channels // RADIX // CORES
    b = np.arange(RADIX)[None, :, None, None]
    e = np.arange(LANES)[None, None, None, :]
    d = np.arange(CORES * per_half).reshape(CORES, 1, per_half, 1)
    angle = (e * (RADIX * d + b) % channels) * (2.0 * math.pi / channels)
    cosine, sine = np.cos(angle), np.sin(angle)
    real_rows = np.concatenate([cosine, sine], axis=3)
    imag_rows = np.concatenate([-sine, cosine], axis=3)
    table = np.concatenate([real_rows, imag_rows], axis=2) / math.sqrt(channels)
    return table.astype(ml_dtypes.bfloat16)


def turned(value, step, size):
    re, im = value
    step %= size
    if step == 0:
        return re, im
    if 4 * step == size:
        return im, -re
    if 2 * step == size:
        return -re, -im
    if 4 * step == 3 * size:
        return -im, re
    cosine, sine = math.cos(2 * math.pi * step / size), math.sin(2 * math.pi * step / size)
    if 8 * step == size:
        return (re + im) * cosine, (im - re) * cosine
    if 8 * step == 3 * size:
        return (im - re) * sine, -(re + im) * sine
    return re * cosine + im * sine, im * cosine - re * sine


def four_points(values):
    (r0, i0), (r1, i1), (r2, i2), (r3, i3) = values
    sr, si, dr, di = r0 + r2, i0 + i2, r0 - r2, i0 - i2
    tr, ti, er, ei = r1 + r3, i1 + i3, r1 - r3, i1 - i3
    return [(sr + tr, si + ti), (dr + ei, di - er), (sr - tr, si - ti), (dr - ei, di + er)]


def sixteen_points(values):
    inner = [four_points([values[4 * a1 + a0] for a1 in range(4)]) for a0 in range(4)]
    result = [None] * 16
    for b0 in range(4):
        outer = four_points([turned(inner[a0][b0], a0 * b0, 16) for a0 in range(4)])
        for b1 in range(4):
            result[4 * b1 + b0] = outer[b1]
    return result


def after(block, *earlier):
    return pl.pallas_call(
        lambda *refs: None,
        out_shape=jax.ShapeDtypeStruct(block.shape, block.dtype),
        in_specs=[pl.BlockSpec(memory_space=pl.ANY)] * (1 + len(earlier)),
        out_specs=pl.BlockSpec(memory_space=pl.ANY),
        input_output_aliases={0: 0},
        cost_estimate=cost(0),
        name="after",
    )(block, *earlier)


def cut_kernel(mine, voltages, *rest):
    count = len(mine)
    outs, (buffer, loads, stores) = rest[-3 - count : -3], rest[-3:]
    half = buffer.shape[0]
    pieces = loads.shape[0]
    size = half // pieces
    side = lax.rem(lax.axis_index("tm"), 2)
    start = half * (side if mine[0] is None else 1 - side)

    def load(k):
        return pltpu.make_async_copy(
            voltages.at[pl.ds(start + k * size, size)], buffer.at[pl.ds(k * size, size)], loads.at[k]
        )

    def store(k, i):
        block = buffer.at[pl.ds(k * size, size)]
        block = block if mine[i] is None else block.at[:, mine[i]]
        return pltpu.make_async_copy(block, outs[i].at[pl.ds(k * size, size)], stores.at[i, k])

    for k in range(pieces):
        load(k).start()
    for k in range(pieces):
        load(k).wait()
        for i in range(count):
            store(k, i).start()
    for k in range(pieces):
        for i in range(count):
            store(k, i).wait()


def cut(voltages, mine, earlier):
    stations, pols, frames, parts, samples = voltages.shape
    whole = (stations // 2, pols, frames, parts, samples)
    shapes = [whole if pol is None else whole[:1] + whole[2:] for pol in mine]
    pieces = 4
    there = pl.BlockSpec(memory_space=pltpu.HBM)
    return pl.pallas_call(
        functools.partial(cut_kernel, mine),
        out_shape=[jax.ShapeDtypeStruct(shape, BF16) for shape in shapes],
        in_specs=[there] + [pl.BlockSpec(memory_space=pl.ANY)] * len(earlier),
        out_specs=[there] * len(shapes),
        scratch_shapes=[
            pltpu.VMEM(whole, BF16),
            pltpu.SemaphoreType.DMA((pieces,)),
            pltpu.SemaphoreType.DMA((len(mine), pieces)),
        ],
        compiler_params=pltpu.CompilerParams(vmem_limit_bytes=VMEM_LIMIT),
        cost_estimate=cost(2),
        name="cut",
    )(voltages, *earlier)


def weighted(taps, first_tap, window, count, lanes, part, rows, sums):
    tap_count = taps.shape[0]
    tap_rows = [taps[k, :, lanes][None] for k in range(tap_count)]
    for j, ref, index in window:
        value = ref[index, part, rows, lanes].astype(F32).reshape(SB // 8, 8, LANES)
        for f in range(count):
            k = f - j - first_tap
            if 0 <= k < tap_count:
                term = tap_rows[k] * value
                sums[f] = term if sums[f] is None else sums[f] + term
    return sums


def over_tiles(stations, samples, step):
    tiles, lane_tiles = stations // SB, samples // LANES

    def body(i, carry):
        lanes = pl.ds(pl.multiple_of(i % lane_tiles * LANES, LANES), LANES)
        rows = pl.ds(pl.multiple_of(i // (2 * lane_tiles) * SB, SB), SB)
        step(lanes, i // lane_tiles % 2, rows)
        return carry

    lax.fori_loop(0, 2 * tiles * lane_tiles, body, 0, unroll=2)


def near_kernel(place, taps, own, other, own_back, other_back, *rest):
    partial = rest[-1]
    frames = own.shape[0]
    count = 2 * frames

    def run(first, second, first_back, second_back):
        window = []
        for start, ref in ((-count, first_back), (frames - count, second_back), (0, first), (frames, second)):
            window += [(start + i, ref, i) for i in range(frames)]

        def step(lanes, part, rows):
            sums = weighted(taps, 0, window, count, lanes, part, rows, [None] * count)
            for f in range(count):
                partial[f, part, rows, lanes] = sums[f].reshape(SB, LANES)

        over_tiles(*own.shape[2:], step)

    @pl.when(place[0] == 0)
    def _():
        run(own, other, own_back, other_back)

    @pl.when(place[0] == 1)
    def _():
        run(other, own, other_back, own_back)


def far_kernel(place, taps, partial, far, *rest):
    keep, send = rest[-2:]
    frames = keep.shape[0]
    count = 2 * frames
    window = [(i + 1 - 2 * count, far, i) for i in range(far.shape[0])]

    def run(first_out, second_out):
        def step(lanes, part, rows):
            sums = [partial[f, part, rows, lanes].reshape(SB // 8, 8, LANES) for f in range(count)]
            sums = weighted(taps, count, window, count, lanes, part, rows, sums)
            for f in range(count):
                out = first_out if f < frames else second_out
                out[f % frames, part, rows, lanes] = sums[f].reshape(SB, LANES).astype(BF16)

        over_tiles(*keep.shape[2:], step)

    @pl.when(place[0] == 0)
    def _():
        run(keep, send)

    @pl.when(place[0] == 1)
    def _():
        run(send, keep)


def near_filter(place, taps, own, other, own_back, other_back, pol, earlier):
    frames, parts, stations, samples = other.shape
    block = 512
    both = pl.BlockSpec((None, frames, parts, stations, block), lambda i, place: (pol, 0, 0, 0, i))
    one = pl.BlockSpec((frames, parts, stations, block), lambda i, place: (0, 0, 0, i))
    return pl.pallas_call(
        near_kernel,
        out_shape=jax.ShapeDtypeStruct((2 * frames, parts, stations, samples), F32),
        grid_spec=pltpu.PrefetchScalarGridSpec(
            num_scalar_prefetch=1,
            grid=(samples // block,),
            in_specs=[pl.BlockSpec((taps.shape[0], 8, block), lambda i, place: (0, 0, i)), both, one, both, one]
            + [pl.BlockSpec(memory_space=pl.ANY)] * len(earlier),
            out_specs=pl.BlockSpec((2 * frames, parts, stations, block), lambda i, place: (0, 0, 0, i)),
        ),
        compiler_params=pltpu.CompilerParams(vmem_limit_bytes=VMEM_LIMIT),
        cost_estimate=cost(8 * stations / 32),
        name="near",
    )(place, taps, own, other, own_back, other_back, *earlier)


def far_filter(place, taps, partial, far, low, size, earlier):
    count, parts, stations, _ = partial.shape
    frames = count // 2
    block = next(size // n for n in (2, 3, 1) if size // n % LANES == 0)

    def spec(depth, start):
        shape = (pl.Element(depth), pl.Element(parts), pl.Element(stations), pl.Element(block))
        return pl.BlockSpec(shape, lambda i, place: (0, 0, 0, pl.multiple_of(start + i * block, LANES)))

    shape = jax.ShapeDtypeStruct((frames, parts, stations, size), BF16)
    return pl.pallas_call(
        far_kernel,
        out_shape=(shape, shape),
        grid_spec=pltpu.PrefetchScalarGridSpec(
            num_scalar_prefetch=1,
            grid=(size // block,),
            in_specs=[
                pl.BlockSpec(
                    (pl.Element(taps.shape[0] - count), pl.Element(8), pl.Element(block)),
                    lambda i, place: (count, 0, pl.multiple_of(low + i * block, LANES)),
                )
            ]
            + [spec(count, low), spec(far.shape[0], 0)]
            + [pl.BlockSpec(memory_space=pl.ANY)] * len(earlier),
            out_specs=[spec(frames, 0)] * 2,
        ),
        compiler_params=pltpu.CompilerParams(vmem_limit_bytes=VMEM_LIMIT),
        cost_estimate=cost(1),
        name="far",
    )(place, taps, partial, far, *earlier)


def onward_kernel(place, own_back, other_back, *rest):
    far = rest[-1]
    frames = other_back.shape[0]
    own_back = own_back.at[0]

    def run(first, second):
        far[: frames - 1] = first[1:]
        far[frames - 1 :] = second[...]

    @pl.when(place[0] == 0)
    def _():
        run(own_back, other_back)

    @pl.when(place[0] == 1)
    def _():
        run(other_back, own_back)


def onward(place, own_back, other_back, pol, low, size, earlier):
    frames, parts, stations, _ = other_back.shape
    depth = 2 * frames - 1

    def spec(depth, *before):
        shape = tuple(pl.Element(n) for n in (1,) * len(before) + (depth, 1, stations, size))
        return pl.BlockSpec(shape, lambda i, place: before + (0, i, 0, low))

    return pl.pallas_call(
        onward_kernel,
        out_shape=jax.ShapeDtypeStruct((depth, parts, stations, size), BF16),
        grid_spec=pltpu.PrefetchScalarGridSpec(
            num_scalar_prefetch=1,
            grid=(parts,),
            in_specs=[spec(frames, pol), spec(frames)] + [pl.BlockSpec(memory_space=pl.ANY)] * len(earlier),
            out_specs=pl.BlockSpec((depth, 1, stations, size), lambda i, place: (0, i, 0, 0)),
        ),
        compiler_params=pltpu.CompilerParams(vmem_limit_bytes=VMEM_LIMIT),
        cost_estimate=cost(3),
        name="onward",
    )(place, own_back, other_back, *earlier)


def weight_kernel(table, index, mask, *rest):
    out = rest[-1]
    groups, depth, width = out.shape
    beams = width // 2
    half = depth // 2
    rows = lax.broadcasted_iota(jnp.int32, (table.shape[0], beams), 0)
    for q in range(index.shape[0]):
        hit = jnp.where((rows == index[q : q + 1, :]) & (mask[q : q + 1, :] != 0), 1.0, 0.0).astype(BF16)
        picked = lax.dot_general(table[...], hit, (((0,), (0,)), ((), ())), preferred_element_type=F32)
        picked = picked.reshape(groups, 2, SB, beams)
        low = q * SB
        re, im = picked[:, 0], picked[:, 1]
        out[:, low : low + SB, :beams] = re.astype(BF16)
        out[:, low : low + SB, beams:] = im.astype(BF16)
        low += half
        out[:, low : low + SB, :beams] = (-im).astype(BF16)
        out[:, low : low + SB, beams:] = re.astype(BF16)


def beam_weights(table, index, mask, earlier):
    blocks, beams = index.shape
    groups = table.shape[1] // (2 * SB)
    shape = (groups, 2 * blocks * SB, 2 * beams)
    return pl.pallas_call(
        weight_kernel,
        out_shape=jax.ShapeDtypeStruct(shape, BF16),
        in_specs=[pl.BlockSpec(memory_space=pltpu.VMEM)] * 3 + [pl.BlockSpec(memory_space=pl.ANY)] * len(earlier),
        compiler_params=pltpu.CompilerParams(vmem_limit_bytes=VMEM_LIMIT),
        cost_estimate=cost(4),
        name="weights",
    )(table, index, mask, *earlier)


def beam_kernel(source_count, ranges, later_count, has_earlier, place, *refs):
    refs = list(refs)
    inputs = [refs.pop(0) for _ in range(source_count + 2 + has_earlier)]
    refs = refs[later_count:]
    out, mixed, spectra, sems, *held = refs
    inputs[source_count] = inputs[source_count].at[pl.ds(place[1], 1)]
    copies = [pltpu.make_async_copy(ref, to, sems.at[k]) for k, (ref, to) in enumerate(zip(inputs, held))]
    table, weights = held[source_count : source_count + 2]
    step = pl.program_id(0)
    frames, _, stations, _ = held[0].shape
    tiles = stations // SB
    station_count = stations * (source_count // ranges)
    groups = spectra.shape[0]
    beams = weights.shape[2] // 2
    rows_of = table.shape[2] // 2 // groups
    pair = 2
    lane_tiles = beams // LANES
    at_once = groups // pl.num_programs(0)

    @pl.when(step == 0)
    def _():
        for copy in copies:
            copy.start()
        for k in range(0, source_count, ranges):
            for copy in copies[k : k + ranges]:
                copy.wait()
            pieces = []
            for ref in held[k : k + ranges]:
                pieces += [(ref, slice(n, n + LANES)) for n in range(0, ref.shape[3], LANES)]

            def radix(i, carry, pieces=pieces, low=k // ranges * stations):
                f, rows = i // tiles, pl.ds(pl.multiple_of(i % tiles * SB, SB), SB)
                values = [tuple(ref[f, part, rows, lanes].astype(F32) for part in range(2)) for ref, lanes in pieces]
                target = pl.ds(pl.multiple_of(f * station_count + low + i % tiles * SB, SB), SB)
                for b, (re, im) in enumerate(sixteen_points(values)):
                    mixed[b, target, :LANES] = re.astype(BF16)
                    mixed[b, target, LANES:] = im.astype(BF16)
                return carry

            lax.fori_loop(0, frames * tiles, radix, 0, unroll=2)
        copies[source_count].wait()

        def transform(b, carry):
            for start in range(0, frames, pair):
                product = lax.dot_general(
                    table[0, b],
                    mixed[b, start * station_count : (start + pair) * station_count],
                    (((1,), (1,)), ((), ())),
                    preferred_element_type=F32,
                )
                product = product.reshape(2, groups, rows_of, pair * station_count)
                rows = slice(start * rows_of, (start + pair) * rows_of)
                for part in range(2):
                    value = jnp.concatenate(
                        [product[part, :, :, f * station_count : (f + 1) * station_count] for f in range(pair)], axis=1
                    )
                    columns = slice(part * station_count, (part + 1) * station_count)
                    spectra[:, b, rows, columns] = value.astype(BF16)
            return carry

        lax.fori_loop(0, RADIX, transform, 0, unroll=True)
        for copy in copies[source_count + 1 :]:
            copy.wait()

    for k in range(at_once):
        group = step * at_once + k
        rows = spectra[group].reshape(RADIX * frames * rows_of, 2 * station_count)
        beam = jnp.dot(rows, weights[group], preferred_element_type=F32)
        re, im = beam[:, :beams], beam[:, beams:]
        power = re * re + im * im
        if not has_earlier:
            out[k] = power
            continue
        power = power + held[-1][group]
        for b in range(RADIX):
            for f in range(frames):
                at = (b * frames + f) * rows_of
                channels = pl.ds(k * rows_of * RADIX + b, rows_of, stride=RADIX)
                for t in range(lane_tiles):
                    out[channels, t, f, :] = power[at : at + rows_of, t * LANES : (t + 1) * LANES]


def beam_power(place, sources, ranges, table, weights, earlier, channels, later=()):
    frames = sources[0].shape[0]
    groups, depth, width = weights.shape
    beams = width // 2
    station_count = sum(s.shape[2] for s in sources) // ranges
    at_once = 4
    flat = (groups, channels // groups * frames, beams)
    flat_spec = pl.BlockSpec((at_once,) + flat[1:], lambda i, place: (i, 0, 0))
    operands = list(sources) + [table, weights] + ([] if earlier is None else [earlier])
    in_specs = [pl.BlockSpec(memory_space=pltpu.HBM)] * len(operands) + [pl.BlockSpec(memory_space=pl.ANY)] * len(later)
    scratch = [
        pltpu.VMEM((RADIX, frames * station_count, 2 * LANES), BF16),
        pltpu.VMEM((groups, RADIX, frames * channels // groups // RADIX, 2 * station_count), BF16),
        pltpu.SemaphoreType.DMA((len(operands),)),
    ]
    for k, block in enumerate(operands):
        scratch.append(pltpu.VMEM(((1,) if k == len(sources) else block.shape[:1]) + block.shape[1:], block.dtype))
    if earlier is None:
        out_shape = jax.ShapeDtypeStruct(flat, F32)
        out_spec = flat_spec
    else:
        out_shape = jax.ShapeDtypeStruct((channels, beams // LANES, frames, LANES), F32)
        out_spec = pl.BlockSpec((channels // groups * at_once,) + out_shape.shape[1:], lambda i, place: (i, 0, 0, 0))
    return pl.pallas_call(
        functools.partial(beam_kernel, len(sources), ranges, len(later), earlier is not None),
        out_shape=out_shape,
        grid_spec=pltpu.PrefetchScalarGridSpec(
            num_scalar_prefetch=1,
            grid=(groups // at_once,),
            in_specs=in_specs,
            out_specs=out_spec,
            scratch_shapes=scratch,
        ),
        compiler_params=pltpu.CompilerParams(vmem_limit_bytes=VMEM_LIMIT),
        cost_estimate=cost(0),
        name="beams",
    )(place, *operands, *later)


def flipped(rows, bit):
    return jnp.where(bit == 1, rows[::-1], rows)


def body(voltages, filter_taps, use_mask, block_index, weight_blocks):
    stations, pols, frames, parts, samples = voltages.shape
    history = filter_taps.shape[0] - 1
    half = stations // 2
    time_devices = lax.axis_size("tm")
    side = lax.axis_index("tm") % 2
    core = lax.axis_index("stn")
    place = jnp.stack([side, core]).astype(jnp.int32)

    def pair(block):
        return lax.ppermute(block, "tm", [(i, i ^ 1) for i in range(time_devices)])

    def hop(block, skip=0):
        return lax.ppermute(block, "tm", [(i, i + 2) for i in range(skip, time_devices - 2)])

    def swap(block):
        return lax.ppermute(block, "stn", [(0, 1), (1, 0)])

    def laid(block):
        return jnp.moveaxis(block, 0, -2)

    (own,) = cut(voltages, [None], [])
    other = cut(voltages, list(range(pols)), [own, place])
    columns = weight_blocks.shape[1] // CORES
    shard = lax.dynamic_slice_in_dim(weight_blocks, core * columns, columns, 1)
    shards = [shard] + [
        lax.ppermute(shard, "tm", [(i, i ^ apart) for i in range(time_devices)]) for apart in range(2, time_devices, 2)
    ]
    own_back = laid(after(hop(own)))
    own = laid(own)
    other = [laid(after(pair(block))) for block in other]

    def ordered(rows):
        rows = rows.T.reshape(2, 2, 2, -1)
        rows = flipped(rows, core)
        rows = flipped(rows.swapaxes(0, 1), side).swapaxes(0, 1)
        return rows.reshape(8, -1)

    each = weight_blocks.shape[0]
    apart = block_index // each ^ lax.axis_index("tm")
    index = (apart % 2 * (time_devices // 2) + apart // 2) * each + block_index % each
    table = jnp.asarray(dft_tables(samples))
    taps = jnp.broadcast_to(filter_taps[:, None, :], (history + 1, 8, samples))

    parts_of = [(samples // 2, samples // 2), (9 * samples // 16, 7 * samples // 16)]
    chunks = [(pol, sum(sizes[:i]), size) for pol, sizes in enumerate(parts_of) for i, size in enumerate(sizes)]
    other_back = [hop(block) for block in other]
    further = []
    for pol, low, size in chunks:
        gates = [] if further else shards[1:]
        further.append(onward(place, own_back, other_back[pol], pol, low, size, gates))
    shards = jnp.concatenate(shards)
    far = [hop(block, 2) for block in further]
    weights = beam_weights(jnp.concatenate([shards, pair(shards)]), ordered(index), ordered(use_mask), [])
    partial = []
    for pol in range(pols):
        gates = further[: 2 * pol + 2] + [weights] + other_back[1:]
        partial.append(near_filter(place, taps, own, other[pol], own_back, other_back[pol], pol, gates))
    keeps, sents, power = [], [], None

    def power_of(pol, earlier, later=()):
        mine, pairs = keeps[2 * pol : 2 * pol + 2], sents[2 * pol : 2 * pol + 2]
        sources = mine + pairs + [swap(block) for block in mine + pairs]
        return beam_power(place, sources, 2, table, weights, earlier, samples // CORES, later)

    for k, (pol, low, size) in enumerate(chunks):
        gates = {0: [], 1: [*sents[:1], partial[1]], 2: sents[1:2], 3: [power]}[k]
        keep, send = far_filter(place, taps, partial[pol], far[k], low, size, gates)
        keeps.append(keep)
        sents.append(pair(send))
        if k == 2:
            power = power_of(0, None, [keep])
    power = power_of(1, power)
    return jnp.moveaxis(power, 1, 2).reshape(power.shape[0], power.shape[2], -1)


def solution(mesh):
    in_specs = (
        P(("parts", "stn"), None, "tm", None, None),
        P(),
        P("parts", None),
        P("parts", None),
        P("tm", None),
    )
    out_specs = P("stn", "tm", "parts")
    return jax.shard_map(body, mesh=mesh, in_specs=in_specs, out_specs=out_specs, check_vma=False)
```

```python
import functools
import math

import jax
import jax.numpy as jnp
import ml_dtypes
import numpy as np
from jax import lax
from jax.experimental import pallas as pl
from jax.experimental.pallas import tpu as pltpu
from jax.sharding import PartitionSpec as P

SB = 16
G = 16
RADIX = 16
LANES = 128
CORES = 2
VMEM_LIMIT = 63 * 1024 * 1024
F32 = jnp.float32
BF16 = jnp.bfloat16


def cost(microseconds):
    return pl.CostEstimate(flops=0, bytes_accessed=int(microseconds * 3.3e6), transcendentals=0)


def dft_tables(channels):
    per_half = channels // RADIX // CORES
    b = np.arange(RADIX)[None, :, None, None]
    e = np.arange(LANES)[None, None, None, :]
    d = np.arange(CORES * per_half).reshape(CORES, 1, per_half, 1)
    angle = (e * (RADIX * d + b) % channels) * (2.0 * math.pi / channels)
    cosine, sine = np.cos(angle), np.sin(angle)
    real_rows = np.concatenate([cosine, sine], axis=3)
    imag_rows = np.concatenate([-sine, cosine], axis=3)
    table = np.concatenate([real_rows, imag_rows], axis=2) / math.sqrt(channels)
    return table.astype(ml_dtypes.bfloat16)


def turned(value, step, size):
    re, im = value
    step %= size
    if step == 0:
        return re, im
    if 4 * step == size:
        return im, -re
    if 2 * step == size:
        return -re, -im
    if 4 * step == 3 * size:
        return -im, re
    cosine, sine = math.cos(2 * math.pi * step / size), math.sin(2 * math.pi * step / size)
    if 8 * step == size:
        return (re + im) * cosine, (im - re) * cosine
    if 8 * step == 3 * size:
        return (im - re) * sine, -(re + im) * sine
    return re * cosine + im * sine, im * cosine - re * sine


def four_points(values):
    (r0, i0), (r1, i1), (r2, i2), (r3, i3) = values
    sr, si, dr, di = r0 + r2, i0 + i2, r0 - r2, i0 - i2
    tr, ti, er, ei = r1 + r3, i1 + i3, r1 - r3, i1 - i3
    return [(sr + tr, si + ti), (dr + ei, di - er), (sr - tr, si - ti), (dr - ei, di + er)]


def sixteen_points(values):
    inner = [four_points([values[4 * a1 + a0] for a1 in range(4)]) for a0 in range(4)]
    result = [None] * 16
    for b0 in range(4):
        outer = four_points([turned(inner[a0][b0], a0 * b0, 16) for a0 in range(4)])
        for b1 in range(4):
            result[4 * b1 + b0] = outer[b1]
    return result


def after(block, *earlier):
    return pl.pallas_call(
        lambda *refs: None,
        out_shape=jax.ShapeDtypeStruct(block.shape, block.dtype),
        in_specs=[pl.BlockSpec(memory_space=pl.ANY)] * (1 + len(earlier)),
        out_specs=pl.BlockSpec(memory_space=pl.ANY),
        input_output_aliases={0: 0},
        cost_estimate=cost(0),
        name="after",
    )(block, *earlier)


def cut_kernel(mine, voltages, *rest):
    count = len(mine)
    outs, (buffer, loads, stores) = rest[-3 - count : -3], rest[-3:]
    half = buffer.shape[0]
    pieces = loads.shape[0]
    size = half // pieces
    side = lax.rem(lax.axis_index("tm"), 2)
    start = half * (side if mine[0] is None else 1 - side)

    def load(k):
        return pltpu.make_async_copy(
            voltages.at[pl.ds(start + k * size, size)], buffer.at[pl.ds(k * size, size)], loads.at[k]
        )

    def store(k, i):
        block = buffer.at[pl.ds(k * size, size)]
        block = block if mine[i] is None else block.at[:, mine[i]]
        return pltpu.make_async_copy(block, outs[i].at[pl.ds(k * size, size)], stores.at[i, k])

    for k in range(pieces):
        load(k).start()
    for k in range(pieces):
        load(k).wait()
        for i in range(count):
            store(k, i).start()
    for k in range(pieces):
        for i in range(count):
            store(k, i).wait()


def cut(voltages, mine, earlier):
    stations, pols, frames, parts, samples = voltages.shape
    whole = (stations // 2, pols, frames, parts, samples)
    shapes = [whole if pol is None else whole[:1] + whole[2:] for pol in mine]
    pieces = 4
    there = pl.BlockSpec(memory_space=pltpu.HBM)
    return pl.pallas_call(
        functools.partial(cut_kernel, mine),
        out_shape=[jax.ShapeDtypeStruct(shape, BF16) for shape in shapes],
        in_specs=[there] + [pl.BlockSpec(memory_space=pl.ANY)] * len(earlier),
        out_specs=[there] * len(shapes),
        scratch_shapes=[
            pltpu.VMEM(whole, BF16),
            pltpu.SemaphoreType.DMA((pieces,)),
            pltpu.SemaphoreType.DMA((len(mine), pieces)),
        ],
        compiler_params=pltpu.CompilerParams(vmem_limit_bytes=VMEM_LIMIT),
        cost_estimate=cost(2),
        name="cut",
    )(voltages, *earlier)


def weighted(taps, first_tap, window, count, lanes, part, rows, sums):
    tap_count = taps.shape[0]
    tap_rows = [taps[k, :, lanes][None] for k in range(tap_count)]
    for j, ref, index in window:
        value = ref[index, part, rows, lanes].astype(F32).reshape(SB // 8, 8, LANES)
        for f in range(count):
            k = f - j - first_tap
            if 0 <= k < tap_count:
                term = tap_rows[k] * value
                sums[f] = term if sums[f] is None else sums[f] + term
    return sums


def over_tiles(stations, samples, step):
    tiles, lane_tiles = stations // SB, samples // LANES

    def body(i, carry):
        lanes = pl.ds(pl.multiple_of(i % lane_tiles * LANES, LANES), LANES)
        rows = pl.ds(pl.multiple_of(i // (2 * lane_tiles) * SB, SB), SB)
        step(lanes, i // lane_tiles % 2, rows)
        return carry

    lax.fori_loop(0, 2 * tiles * lane_tiles, body, 0, unroll=2)


def near_kernel(place, taps, own, other, own_back, other_back, *rest):
    partial = rest[-1]
    frames = own.shape[0]
    count = 2 * frames

    def run(first, second, first_back, second_back):
        window = []
        for start, ref in ((-count, first_back), (frames - count, second_back), (0, first), (frames, second)):
            window += [(start + i, ref, i) for i in range(frames)]

        def step(lanes, part, rows):
            sums = weighted(taps, 0, window, count, lanes, part, rows, [None] * count)
            for f in range(count):
                partial[f, part, rows, lanes] = sums[f].reshape(SB, LANES)

        over_tiles(*own.shape[2:], step)

    @pl.when(place[0] == 0)
    def _():
        run(own, other, own_back, other_back)

    @pl.when(place[0] == 1)
    def _():
        run(other, own, other_back, own_back)


def far_kernel(place, taps, partial, far, *rest):
    keep, send = rest[-2:]
    frames = keep.shape[0]
    count = 2 * frames
    window = [(i + 1 - 2 * count, far, i) for i in range(far.shape[0])]

    def run(first_out, second_out):
        def step(lanes, part, rows):
            sums = [partial[f, part, rows, lanes].reshape(SB // 8, 8, LANES) for f in range(count)]
            sums = weighted(taps, count, window, count, lanes, part, rows, sums)
            for f in range(count):
                out = first_out if f < frames else second_out
                out[f % frames, part, rows, lanes] = sums[f].reshape(SB, LANES).astype(BF16)

        over_tiles(*keep.shape[2:], step)

    @pl.when(place[0] == 0)
    def _():
        run(keep, send)

    @pl.when(place[0] == 1)
    def _():
        run(send, keep)


def near_filter(place, taps, own, other, own_back, other_back, pol, earlier):
    frames, parts, stations, samples = other.shape
    block = 512
    both = pl.BlockSpec((None, frames, parts, stations, block), lambda i, place: (pol, 0, 0, 0, i))
    one = pl.BlockSpec((frames, parts, stations, block), lambda i, place: (0, 0, 0, i))
    return pl.pallas_call(
        near_kernel,
        out_shape=jax.ShapeDtypeStruct((2 * frames, parts, stations, samples), F32),
        grid_spec=pltpu.PrefetchScalarGridSpec(
            num_scalar_prefetch=1,
            grid=(samples // block,),
            in_specs=[pl.BlockSpec((taps.shape[0], 8, block), lambda i, place: (0, 0, i)), both, one, both, one]
            + [pl.BlockSpec(memory_space=pl.ANY)] * len(earlier),
            out_specs=pl.BlockSpec((2 * frames, parts, stations, block), lambda i, place: (0, 0, 0, i)),
        ),
        compiler_params=pltpu.CompilerParams(vmem_limit_bytes=VMEM_LIMIT),
        cost_estimate=cost(8 * stations / 32),
        name="near",
    )(place, taps, own, other, own_back, other_back, *earlier)


def far_filter(place, taps, partial, far, low, size, earlier):
    count, parts, stations, _ = partial.shape
    frames = count // 2
    block = next(size // n for n in (2, 1) if size // n % LANES == 0)

    def spec(depth, start):
        shape = (pl.Element(depth), pl.Element(parts), pl.Element(stations), pl.Element(block))
        return pl.BlockSpec(shape, lambda i, place: (0, 0, 0, pl.multiple_of(start + i * block, LANES)))

    shape = jax.ShapeDtypeStruct((frames, parts, stations, size), BF16)
    return pl.pallas_call(
        far_kernel,
        out_shape=(shape, shape),
        grid_spec=pltpu.PrefetchScalarGridSpec(
            num_scalar_prefetch=1,
            grid=(size // block,),
            in_specs=[
                pl.BlockSpec(
                    (pl.Element(taps.shape[0] - count), pl.Element(8), pl.Element(block)),
                    lambda i, place: (count, 0, pl.multiple_of(low + i * block, LANES)),
                )
            ]
            + [spec(count, low), spec(far.shape[0], 0)]
            + [pl.BlockSpec(memory_space=pl.ANY)] * len(earlier),
            out_specs=[spec(frames, 0)] * 2,
        ),
        compiler_params=pltpu.CompilerParams(vmem_limit_bytes=VMEM_LIMIT),
        cost_estimate=cost(1),
        name="far",
    )(place, taps, partial, far, *earlier)


def onward_kernel(place, own_back, other_back, *rest):
    far = rest[-1]
    frames = other_back.shape[0]
    own_back = own_back.at[0]

    def run(first, second):
        far[: frames - 1] = first[1:]
        far[frames - 1 :] = second[...]

    @pl.when(place[0] == 0)
    def _():
        run(own_back, other_back)

    @pl.when(place[0] == 1)
    def _():
        run(other_back, own_back)


def onward(place, own_back, other_back, pol, low, size, earlier):
    frames, parts, stations, _ = other_back.shape
    depth = 2 * frames - 1

    def spec(depth, *before):
        shape = tuple(pl.Element(n) for n in (1,) * len(before) + (depth, 1, stations, size))
        return pl.BlockSpec(shape, lambda i, place: before + (0, i, 0, low))

    return pl.pallas_call(
        onward_kernel,
        out_shape=jax.ShapeDtypeStruct((depth, parts, stations, size), BF16),
        grid_spec=pltpu.PrefetchScalarGridSpec(
            num_scalar_prefetch=1,
            grid=(parts,),
            in_specs=[spec(frames, pol), spec(frames)] + [pl.BlockSpec(memory_space=pl.ANY)] * len(earlier),
            out_specs=pl.BlockSpec((depth, 1, stations, size), lambda i, place: (0, i, 0, 0)),
        ),
        compiler_params=pltpu.CompilerParams(vmem_limit_bytes=VMEM_LIMIT),
        cost_estimate=cost(3),
        name="onward",
    )(place, own_back, other_back, *earlier)


def weight_kernel(table, index, mask, *rest):
    out = rest[-1]
    groups, depth, width = out.shape
    beams = width // 2
    half = depth // 2
    rows = lax.broadcasted_iota(jnp.int32, (table.shape[0], beams), 0)
    for q in range(index.shape[0]):
        hit = jnp.where((rows == index[q : q + 1, :]) & (mask[q : q + 1, :] != 0), 1.0, 0.0).astype(BF16)
        picked = lax.dot_general(table[...], hit, (((0,), (0,)), ((), ())), preferred_element_type=F32)
        picked = picked.reshape(groups, 2, SB, beams)
        low = q * SB
        re, im = picked[:, 0], picked[:, 1]
        out[:, low : low + SB, :beams] = re.astype(BF16)
        out[:, low : low + SB, beams:] = im.astype(BF16)
        low += half
        out[:, low : low + SB, :beams] = (-im).astype(BF16)
        out[:, low : low + SB, beams:] = re.astype(BF16)


def beam_weights(table, index, mask, earlier):
    blocks, beams = index.shape
    groups = table.shape[1] // (2 * SB)
    shape = (groups, 2 * blocks * SB, 2 * beams)
    return pl.pallas_call(
        weight_kernel,
        out_shape=jax.ShapeDtypeStruct(shape, BF16),
        in_specs=[pl.BlockSpec(memory_space=pltpu.VMEM)] * 3 + [pl.BlockSpec(memory_space=pl.ANY)] * len(earlier),
        compiler_params=pltpu.CompilerParams(vmem_limit_bytes=VMEM_LIMIT),
        cost_estimate=cost(4),
        name="weights",
    )(table, index, mask, *earlier)


def beam_kernel(source_count, ranges, later_count, has_earlier, place, *refs):
    refs = list(refs)
    inputs = [refs.pop(0) for _ in range(source_count + 2 + has_earlier)]
    refs = refs[later_count:]
    out, mixed, spectra, sems, *held = refs
    inputs[source_count] = inputs[source_count].at[pl.ds(place[1], 1)]
    copies = [pltpu.make_async_copy(ref, to, sems.at[k]) for k, (ref, to) in enumerate(zip(inputs, held))]
    table, weights = held[source_count : source_count + 2]
    step = pl.program_id(0)
    frames, _, stations, _ = held[0].shape
    tiles = stations // SB
    station_count = stations * (source_count // ranges)
    groups = spectra.shape[0]
    beams = weights.shape[2] // 2
    rows_of = table.shape[2] // 2 // groups
    pair = 2
    lane_tiles = beams // LANES
    at_once = groups // pl.num_programs(0)

    @pl.when(step == 0)
    def _():
        for copy in copies:
            copy.start()
        for k in range(0, source_count, ranges):
            for copy in copies[k : k + ranges]:
                copy.wait()
            pieces = []
            for ref in held[k : k + ranges]:
                pieces += [(ref, slice(n, n + LANES)) for n in range(0, ref.shape[3], LANES)]

            def radix(i, carry, pieces=pieces, low=k // ranges * stations):
                f, rows = i // tiles, pl.ds(pl.multiple_of(i % tiles * SB, SB), SB)
                values = [tuple(ref[f, part, rows, lanes].astype(F32) for part in range(2)) for ref, lanes in pieces]
                target = pl.ds(pl.multiple_of(f * station_count + low + i % tiles * SB, SB), SB)
                for b, (re, im) in enumerate(sixteen_points(values)):
                    mixed[b, target, :LANES] = re.astype(BF16)
                    mixed[b, target, LANES:] = im.astype(BF16)
                return carry

            lax.fori_loop(0, frames * tiles, radix, 0, unroll=2)
        copies[source_count].wait()

        def transform(b, carry):
            for start in range(0, frames, pair):
                product = lax.dot_general(
                    table[0, b],
                    mixed[b, start * station_count : (start + pair) * station_count],
                    (((1,), (1,)), ((), ())),
                    preferred_element_type=F32,
                )
                product = product.reshape(2, groups, rows_of, pair * station_count)
                rows = slice(start * rows_of, (start + pair) * rows_of)
                for part in range(2):
                    value = jnp.concatenate(
                        [product[part, :, :, f * station_count : (f + 1) * station_count] for f in range(pair)], axis=1
                    )
                    columns = slice(part * station_count, (part + 1) * station_count)
                    spectra[:, b, rows, columns] = value.astype(BF16)
            return carry

        lax.fori_loop(0, RADIX, transform, 0, unroll=True)
        for copy in copies[source_count + 1 :]:
            copy.wait()

    for k in range(at_once):
        group = step * at_once + k
        rows = spectra[group].reshape(RADIX * frames * rows_of, 2 * station_count)
        beam = jnp.dot(rows, weights[group], preferred_element_type=F32)
        re, im = beam[:, :beams], beam[:, beams:]
        power = re * re + im * im
        if not has_earlier:
            out[k] = power
            continue
        power = power + held[-1][group]
        for b in range(RADIX):
            for f in range(frames):
                at = (b * frames + f) * rows_of
                channels = pl.ds(k * rows_of * RADIX + b, rows_of, stride=RADIX)
                for t in range(lane_tiles):
                    out[channels, t, f, :] = power[at : at + rows_of, t * LANES : (t + 1) * LANES]


def beam_power(place, sources, ranges, table, weights, earlier, channels, later=()):
    frames = sources[0].shape[0]
    groups, depth, width = weights.shape
    beams = width // 2
    station_count = sum(s.shape[2] for s in sources) // ranges
    at_once = 4
    flat = (groups, channels // groups * frames, beams)
    flat_spec = pl.BlockSpec((at_once,) + flat[1:], lambda i, place: (i, 0, 0))
    operands = list(sources) + [table, weights] + ([] if earlier is None else [earlier])
    in_specs = [pl.BlockSpec(memory_space=pltpu.HBM)] * len(operands) + [pl.BlockSpec(memory_space=pl.ANY)] * len(later)
    scratch = [
        pltpu.VMEM((RADIX, frames * station_count, 2 * LANES), BF16),
        pltpu.VMEM((groups, RADIX, frames * channels // groups // RADIX, 2 * station_count), BF16),
        pltpu.SemaphoreType.DMA((len(operands),)),
    ]
    for k, block in enumerate(operands):
        scratch.append(pltpu.VMEM(((1,) if k == len(sources) else block.shape[:1]) + block.shape[1:], block.dtype))
    if earlier is None:
        out_shape = jax.ShapeDtypeStruct(flat, F32)
        out_spec = flat_spec
    else:
        out_shape = jax.ShapeDtypeStruct((channels, beams // LANES, frames, LANES), F32)
        out_spec = pl.BlockSpec((channels // groups * at_once,) + out_shape.shape[1:], lambda i, place: (i, 0, 0, 0))
    return pl.pallas_call(
        functools.partial(beam_kernel, len(sources), ranges, len(later), earlier is not None),
        out_shape=out_shape,
        grid_spec=pltpu.PrefetchScalarGridSpec(
            num_scalar_prefetch=1,
            grid=(groups // at_once,),
            in_specs=in_specs,
            out_specs=out_spec,
            scratch_shapes=scratch,
        ),
        compiler_params=pltpu.CompilerParams(vmem_limit_bytes=VMEM_LIMIT),
        cost_estimate=cost(0),
        name="beams",
    )(place, *operands, *later)


def flipped(rows, bit):
    return jnp.where(bit == 1, rows[::-1], rows)


def body(voltages, filter_taps, use_mask, block_index, weight_blocks):
    stations, pols, frames, parts, samples = voltages.shape
    history = filter_taps.shape[0] - 1
    half = stations // 2
    time_devices = lax.axis_size("tm")
    side = lax.axis_index("tm") % 2
    core = lax.axis_index("stn")
    place = jnp.stack([side, core]).astype(jnp.int32)

    def pair(block):
        return lax.ppermute(block, "tm", [(i, i ^ 1) for i in range(time_devices)])

    def hop(block, skip=0):
        return lax.ppermute(block, "tm", [(i, i + 2) for i in range(skip, time_devices - 2)])

    def swap(block):
        return lax.ppermute(block, "stn", [(0, 1), (1, 0)])

    def laid(block):
        return jnp.moveaxis(block, 0, -2)

    (own,) = cut(voltages, [None], [])
    other = cut(voltages, list(range(pols)), [own, place])
    columns = weight_blocks.shape[1] // CORES
    shard = lax.dynamic_slice_in_dim(weight_blocks, core * columns, columns, 1)
    shards = [shard] + [
        lax.ppermute(shard, "tm", [(i, i ^ apart) for i in range(time_devices)]) for apart in range(2, time_devices, 2)
    ]
    own_back = laid(after(hop(own)))
    own = laid(own)
    other = [laid(after(pair(block))) for block in other]

    def ordered(rows):
        rows = rows.T.reshape(2, 2, 2, -1)
        rows = flipped(rows, core)
        rows = flipped(rows.swapaxes(0, 1), side).swapaxes(0, 1)
        return rows.reshape(8, -1)

    each = weight_blocks.shape[0]
    apart = block_index // each ^ lax.axis_index("tm")
    index = (apart % 2 * (time_devices // 2) + apart // 2) * each + block_index % each
    table = jnp.asarray(dft_tables(samples))
    taps = jnp.broadcast_to(filter_taps[:, None, :], (history + 1, 8, samples))

    parts_of = [tuple(n * samples // 16 for n in sizes) for sizes in ((10,6), (8,5,3))]
    chunks = [(pol, sum(sizes[:i]), size) for pol, sizes in enumerate(parts_of) for i, size in enumerate(sizes)]
    other_back = [hop(block) for block in other]
    further = []
    for pol, low, size in chunks:
        gates = [] if further else shards[1:]
        further.append(onward(place, own_back, other_back[pol], pol, low, size, gates))
    shards = jnp.concatenate(shards)
    far = [hop(block, 2) for block in further]
    weights = beam_weights(jnp.concatenate([shards, pair(shards)]), ordered(index), ordered(use_mask), [])
    partial = []
    for pol in range(pols):
        gates = (further if pol else further[:2]) + [weights] + other_back[1:]
        partial.append(near_filter(place, taps, own, other[pol], own_back, other_back[pol], pol, gates))
    keeps, sents, power = [], [], None

    def power_of(pol, earlier, later=()):
        here = slice(2 * pol, 2 + len(chunks) * pol)
        mine, pairs = keeps[here], sents[here]
        sources = mine + pairs + [swap(block) for block in mine + pairs]
        return beam_power(place, sources, len(mine), table, weights, earlier, samples // CORES, later)

    for k, (pol, low, size) in enumerate(chunks):
        gates = {0: [], 1: [*sents[:1], partial[1]], 2: sents[1:2], 3: [power], 4: keeps[3:4]}[k]
        keep, send = far_filter(place, taps, partial[pol], far[k], low, size, gates)
        keeps.append(keep)
        sents.append(pair(send))
        if k == 2:
            power = power_of(0, None, [keep])
    power = power_of(1, power)
    return jnp.moveaxis(power, 1, 2).reshape(power.shape[0], power.shape[2], -1)


def solution(mesh):
    in_specs = (
        P(("parts", "stn"), None, "tm", None, None),
        P(),
        P("parts", None),
        P("parts", None),
        P("tm", None),
    )
    out_specs = P("stn", "tm", "parts")
    return jax.shard_map(body, mesh=mesh, in_specs=in_specs, out_specs=out_specs, check_vma=False)
```

```python
import functools
import math

import jax
import jax.numpy as jnp
import ml_dtypes
import numpy as np
from jax import lax
from jax.experimental import pallas as pl
from jax.experimental.pallas import tpu as pltpu
from jax.sharding import PartitionSpec as P

SB = 16
G = 16
RADIX = 16
LANES = 128
CORES = 2
VMEM_LIMIT = 63 * 1024 * 1024
F32 = jnp.float32
BF16 = jnp.bfloat16


def cost(microseconds):
    return pl.CostEstimate(flops=0, bytes_accessed=int(microseconds * 3.3e6), transcendentals=0)


def dft_tables(channels):
    per_half = channels // RADIX // CORES
    b = np.arange(RADIX)[None, :, None, None]
    e = np.arange(LANES)[None, None, None, :]
    d = np.arange(CORES * per_half).reshape(CORES, 1, per_half, 1)
    angle = (e * (RADIX * d + b) % channels) * (2.0 * math.pi / channels)
    cosine, sine = np.cos(angle), np.sin(angle)
    real_rows = np.concatenate([cosine, sine], axis=3)
    imag_rows = np.concatenate([-sine, cosine], axis=3)
    table = np.concatenate([real_rows, imag_rows], axis=2) / math.sqrt(channels)
    return table.astype(ml_dtypes.bfloat16)


def turned(value, step, size):
    re, im = value
    step %= size
    if step == 0:
        return re, im
    if 4 * step == size:
        return im, -re
    if 2 * step == size:
        return -re, -im
    if 4 * step == 3 * size:
        return -im, re
    cosine, sine = math.cos(2 * math.pi * step / size), math.sin(2 * math.pi * step / size)
    if 8 * step == size:
        return (re + im) * cosine, (im - re) * cosine
    if 8 * step == 3 * size:
        return (im - re) * sine, -(re + im) * sine
    return re * cosine + im * sine, im * cosine - re * sine


def four_points(values):
    (r0, i0), (r1, i1), (r2, i2), (r3, i3) = values
    sr, si, dr, di = r0 + r2, i0 + i2, r0 - r2, i0 - i2
    tr, ti, er, ei = r1 + r3, i1 + i3, r1 - r3, i1 - i3
    return [(sr + tr, si + ti), (dr + ei, di - er), (sr - tr, si - ti), (dr - ei, di + er)]


def sixteen_points(values):
    inner = [four_points([values[4 * a1 + a0] for a1 in range(4)]) for a0 in range(4)]
    result = [None] * 16
    for b0 in range(4):
        outer = four_points([turned(inner[a0][b0], a0 * b0, 16) for a0 in range(4)])
        for b1 in range(4):
            result[4 * b1 + b0] = outer[b1]
    return result


def after(block, *earlier):
    return pl.pallas_call(
        lambda *refs: None,
        out_shape=jax.ShapeDtypeStruct(block.shape, block.dtype),
        in_specs=[pl.BlockSpec(memory_space=pl.ANY)] * (1 + len(earlier)),
        out_specs=pl.BlockSpec(memory_space=pl.ANY),
        input_output_aliases={0: 0},
        cost_estimate=cost(0),
        name="after",
    )(block, *earlier)


def cut_kernel(mine, voltages, *rest):
    count = len(mine)
    outs, (buffer, loads, stores) = rest[-3 - count : -3], rest[-3:]
    half = buffer.shape[0]
    pieces = loads.shape[0]
    size = half // pieces
    side = lax.rem(lax.axis_index("tm"), 2)
    start = half * (side if mine[0] is None else 1 - side)

    def load(k):
        return pltpu.make_async_copy(
            voltages.at[pl.ds(start + k * size, size)], buffer.at[pl.ds(k * size, size)], loads.at[k]
        )

    def store(k, i):
        block = buffer.at[pl.ds(k * size, size)]
        block = block if mine[i] is None else block.at[:, mine[i]]
        return pltpu.make_async_copy(block, outs[i].at[pl.ds(k * size, size)], stores.at[i, k])

    for k in range(pieces):
        load(k).start()
    for k in range(pieces):
        load(k).wait()
        for i in range(count):
            store(k, i).start()
    for k in range(pieces):
        for i in range(count):
            store(k, i).wait()


def cut(voltages, mine, earlier):
    stations, pols, frames, parts, samples = voltages.shape
    whole = (stations // 2, pols, frames, parts, samples)
    shapes = [whole if pol is None else whole[:1] + whole[2:] for pol in mine]
    pieces = 4
    there = pl.BlockSpec(memory_space=pltpu.HBM)
    return pl.pallas_call(
        functools.partial(cut_kernel, mine),
        out_shape=[jax.ShapeDtypeStruct(shape, BF16) for shape in shapes],
        in_specs=[there] + [pl.BlockSpec(memory_space=pl.ANY)] * len(earlier),
        out_specs=[there] * len(shapes),
        scratch_shapes=[
            pltpu.VMEM(whole, BF16),
            pltpu.SemaphoreType.DMA((pieces,)),
            pltpu.SemaphoreType.DMA((len(mine), pieces)),
        ],
        compiler_params=pltpu.CompilerParams(vmem_limit_bytes=VMEM_LIMIT),
        cost_estimate=cost(2),
        name="cut",
    )(voltages, *earlier)


def weighted(taps, first_tap, window, count, lanes, part, rows, sums):
    tap_count = taps.shape[0]
    tap_rows = [taps[k, :, lanes][None] for k in range(tap_count)]
    for j, ref, index in window:
        value = ref[index, part, rows, lanes].astype(F32).reshape(SB // 8, 8, LANES)
        for f in range(count):
            k = f - j - first_tap
            if 0 <= k < tap_count:
                term = tap_rows[k] * value
                sums[f] = term if sums[f] is None else sums[f] + term
    return sums


def over_tiles(stations, samples, step):
    tiles, lane_tiles = stations // SB, samples // LANES

    def body(i, carry):
        lanes = pl.ds(pl.multiple_of(i % lane_tiles * LANES, LANES), LANES)
        rows = pl.ds(pl.multiple_of(i // (2 * lane_tiles) * SB, SB), SB)
        step(lanes, i // lane_tiles % 2, rows)
        return carry

    lax.fori_loop(0, 2 * tiles * lane_tiles, body, 0, unroll=2)


def near_kernel(place, taps, own, other, own_back, other_back, *rest):
    partial = rest[-1]
    frames = own.shape[0]
    count = 2 * frames

    def run(first, second, first_back, second_back):
        window = []
        for start, ref in ((-count, first_back), (frames - count, second_back), (0, first), (frames, second)):
            window += [(start + i, ref, i) for i in range(frames)]

        def step(lanes, part, rows):
            sums = weighted(taps, 0, window, count, lanes, part, rows, [None] * count)
            for f in range(count):
                partial[f, part, rows, lanes] = sums[f].reshape(SB, LANES)

        over_tiles(*own.shape[2:], step)

    @pl.when(place[0] == 0)
    def _():
        run(own, other, own_back, other_back)

    @pl.when(place[0] == 1)
    def _():
        run(other, own, other_back, own_back)


def far_kernel(place, taps, partial, far, *rest):
    keep, send = rest[-2:]
    frames = keep.shape[0]
    count = 2 * frames
    window = [(i + 1 - 2 * count, far, i) for i in range(far.shape[0])]

    def run(first_out, second_out):
        def step(lanes, part, rows):
            sums = [partial[f, part, rows, lanes].reshape(SB // 8, 8, LANES) for f in range(count)]
            sums = weighted(taps, count, window, count, lanes, part, rows, sums)
            for f in range(count):
                out = first_out if f < frames else second_out
                out[f % frames, part, rows, lanes] = sums[f].reshape(SB, LANES).astype(BF16)

        over_tiles(*keep.shape[2:], step)

    @pl.when(place[0] == 0)
    def _():
        run(keep, send)

    @pl.when(place[0] == 1)
    def _():
        run(send, keep)


def near_filter(place, taps, own, other, own_back, other_back, pol, earlier):
    frames, parts, stations, samples = other.shape
    block = 512
    both = pl.BlockSpec((None, frames, parts, stations, block), lambda i, place: (pol, 0, 0, 0, i))
    one = pl.BlockSpec((frames, parts, stations, block), lambda i, place: (0, 0, 0, i))
    return pl.pallas_call(
        near_kernel,
        out_shape=jax.ShapeDtypeStruct((2 * frames, parts, stations, samples), F32),
        grid_spec=pltpu.PrefetchScalarGridSpec(
            num_scalar_prefetch=1,
            grid=(samples // block,),
            in_specs=[pl.BlockSpec((taps.shape[0], 8, block), lambda i, place: (0, 0, i)), both, one, both, one]
            + [pl.BlockSpec(memory_space=pl.ANY)] * len(earlier),
            out_specs=pl.BlockSpec((2 * frames, parts, stations, block), lambda i, place: (0, 0, 0, i)),
        ),
        compiler_params=pltpu.CompilerParams(vmem_limit_bytes=VMEM_LIMIT),
        cost_estimate=cost(8 * stations / 32),
        name="near",
    )(place, taps, own, other, own_back, other_back, *earlier)


def far_filter(place, taps, partial, far, low, size, earlier):
    count, parts, stations, _ = partial.shape
    frames = count // 2
    block = next(size // n for n in (2, 3, 1) if size // n % LANES == 0)

    def spec(depth, start):
        shape = (pl.Element(depth), pl.Element(parts), pl.Element(stations), pl.Element(block))
        return pl.BlockSpec(shape, lambda i, place: (0, 0, 0, pl.multiple_of(start + i * block, LANES)))

    shape = jax.ShapeDtypeStruct((frames, parts, stations, size), BF16)
    return pl.pallas_call(
        far_kernel,
        out_shape=(shape, shape),
        grid_spec=pltpu.PrefetchScalarGridSpec(
            num_scalar_prefetch=1,
            grid=(size // block,),
            in_specs=[
                pl.BlockSpec(
                    (pl.Element(taps.shape[0] - count), pl.Element(8), pl.Element(block)),
                    lambda i, place: (count, 0, pl.multiple_of(low + i * block, LANES)),
                )
            ]
            + [spec(count, low), spec(far.shape[0], 0)]
            + [pl.BlockSpec(memory_space=pl.ANY)] * len(earlier),
            out_specs=[spec(frames, 0)] * 2,
        ),
        compiler_params=pltpu.CompilerParams(vmem_limit_bytes=VMEM_LIMIT),
        cost_estimate=cost(1),
        name="far",
    )(place, taps, partial, far, *earlier)


def onward_kernel(place, own_back, other_back, *rest):
    far = rest[-1]
    frames = other_back.shape[0]
    own_back = own_back.at[0]

    def run(first, second):
        far[: frames - 1] = first[1:]
        far[frames - 1 :] = second[...]

    @pl.when(place[0] == 0)
    def _():
        run(own_back, other_back)

    @pl.when(place[0] == 1)
    def _():
        run(other_back, own_back)


def onward(place, own_back, other_back, pol, low, size, earlier):
    frames, parts, stations, _ = other_back.shape
    depth = 2 * frames - 1

    def spec(depth, *before):
        shape = tuple(pl.Element(n) for n in (1,) * len(before) + (depth, 1, stations, size))
        return pl.BlockSpec(shape, lambda i, place: before + (0, i, 0, low))

    return pl.pallas_call(
        onward_kernel,
        out_shape=jax.ShapeDtypeStruct((depth, parts, stations, size), BF16),
        grid_spec=pltpu.PrefetchScalarGridSpec(
            num_scalar_prefetch=1,
            grid=(parts,),
            in_specs=[spec(frames, pol), spec(frames)] + [pl.BlockSpec(memory_space=pl.ANY)] * len(earlier),
            out_specs=pl.BlockSpec((depth, 1, stations, size), lambda i, place: (0, i, 0, 0)),
        ),
        compiler_params=pltpu.CompilerParams(vmem_limit_bytes=VMEM_LIMIT),
        cost_estimate=cost(3),
        name="onward",
    )(place, own_back, other_back, *earlier)


def weight_kernel(table, index, mask, *rest):
    out = rest[-1]
    groups, depth, width = out.shape
    beams = width // 2
    half = depth // 2
    rows = lax.broadcasted_iota(jnp.int32, (table.shape[0], beams), 0)
    for q in range(index.shape[0]):
        hit = jnp.where((rows == index[q : q + 1, :]) & (mask[q : q + 1, :] != 0), 1.0, 0.0).astype(BF16)
        picked = lax.dot_general(table[...], hit, (((0,), (0,)), ((), ())), preferred_element_type=F32)
        picked = picked.reshape(groups, 2, SB, beams)
        low = q * SB
        re, im = picked[:, 0], picked[:, 1]
        out[:, low : low + SB, :beams] = re.astype(BF16)
        out[:, low : low + SB, beams:] = im.astype(BF16)
        low += half
        out[:, low : low + SB, :beams] = (-im).astype(BF16)
        out[:, low : low + SB, beams:] = re.astype(BF16)


def beam_weights(table, index, mask, earlier):
    blocks, beams = index.shape
    groups = table.shape[1] // (2 * SB)
    shape = (groups, 2 * blocks * SB, 2 * beams)
    return pl.pallas_call(
        weight_kernel,
        out_shape=jax.ShapeDtypeStruct(shape, BF16),
        in_specs=[pl.BlockSpec(memory_space=pltpu.VMEM)] * 3 + [pl.BlockSpec(memory_space=pl.ANY)] * len(earlier),
        compiler_params=pltpu.CompilerParams(vmem_limit_bytes=VMEM_LIMIT),
        cost_estimate=cost(4),
        name="weights",
    )(table, index, mask, *earlier)


def beam_kernel(source_count, ranges, later_count, has_earlier, place, *refs):
    refs = list(refs)
    inputs = [refs.pop(0) for _ in range(source_count + 2 + has_earlier)]
    refs = refs[later_count:]
    out, mixed, spectra, sems, *held = refs
    inputs[source_count] = inputs[source_count].at[pl.ds(place[1], 1)]
    copies = [pltpu.make_async_copy(ref, to, sems.at[k]) for k, (ref, to) in enumerate(zip(inputs, held))]
    table, weights = held[source_count : source_count + 2]
    step = pl.program_id(0)
    frames, _, stations, _ = held[0].shape
    tiles = stations // SB
    station_count = stations * (source_count // ranges)
    groups = spectra.shape[0]
    beams = weights.shape[2] // 2
    rows_of = table.shape[2] // 2 // groups
    pair = frames if has_earlier else 2
    lane_tiles = beams // LANES
    at_once = groups // pl.num_programs(0)

    @pl.when(step == 0)
    def _():
        for copy in copies:
            copy.start()
        for k in range(0, source_count, ranges):
            for copy in copies[k : k + ranges]:
                copy.wait()
            pieces = []
            for ref in held[k : k + ranges]:
                pieces += [(ref, slice(n, n + LANES)) for n in range(0, ref.shape[3], LANES)]

            def radix(i, carry, pieces=pieces, low=k // ranges * stations):
                f, rows = i // tiles, pl.ds(pl.multiple_of(i % tiles * SB, SB), SB)
                values = [tuple(ref[f, part, rows, lanes].astype(F32) for part in range(2)) for ref, lanes in pieces]
                target = pl.ds(pl.multiple_of(f * station_count + low + i % tiles * SB, SB), SB)
                for b, (re, im) in enumerate(sixteen_points(values)):
                    mixed[b, target, :LANES] = re.astype(BF16)
                    mixed[b, target, LANES:] = im.astype(BF16)
                return carry

            lax.fori_loop(0, frames * tiles, radix, 0, unroll=2)
        copies[source_count].wait()

        def transform(b, carry):
            for start in range(0, frames, pair):
                product = lax.dot_general(
                    table[0, b],
                    mixed[b, start * station_count : (start + pair) * station_count],
                    (((1,), (1,)), ((), ())),
                    preferred_element_type=F32,
                )
                product = product.reshape(2, groups, rows_of, pair * station_count)
                rows = slice(start * rows_of, (start + pair) * rows_of)
                for part in range(2):
                    value = jnp.concatenate(
                        [product[part, :, :, f * station_count : (f + 1) * station_count] for f in range(pair)], axis=1
                    )
                    columns = slice(part * station_count, (part + 1) * station_count)
                    spectra[:, b, rows, columns] = value.astype(BF16)
            return carry

        lax.fori_loop(0, RADIX, transform, 0, unroll=True)
        for copy in copies[source_count + 1 :]:
            copy.wait()

    for k in range(at_once):
        group = step * at_once + k
        rows = spectra[group].reshape(RADIX * frames * rows_of, 2 * station_count)
        beam = jnp.dot(rows, weights[group], preferred_element_type=F32)
        re, im = beam[:, :beams], beam[:, beams:]
        power = re * re + im * im
        if not has_earlier:
            out[k] = power
            continue
        power = power + held[-1][group]
        for b in range(RADIX):
            for f in range(frames):
                at = (b * frames + f) * rows_of
                channels = pl.ds(k * rows_of * RADIX + b, rows_of, stride=RADIX)
                for t in range(lane_tiles):
                    out[channels, t, f, :] = power[at : at + rows_of, t * LANES : (t + 1) * LANES]


def beam_power(place, sources, ranges, table, weights, earlier, channels, later=()):
    frames = sources[0].shape[0]
    groups, depth, width = weights.shape
    beams = width // 2
    station_count = sum(s.shape[2] for s in sources) // ranges
    at_once = 4
    flat = (groups, channels // groups * frames, beams)
    flat_spec = pl.BlockSpec((at_once,) + flat[1:], lambda i, place: (i, 0, 0))
    operands = list(sources) + [table, weights] + ([] if earlier is None else [earlier])
    in_specs = [pl.BlockSpec(memory_space=pltpu.HBM)] * len(operands) + [pl.BlockSpec(memory_space=pl.ANY)] * len(later)
    scratch = [
        pltpu.VMEM((RADIX, frames * station_count, 2 * LANES), BF16),
        pltpu.VMEM((groups, RADIX, frames * channels // groups // RADIX, 2 * station_count), BF16),
        pltpu.SemaphoreType.DMA((len(operands),)),
    ]
    for k, block in enumerate(operands):
        scratch.append(pltpu.VMEM(((1,) if k == len(sources) else block.shape[:1]) + block.shape[1:], block.dtype))
    if earlier is None:
        out_shape = jax.ShapeDtypeStruct(flat, F32)
        out_spec = flat_spec
    else:
        out_shape = jax.ShapeDtypeStruct((channels, beams // LANES, frames, LANES), F32)
        out_spec = pl.BlockSpec((channels // groups * at_once,) + out_shape.shape[1:], lambda i, place: (i, 0, 0, 0))
    return pl.pallas_call(
        functools.partial(beam_kernel, len(sources), ranges, len(later), earlier is not None),
        out_shape=out_shape,
        grid_spec=pltpu.PrefetchScalarGridSpec(
            num_scalar_prefetch=1,
            grid=(groups // at_once,),
            in_specs=in_specs,
            out_specs=out_spec,
            scratch_shapes=scratch,
        ),
        compiler_params=pltpu.CompilerParams(vmem_limit_bytes=VMEM_LIMIT),
        cost_estimate=cost(0),
        name="beams",
    )(place, *operands, *later)


def flipped(rows, bit):
    return jnp.where(bit == 1, rows[::-1], rows)


def body(voltages, filter_taps, use_mask, block_index, weight_blocks):
    stations, pols, frames, parts, samples = voltages.shape
    history = filter_taps.shape[0] - 1
    half = stations // 2
    time_devices = lax.axis_size("tm")
    side = lax.axis_index("tm") % 2
    core = lax.axis_index("stn")
    place = jnp.stack([side, core]).astype(jnp.int32)

    def pair(block):
        return lax.ppermute(block, "tm", [(i, i ^ 1) for i in range(time_devices)])

    def hop(block, skip=0):
        return lax.ppermute(block, "tm", [(i, i + 2) for i in range(skip, time_devices - 2)])

    def swap(block):
        return lax.ppermute(block, "stn", [(0, 1), (1, 0)])

    def laid(block):
        return jnp.moveaxis(block, 0, -2)

    (own,) = cut(voltages, [None], [])
    other = cut(voltages, list(range(pols)), [own, place])
    columns = weight_blocks.shape[1] // CORES
    shard = lax.dynamic_slice_in_dim(weight_blocks, core * columns, columns, 1)
    shards = [shard] + [
        lax.ppermute(shard, "tm", [(i, i ^ apart) for i in range(time_devices)]) for apart in range(2, time_devices, 2)
    ]
    own_back = laid(after(hop(own)))
    own = laid(own)
    other = [laid(after(pair(block))) for block in other]

    def ordered(rows):
        rows = rows.T.reshape(2, 2, 2, -1)
        rows = flipped(rows, core)
        rows = flipped(rows.swapaxes(0, 1), side).swapaxes(0, 1)
        return rows.reshape(8, -1)

    each = weight_blocks.shape[0]
    apart = block_index // each ^ lax.axis_index("tm")
    index = (apart % 2 * (time_devices // 2) + apart // 2) * each + block_index % each
    table = jnp.asarray(dft_tables(samples))
    taps = jnp.broadcast_to(filter_taps[:, None, :], (history + 1, 8, samples))

    parts_of = [(samples // 2, samples // 2), (9 * samples // 16, 7 * samples // 16)]
    chunks = [(pol, sum(sizes[:i]), size) for pol, sizes in enumerate(parts_of) for i, size in enumerate(sizes)]
    other_back = [hop(block) for block in other]
    further = []
    for pol, low, size in chunks:
        gates = [] if further else shards[1:]
        further.append(onward(place, own_back, other_back[pol], pol, low, size, gates))
    shards = jnp.concatenate(shards)
    far = [hop(block, 2) for block in further]
    weights = beam_weights(jnp.concatenate([shards, pair(shards)]), ordered(index), ordered(use_mask), [])
    partial = []
    for pol in range(pols):
        gates = further[: 2 * pol + 2] + [weights] + other_back[1:]
        partial.append(near_filter(place, taps, own, other[pol], own_back, other_back[pol], pol, gates))
    keeps, sents, power = [], [], None

    def power_of(pol, earlier, later=()):
        mine, pairs = keeps[2 * pol : 2 * pol + 2], sents[2 * pol : 2 * pol + 2]
        sources = mine + pairs + [swap(block) for block in mine + pairs]
        return beam_power(place, sources, 2, table, weights, earlier, samples // CORES, later)

    for k, (pol, low, size) in enumerate(chunks):
        gates = {0: [], 1: [*sents[:1], partial[1]], 2: sents[1:2], 3: [power]}[k]
        keep, send = far_filter(place, taps, partial[pol], far[k], low, size, gates)
        keeps.append(keep)
        sents.append(pair(send))
        if k == 2:
            power = power_of(0, None, [keep])
    power = power_of(1, power)
    return jnp.moveaxis(power, 1, 2).reshape(power.shape[0], power.shape[2], -1)


def solution(mesh):
    in_specs = (
        P(("parts", "stn"), None, "tm", None, None),
        P(),
        P("parts", None),
        P("parts", None),
        P("tm", None),
    )
    out_specs = P("stn", "tm", "parts")
    return jax.shard_map(body, mesh=mesh, in_specs=in_specs, out_specs=out_specs, check_vma=False)
```
